128 devices in a mesh: section: 4 (over x), dp: 32 (over y, z, core).
Axes of the slice: x: 4, y: 4, z: 4, core: 2. Of those that a mesh axis runs over, the one named last changes fastest.
Arguments:
- embeddings: bfloat16 [8192, 1024], P('dp'), may hold values from -6 to 6
- in_proj: bfloat16 [4, 1024, 2048], P('section'), may hold values from -0.1875 to 0.1875
- out_proj: bfloat16 [4, 1024, 512], P('section'), may hold values from -0.25 to 0.25
- hist_cache: bfloat16 [4, 512, 128, 1024], P('section', 'dp'), may hold values from -6 to 6
- hist_len: int32 [64], P('dp'), may hold values from 1 to 2048, 98304 in all
- block_mask: int32 [64, 16], P('dp'), may hold values 0 or 1
- block_owner: int32 [64, 16, 1], P('dp'), may hold values from 0 to 31; in each aligned block of 32 rows (0 to 31, 32 to 63, ..., all dimensions but the last counted through in order) at most 2 rows name the same one
- block_slot: int32 [64, 16], P('dp'), may hold values from 0 to 15
- cotangent: bfloat16 [8192, 1024], P('dp'), may hold values from -1.5 to 1.5
Outputs:
- layer_outputs: bfloat16 [4, 8192, 1024], P('section', 'dp')
- input_grads: bfloat16 [4, 8192, 1024], P('section', 'dp')
- grad_in_proj: float32 [4, 1024, 2048], P('section', 'dp')
- grad_out_proj: float32 [4, 1024, 512], P('section', 'dp')
The draws below stay inside these ranges and needn't reach their ends.
Inputs may be any that keep to these rules, and one draw needn't show every extreme that they name: `hist_len`: some user has exactly 2048 history events. `block_owner`: among the blocks listed for the users of one dp index, at most 2 lie on any one owner, and in every draw some owner holds exactly 2 of them.
All inputs are finite; a program needn't handle non-finite values. No bound on the sum of `hist_len` or of `block_mask` on one device may be relied on, other than what follows from the above.
Results may differ from the reference program's by a relative error of at most 0.035.
Values may be sent and summed in bfloat16 or wider, within the bound.
A program may use at most 320 MiB of HBM per device.

```python
import math
from functools import partial
import jax
import jax.numpy as jnp
import numpy as np
from jax import lax

D = 1024
HEADS = 4
HA = 512
EVT = 128
HBLK = 16
U_DEV = 2
USERS = 64
TOKENS = 8192
LAYERS = 4
CAP = 2
CB = 16
CACHE_BLOCKS = 512
N_DP = 32


def place_ends(array, stream_key, smallest, high):
    extent = array.shape
    spot = [jax.random.randint(jax.random.fold_in(stream_key, axis), (), 0, extent[axis]) for axis in range(len(extent))]
    array = array.at[tuple(spot)].set(smallest)
    longest = extent.index(max(extent))
    spot[longest] = (spot[longest] + 1) % extent[longest]
    return array.at[tuple(spot)].set(high)


def raised(array, rng, source, target, blocks, factor):
    owner, partner = [(jnp.arange(array.shape[axis_at]) // (array.shape[axis_at] // blocks)).reshape([-1 if axis == axis_at else 1 for axis in range(array.ndim)]) for axis_at in (source, target)]
    chosen = jax.random.permutation(rng, blocks)[partner]
    strong = (owner == chosen) | (owner == (partner + blocks // 2) % blocks)
    return jnp.where(strong, factor * array, array)


def shard_levels(key, shape, shards, smallest, high):
    loudness, own = 1.0, jax.random.fold_in(key, 6)
    for dim, blocks in shards:
        steps = jnp.exp(jax.random.uniform(jax.random.fold_in(own, dim), (blocks,), jnp.float32, smallest / len(shards), high / len(shards)))
        loudness = loudness * jnp.repeat(steps, shape[dim] // blocks).reshape([-1 if axis == dim else 1 for axis in range(len(shape))])
    return loudness


def split_up(count, total, reach, slope):
    portions = [(1 << 20) // math.isqrt(rank ** slope) + 1 for rank in range(2, count + 1)]
    surplus, counts = total - reach - (count - 1), [1] * (count - 1)
    while surplus > 0:
        movable = [i for i in range(count - 1) if counts[i] < reach]
        whole, left = sum([portions[i] for i in movable]), surplus
        for i in movable:
            extra = min(reach - counts[i], max(1, left * portions[i] // whole), surplus)
            counts[i] = counts[i] + extra
            surplus = surplus - extra
    return np.array([reach] + counts)


def uneven_parts(stream_key, count, total, most, slope):
    if count == 2:
        one = jax.random.randint(stream_key, (), max(1, total - most), min(most, total - 1) + 1)
        return jnp.stack([one, total - one])
    tallies = jnp.asarray(split_up(count, total, most, slope), jnp.int32)
    couples = (count - 1) // 2
    donor, taker = tallies[1:1 + 2 * couples:2], tallies[2:2 + 2 * couples:2]
    margin = jnp.minimum(donor - 1, most - taker)
    moved = jax.random.randint(jax.random.fold_in(stream_key, 1), (couples,), 0, 1 << 20) % (margin + 1)
    tallies = tallies.at[1:1 + 2 * couples:2].set(donor - moved).at[2:2 + 2 * couples:2].set(taker + moved)
    return tallies[jax.random.permutation(jax.random.fold_in(stream_key, 2), count)]


def routed_block(key, own, number, rows, amount, top, limit, lean):
    order = jax.random.permutation(key, amount)
    crowded, ordinary = portions_of(amount, rows * top, limit, lean, True), portions_of(amount, rows * top, limit, lean, False)
    places = jnp.arange(amount)

    def named(sizes, offset_by):
        used = int((sizes > 0).sum())
        fixed = max(1, used // 4)
        passed = fixed + (places - fixed + offset_by * (used - fixed)) % max(1, amount - fixed)
        return jnp.zeros((amount,), jnp.int32).at[order[jnp.where(places < fixed, places, passed)]].set(jnp.asarray(sizes, jnp.int32))

    sizes = jnp.where(number % 4 == 0, named(crowded, number // 4), named(ordinary, number - number // 4 - 1))
    mixed = jax.random.permutation(jax.random.fold_in(own, 3), amount)
    donor, sink = mixed[0:amount // 2 * 2:2], mixed[1:amount // 2 * 2:2]
    slack = jnp.minimum(sizes[donor] - 1, limit - sizes[sink]) // 2
    slack = jnp.where((donor == order[0]) | (sink == order[0]) | (sizes[sink] == 0), 0, jnp.maximum(slack, 0))
    passed = jax.random.randint(jax.random.fold_in(own, 4), (amount // 2,), 0, 1 << 20) % (slack + 1)
    sizes = sizes.at[donor].add(-passed).at[sink].add(passed)
    members = jnp.searchsorted(jnp.cumsum(sizes), jnp.arange(rows * top), side="right").astype(jnp.int32)
    listing = members.reshape(top, rows).T
    listing = listing[jax.random.permutation(jax.random.fold_in(own, 1), rows)]
    offset_by = jax.random.randint(jax.random.fold_in(own, 2), (rows, 1), 0, top)
    return jnp.take_along_axis(listing, (jnp.arange(top)[None, :] + offset_by) % top, axis=1)


def portions_of(number_of, total, reach, slope, full):
    loads = [(1 << 20) // math.isqrt(grade ** slope) + 1 for grade in range(1, number_of + 1)]
    largest = reach if full else min(reach, max(-(-total // number_of), total * loads[0] // sum(loads)))
    least = 1 if total - largest >= number_of - 1 else 0
    holding, surplus = [largest] + [least] * (number_of - 1), total - largest - least * (number_of - 1)
    while surplus > 0:
        movable = [i for i in range(1, number_of) if holding[i] < largest] or [i for i in range(1, number_of) if holding[i] < reach]
        mass, remaining = sum([loads[i] for i in movable]), surplus
        for i in movable:
            more = min(reach - holding[i], max(1, remaining * loads[i] // mass), surplus)
            holding[i] = holding[i] + more
            surplus = surplus - more
    return np.array(holding)


def gaussian(rng, shape, spread, most, cuts=(), kind=jnp.bfloat16):
    factor_of = shard_levels(rng, shape, cuts, -0.22, 0.18) if cuts else 1.0
    entries = jax.random.normal(rng, shape, jnp.float32) * spread * factor_of
    return jnp.minimum(jnp.maximum(entries, -most), most).astype(kind)


def noise_with(key, shape, scale, reach, split, heavy, kind=jnp.bfloat16):
    drawn = scale * jax.random.normal(key, shape, jnp.float32)
    if split:
        drawn = drawn * shard_levels(key, shape, split, -0.22, 0.18)
    return jnp.clip(raised(drawn, jax.random.fold_in(key, 3), *heavy), -reach, reach).astype(kind)


def setup_inputs(seed: int = 0) -> dict:
    arg_keys = jax.random.split(jax.random.key(seed), 10)
    embeddings = gaussian(arg_keys[0], (TOKENS, D), 1.0, 6.0, ((0, 32),))
    in_proj = gaussian(arg_keys[1], (LAYERS, D, 4 * HA), D ** -0.5, 0.1875, ((0, 4),))
    out_proj = gaussian(arg_keys[2], (LAYERS, D, HA), HA ** -0.5, 0.25, ((0, 4),))
    hist_cache = gaussian(arg_keys[3], (LAYERS, CACHE_BLOCKS, EVT, 2 * HA), 1.0, 6.0, ((0, 4), (1, 32)))
    hist_len = uneven_parts(arg_keys[4], USERS, 3 * USERS * HBLK * EVT // 4, HBLK * EVT, 2).astype(jnp.int32)
    block_mask = place_ends((jax.random.randint(arg_keys[5], (USERS, HBLK), 0, 8) < 7).astype(jnp.int32), jax.random.fold_in(arg_keys[5], 1), 0, 1)
    block_owner_keys = jax.random.split(jax.random.fold_in(arg_keys[6], 1), USERS * HBLK // (U_DEV * HBLK))
    block_owner_turns = jax.random.permutation(jax.random.fold_in(arg_keys[6], 3), USERS * HBLK // (U_DEV * HBLK))
    block_owner = jax.vmap(lambda own, number: routed_block(jax.random.fold_in(arg_keys[6], 2), own, number, U_DEV * HBLK, N_DP, 1, CAP, 2))(block_owner_keys, block_owner_turns).reshape((USERS, HBLK, 1))
    block_slot = place_ends(jax.random.randint(arg_keys[7], (USERS, HBLK), 0, CB), jax.random.fold_in(arg_keys[7], 1), 0, CB - 1).astype(jnp.int32)
    cotangent = noise_with(arg_keys[8], (TOKENS, D), 0.25, 1.5, ((0, 32),), (0, 1, 32, 2.75))
    return {"embeddings": embeddings, "in_proj": in_proj, "out_proj": out_proj, "hist_cache": hist_cache, "hist_len": hist_len, "block_mask": block_mask, "block_owner": block_owner, "block_slot": block_slot, "cotangent": cotangent}


epsilon = 1e-06

def norm_rows(values):
    row_mean = lax.optimization_barrier(jnp.mean(values, axis=-1, keepdims=True))
    centred = values - row_mean
    return centred * lax.rsqrt(lax.optimization_barrier(jnp.mean(centred * centred, axis=-1, keepdims=True)) + epsilon)

def event_mask(lengths, blocks):
    position = jnp.arange(HBLK * EVT, dtype=jnp.int32).reshape(HBLK, EVT)
    live_cells = (position[None, :, :] < lengths[:, None, None]) & (blocks[:, :, None] > 0)
    return live_cells.astype(jnp.float32)

def to_float(values):
    return values.astype(jnp.float32)

def attend(projected, history, key_mask, inv_count, converter):
    user_count = history.shape[0]
    width = projected.shape[1] // 4
    head_size = width // HEADS
    activated = jax.nn.silu(projected).astype(jnp.bfloat16)
    gate_units = activated[:, :width]
    own_value = activated[:, width:2 * width]
    own_query = activated[:, 2 * width:3 * width]
    own_key = activated[:, 3 * width:]
    events = own_query.shape[0] // user_count
    all_keys = jnp.concatenate([history[:, :, :width], own_key.reshape(user_count, events, width)], axis=1)
    all_values = jnp.concatenate([history[:, :, width:], own_value.reshape(user_count, events, width)], axis=1)
    causal = (jnp.arange(events)[None, :] <= jnp.arange(events)[:, None]).astype(jnp.float32)
    history_part = jnp.broadcast_to(key_mask[:, None, :], (user_count, events, key_mask.shape[1]))
    own_part = jnp.broadcast_to(causal[None, :, :], (user_count, events, events))
    weight_mask = jnp.concatenate([history_part, own_part], axis=2) * inv_count[:, None, None]
    query_heads = converter(own_query.reshape(user_count, events, HEADS, head_size))
    key_heads = converter(all_keys.reshape(user_count, -1, HEADS, head_size))
    value_heads = converter(all_values.reshape(user_count, -1, HEADS, head_size))
    scores = jnp.einsum('bqhd,bkhd->bhqk', query_heads, key_heads, preferred_element_type=jnp.float32) * (1.0 / math.sqrt(head_size))
    weights = (jax.nn.silu(scores) * weight_mask[:, None, :, :]).astype(jnp.bfloat16)
    mixed = jnp.einsum('bhqk,bkhd->bqhd', converter(weights), value_heads, preferred_element_type=jnp.float32)
    return norm_rows(mixed.reshape(user_count * events, width)) * gate_units

def layer_forward(layer_input, w_in, w_out, attention):
    x_norm = norm_rows(layer_input.astype(jnp.float32)).astype(jnp.bfloat16)
    projected = jnp.dot(x_norm, w_in, preferred_element_type=jnp.float32)
    gated = attention(projected).astype(jnp.bfloat16)
    output_part = lax.dot_general(gated, w_out, (((1,), (1,)), ((), ())), preferred_element_type=jnp.float32)
    return (layer_input.astype(jnp.float32) + output_part).astype(jnp.bfloat16)

def layer_backward(layer_input, grad_y, w_in, w_out, attention):
    norm_value, norm_back = jax.vjp(norm_rows, layer_input.astype(jnp.float32))
    x_norm = norm_value.astype(jnp.bfloat16)
    projected = jnp.dot(x_norm, w_in, preferred_element_type=jnp.float32)
    gated_value, attend_back = jax.vjp(attention, projected)
    gated = gated_value.astype(jnp.bfloat16)
    grad_gated = jnp.dot(grad_y, w_out, preferred_element_type=jnp.float32)
    grad_projected = attend_back(grad_gated)[0].astype(jnp.bfloat16)
    grad_norm = lax.dot_general(grad_projected, w_in, (((1,), (1,)), ((), ())), preferred_element_type=jnp.float32)
    grad_x = (grad_y.astype(jnp.float32) + norm_back(grad_norm)[0]).astype(jnp.bfloat16)
    return (grad_x, x_norm, grad_projected, gated)

def contract_rows(left, right):
    return lax.dot_general(left, right, (((0,), (0,)), ((), ())), preferred_element_type=jnp.float32)

def reference(embeddings, in_proj, out_proj, hist_cache, hist_len, block_mask, block_owner, block_slot, cotangent):
    block_index = (block_owner[:, :, 0] * CB + block_slot).astype(jnp.int32).reshape(N_DP, U_DEV, HBLK)
    live_events = event_mask(hist_len, block_mask).reshape(N_DP, U_DEV, HBLK * EVT)
    inv_counts = 1.0 / (lax.optimization_barrier(jnp.sum(live_events, axis=2)) + EVT)
    group_rows = U_DEV * EVT
    start_input = embeddings.reshape(N_DP, group_rows, D)
    start_grad = cotangent.reshape(N_DP, group_rows, D)

    def one_group(totals, inputs):
        layer_input, grad_y, indices, key_mask, inverse = inputs
        attentions = []
        for layer_index in range(LAYERS):
            history = hist_cache[layer_index][indices].reshape(U_DEV, HBLK * EVT, 2 * HA)
            attentions.append(partial(attend, history=history, key_mask=key_mask, inv_count=inverse, converter=to_float))
        layer_inputs = []
        results = []
        for layer_index in range(LAYERS):
            layer_inputs.append(layer_input)
            layer_input = layer_forward(layer_input, in_proj[layer_index], out_proj[layer_index], attentions[layer_index])
            results.append(layer_input)
        grads_x = [None] * LAYERS
        terms_in = [None] * LAYERS
        terms_out = [None] * LAYERS
        for layer_index in reversed(range(LAYERS)):
            grad_x, x_norm, grad_projected, gated = layer_backward(layer_inputs[layer_index], grad_y, in_proj[layer_index], out_proj[layer_index], attentions[layer_index])
            terms_in[layer_index] = contract_rows(x_norm, grad_projected)
            terms_out[layer_index] = contract_rows(grad_y, gated)
            grads_x[layer_index] = grad_x
            grad_y = grad_x
        totals = (totals[0] + jnp.stack(terms_in), totals[1] + jnp.stack(terms_out))
        return (totals, (jnp.stack(results), jnp.stack(grads_x)))
    initial = (jnp.zeros((LAYERS, D, 4 * HA), jnp.float32), jnp.zeros((LAYERS, D, HA), jnp.float32))
    totals, stacked = lax.scan(one_group, initial, (start_input, start_grad, block_index, live_events, inv_counts))
    layer_outputs = stacked[0].transpose(1, 0, 2, 3).reshape(LAYERS, TOKENS, D)
    input_grads = stacked[1].transpose(1, 0, 2, 3).reshape(LAYERS, TOKENS, D)
    return (layer_outputs, input_grads, totals[0], totals[1])
```

```python
from functools import partial
import math

import jax
import jax.numpy as jnp
from jax import lax
from jax.experimental import pallas as pl
from jax.experimental.pallas import tpu as pltpu
from jax.sharding import PartitionSpec as P

HEADS = 4
EVT = 128
HBLK = 16
USERS = 2
ROWS = USERS * EVT
D = 1024
HA = 512
HD = HA // HEADS
CAP = 2
GROUP = 4
KEYS = HBLK * EVT
OWNERS = 32
epsilon = 1e-06
SCALE = 1.0 / math.sqrt(HD)
MESH = pl.DeviceIdType.MESH
F32 = jnp.float32
BF16 = jnp.bfloat16


def dot(a, b, ca=1, cb=0):
    return lax.dot_general(a, b, (((ca,), (cb,)), ((), ())), preferred_element_type=F32)


def normed(values):
    centred = values - jnp.mean(values, axis=-1, keepdims=True)
    inverse = lax.rsqrt(jnp.mean(centred * centred, axis=-1, keepdims=True) + epsilon)
    return centred * inverse, inverse


def norm_back(grad, value, inverse):
    return inverse * (
        grad
        - jnp.mean(grad, axis=-1, keepdims=True)
        - value * jnp.mean(grad * value, axis=-1, keepdims=True)
    )


def silu_parts(half):
    t = jnp.tanh(half)
    return half + half * t, 0.5 * ((1.0 + t) + half * (1.0 - t * t))


def barrier_with(peers):
    barrier = pltpu.get_barrier_semaphore()
    for peer in peers:
        pl.semaphore_signal(barrier, inc=1, device_id=peer, device_id_type=MESH)
    pl.semaphore_wait(barrier, len(peers))


def exchange_kernel(
    table_ref, cache_ref, out_ref, asked, asked_s, outgoing, ask_send, ask_recv, send_sem, recv_sem, local_sem
):
    me = lax.axis_index("dp")
    barrier = pltpu.get_barrier_semaphore()

    def greet(i, carry):
        pl.semaphore_signal(
            barrier, inc=1, device_id={"dp": lax.rem(me + i, OWNERS)}, device_id_type=MESH
        )
        return carry

    lax.fori_loop(1, OWNERS, greet, 0)
    pl.semaphore_wait(barrier, OWNERS - 1)

    def ask(i):
        peer = lax.rem(me + i, OWNERS)
        return pltpu.make_async_remote_copy(
            src_ref=table_ref,
            dst_ref=asked.at[me],
            send_sem=ask_send.at[peer],
            recv_sem=ask_recv.at[me],
            device_id={"dp": peer},
            device_id_type=MESH,
        )

    def asked_by(i):
        peer = lax.rem(me + i, OWNERS)
        return pltpu.make_async_remote_copy(
            src_ref=table_ref,
            dst_ref=asked.at[peer],
            send_sem=ask_send.at[peer],
            recv_sem=ask_recv.at[peer],
            device_id={"dp": peer},
            device_id_type=MESH,
        )

    def start_ask(i, carry):
        ask(i).start()
        return carry

    lax.fori_loop(1, OWNERS, start_ask, 0)
    own = pltpu.make_async_copy(table_ref, asked.at[me], local_sem.at[0])
    own.start()
    own.wait()

    def wait_ask(i, carry):
        asked_by(i).wait()
        return carry

    lax.fori_loop(1, OWNERS, wait_ask, 0)
    down = pltpu.make_async_copy(asked, asked_s, local_sem.at[1])
    down.start()
    down.wait()

    def fill(peer):
        for k in range(CAP):
            outgoing[peer, k] = cache_ref[asked_s[peer, 0, me * CAP + k]]

    def send(i, carry):
        peer = lax.rem(me + i, OWNERS)
        fill(peer)
        pltpu.make_async_remote_copy(
            src_ref=outgoing.at[peer],
            dst_ref=out_ref.at[me],
            send_sem=send_sem.at[peer],
            recv_sem=recv_sem.at[me],
            device_id={"dp": peer},
            device_id_type=MESH,
        ).start()
        return carry

    lax.fori_loop(1, OWNERS, send, 0)
    fill(me)
    kept = pltpu.make_async_copy(outgoing.at[me], out_ref.at[me], local_sem.at[2])
    kept.start()

    def finish(i, carry):
        peer = lax.rem(me + i, OWNERS)
        pltpu.make_async_remote_copy(
            src_ref=outgoing.at[peer],
            dst_ref=out_ref.at[peer],
            send_sem=send_sem.at[peer],
            recv_sem=recv_sem.at[peer],
            device_id={"dp": peer},
            device_id_type=MESH,
        ).wait()
        return carry

    lax.fori_loop(1, OWNERS, finish, 0)
    kept.wait()


def exchange(table, cache):
    return pl.pallas_call(
        exchange_kernel,
        out_shape=jax.ShapeDtypeStruct((OWNERS, CAP, EVT, 2 * HA), BF16),
        in_specs=[pl.BlockSpec(memory_space=pltpu.VMEM)] * 2,
        out_specs=pl.BlockSpec(memory_space=pl.ANY),
        scratch_shapes=[
            pltpu.VMEM((OWNERS, 1, 128), jnp.int32),
            pltpu.SMEM((OWNERS, 1, 128), jnp.int32),
            pltpu.VMEM((OWNERS, CAP, EVT, 2 * HA), BF16),
            pltpu.SemaphoreType.DMA((OWNERS,)),
            pltpu.SemaphoreType.DMA((OWNERS,)),
            pltpu.SemaphoreType.DMA((OWNERS,)),
            pltpu.SemaphoreType.DMA((OWNERS,)),
            pltpu.SemaphoreType.DMA((3,)),
        ],
        compiler_params=pltpu.CompilerParams(
            collective_id=0, has_side_effects=True, vmem_limit_bytes=48 << 20
        ),
        name="exchange",
    )(table, cache)


def start_loads(where_ref, fetched_ref, hist, hist_sem):
    def one(r, carry):
        pltpu.make_async_copy(fetched_ref.at[where_ref[r]], hist.at[r], hist_sem.at[r]).start()
        return carry

    lax.fori_loop(0, USERS * HBLK, one, 0)


def wait_loads(fetched_ref, hist, hist_sem):
    def one(r, carry):
        pltpu.make_async_copy(fetched_ref.at[0], hist.at[r], hist_sem.at[r]).wait()
        return carry

    lax.fori_loop(0, USERS * HBLK, one, 0)


def mask_values(live_ref, hist):
    row = lax.broadcasted_iota(jnp.int32, (EVT, HA), 0)

    def one(r, carry):
        keep = (row < live_ref[r]).astype(F32).astype(BF16)
        hist[r, :, HA:] = hist[r, :, HA:] * keep
        return carry

    lax.fori_loop(0, USERS * HBLK, one, 0)


def inverse_count(live_ref, user):
    total = live_ref[user * HBLK]
    for j in range(1, HBLK):
        total = total + live_ref[user * HBLK + j]
    return 1.0 / (jnp.full((EVT, 1), total, jnp.int32).astype(F32) + float(EVT))


def columns(start):
    return pl.ds(pl.multiple_of(start, HD), HD)


def causal_mask():
    return lax.broadcasted_iota(jnp.int32, (EVT, EVT), 1) <= lax.broadcasted_iota(
        jnp.int32, (EVT, EVT), 0
    )


def attend_forward(act, hist, mixed, slope, own_weights, counts):
    causal = causal_mask()

    def one(index, carry):
        user, head = index // HEADS, index % HEADS
        rows = pl.ds(pl.multiple_of(user * EVT, EVT), EVT)
        query = act[rows, columns(2 * HA + head * HD)]
        total = jnp.zeros((EVT, HD), F32)
        for group in range(HBLK // GROUP):
            blocks = pl.ds(user * HBLK + group * GROUP, GROUP)
            keys = hist[blocks, :, columns(head * HD)].reshape(GROUP * EVT, HD)
            values = hist[blocks, :, columns(HA + head * HD)].reshape(GROUP * EVT, HD)
            weights, rise = silu_parts(dot(query, keys, 1, 1) * (0.5 * SCALE))
            total += dot(weights.astype(BF16), values)
            if slope is not None:
                slope[index, :, group * GROUP * EVT : (group + 1) * GROUP * EVT] = (
                    rise * SCALE
                ).astype(BF16)
        keys = act[rows, columns(3 * HA + head * HD)]
        values = act[rows, columns(HA + head * HD)]
        weights, rise = silu_parts(dot(query, keys, 1, 1) * (0.5 * SCALE))
        weights = jnp.where(causal, weights, 0.0).astype(BF16)
        total += dot(weights, values)
        if slope is not None:
            slope[index, :, KEYS:] = jnp.where(causal, rise * SCALE, 0.0).astype(BF16)
            own_weights[index] = weights
        mixed[rows, columns(head * HD)] = total * jnp.where(user == 0, counts[0], counts[1])
        return carry

    lax.fori_loop(0, USERS * HEADS, one, 0)


def forward_kernel(
    keep, where_ref, live_ref, x_ref, w_in_ref, w_out_ref, fetched_ref, *refs
):
    if keep:
        y_ref, x_norm_ref, act, slope_in, slope, own_weights, value_ref, gated_ref, rate_ref = refs[:9]
        refs = refs[9:]
    else:
        y_ref, refs = refs[0], refs[1:]
        slope = own_weights = None
        act, refs = refs[0], refs[1:]
    hist, mixed, hist_sem = refs
    start_loads(where_ref, fetched_ref, hist, hist_sem)
    x = x_ref[...].astype(F32)
    x_norm = normed(x)[0].astype(BF16)
    if keep:
        x_norm_ref[...] = x_norm
    for c in range(4):
        part = slice(c * HA, (c + 1) * HA)
        value, rise = silu_parts(dot(x_norm, w_in_ref[:, part]) * 0.5)
        act[:, part] = value.astype(BF16)
        if keep:
            slope_in[:, part] = rise
    wait_loads(fetched_ref, hist, hist_sem)
    mask_values(live_ref, hist)
    counts = [inverse_count(live_ref, user) for user in range(USERS)]
    attend_forward(act, hist, mixed, slope, own_weights, counts)
    value, rate = normed(mixed[...])
    gated = (value * act[:, :HA].astype(F32)).astype(BF16)
    if keep:
        value_ref[...] = value
        gated_ref[...] = gated
        rate_ref[...] = jnp.broadcast_to(rate, rate_ref.shape)
    y_ref[...] = (x + dot(gated, w_out_ref[...], 1, 1)).astype(BF16)


VM = pl.BlockSpec(memory_space=pltpu.VMEM)
SM = pl.BlockSpec(memory_space=pltpu.SMEM)
ANY = pl.BlockSpec(memory_space=pl.ANY)


def forward(where, live, x, w_in, w_out, fetched, keep):
    outs = [jax.ShapeDtypeStruct((ROWS, D), BF16)]
    scratch = [pltpu.VMEM((USERS * HBLK, EVT, 2 * HA), BF16), pltpu.VMEM((ROWS, HA), F32)]
    scratch += [pltpu.SemaphoreType.DMA((USERS * HBLK,))]
    if keep:
        outs += [
            jax.ShapeDtypeStruct((ROWS, D), BF16),
            jax.ShapeDtypeStruct((ROWS, 4 * HA), BF16),
            jax.ShapeDtypeStruct((ROWS, 4 * HA), F32),
            jax.ShapeDtypeStruct((USERS * HEADS, EVT, KEYS + EVT), BF16),
            jax.ShapeDtypeStruct((USERS * HEADS, EVT, EVT), BF16),
            jax.ShapeDtypeStruct((ROWS, HA), F32),
            jax.ShapeDtypeStruct((ROWS, HA), BF16),
            jax.ShapeDtypeStruct((ROWS, 128), F32),
        ]
    else:
        scratch = [pltpu.VMEM((ROWS, 4 * HA), BF16)] + scratch
    return pl.pallas_call(
        partial(forward_kernel, keep),
        out_shape=outs,
        in_specs=[SM, SM, VM, VM, VM, ANY],
        out_specs=[VM] * len(outs),
        scratch_shapes=scratch,
        compiler_params=pltpu.CompilerParams(vmem_limit_bytes=52 << 20),
        name="forward_keep" if keep else "forward",
    )(where, live, x, w_in, w_out, fetched)


def backward_kernel(
    where_ref, live_ref, x_ref, dy_ref, w_in_ref, w_out_ref, fetched_ref,
    act, slope_in, slope, own_weights, value_ref, rate_ref,
    dx_ref, dproj, hist, dmixed, hist_sem,
):
    start_loads(where_ref, fetched_ref, hist, hist_sem)
    dy = dy_ref[...]
    dgated = dot(dy, w_out_ref[...])
    value = value_ref[...]
    dproj[:, :HA] = (dgated * value * slope_in[:, :HA]).astype(BF16)
    grad = norm_back(dgated * act[:, :HA].astype(F32), value, rate_ref[:, :1])
    for user in range(USERS):
        rows = slice(user * EVT, (user + 1) * EVT)
        dmixed[rows] = (grad[rows] * inverse_count(live_ref, user)).astype(BF16)
    wait_loads(fetched_ref, hist, hist_sem)
    mask_values(live_ref, hist)

    def one(index, carry):
        user, head = index // HEADS, index % HEADS
        rows = pl.ds(pl.multiple_of(user * EVT, EVT), EVT)
        grad_mixed = dmixed[rows, columns(head * HD)]
        total = jnp.zeros((EVT, HD), F32)
        for group in range(HBLK // GROUP):
            blocks = pl.ds(user * HBLK + group * GROUP, GROUP)
            keys = hist[blocks, :, columns(head * HD)].reshape(GROUP * EVT, HD)
            values = hist[blocks, :, columns(HA + head * HD)].reshape(GROUP * EVT, HD)
            rise = slope[index, :, group * GROUP * EVT : (group + 1) * GROUP * EVT].astype(F32)
            ds = (dot(grad_mixed, values, 1, 1) * rise).astype(BF16)
            total += dot(ds, keys)
        query = act[rows, columns(2 * HA + head * HD)]
        keys = act[rows, columns(3 * HA + head * HD)]
        values = act[rows, columns(HA + head * HD)]
        ds = (dot(grad_mixed, values, 1, 1) * slope[index, :, KEYS:].astype(F32)).astype(BF16)
        total += dot(ds, keys)
        dvalue = dot(own_weights[index], grad_mixed, 0, 0)
        dkey = dot(ds, query, 0, 0)
        for base, part in ((HA, dvalue), (2 * HA, total), (3 * HA, dkey)):
            at = columns(base + head * HD)
            dproj[rows, at] = (part * slope_in[rows, at]).astype(BF16)
        return carry

    lax.fori_loop(0, USERS * HEADS, one, 0)
    dnorm = dot(dproj[...], w_in_ref[...], 1, 1)
    x_norm, rate = normed(x_ref[...].astype(F32))
    dx_ref[...] = (dy.astype(F32) + norm_back(dnorm, x_norm, rate)).astype(BF16)


def backward(where, live, x, dy, w_in, w_out, fetched, kept):
    return pl.pallas_call(
        backward_kernel,
        out_shape=[
            jax.ShapeDtypeStruct((ROWS, D), BF16),
            jax.ShapeDtypeStruct((ROWS, 4 * HA), BF16),
        ],
        in_specs=[SM, SM, VM, VM, VM, VM, ANY] + [VM] * 6,
        out_specs=[VM, VM],
        scratch_shapes=[
            pltpu.VMEM((USERS * HBLK, EVT, 2 * HA), BF16),
            pltpu.VMEM((ROWS, HA), BF16),
            pltpu.SemaphoreType.DMA((USERS * HBLK,)),
        ],
        compiler_params=pltpu.CompilerParams(vmem_limit_bytes=52 << 20),
        name="backward",
    )(where, live, x, dy, w_in, w_out, fetched, *kept)


def passed_along(array, axis, by):
    peers = lax.axis_size(axis)
    pairs = [(i, i + by) for i in range(peers) if 0 <= i + by < peers]
    return lax.ppermute(array, axis, pairs)


def body(
    embeddings, in_proj, out_proj, hist_cache, hist_len, block_mask, block_owner, block_slot, cotangent
):
    sections = lax.axis_size("section")
    section = lax.axis_index("section")
    w_in, w_out = in_proj[0], out_proj[0]
    requests = USERS * HBLK
    owner = block_owner.reshape(requests)
    order = jnp.arange(requests, dtype=jnp.int32)
    earlier = (owner[:, None] == owner[None, :]) & (order[None, :] < order[:, None])
    where = owner * CAP + jnp.sum(earlier.astype(jnp.int32), axis=1)
    names = jnp.arange(128, dtype=jnp.int32)
    table = jnp.sum(
        jnp.where(where[:, None] == names[None, :], block_slot.reshape(requests, 1), 0), axis=0
    )
    start = jnp.arange(HBLK, dtype=jnp.int32)[None, :] * EVT
    live = jnp.where(block_mask > 0, jnp.clip(hist_len[:, None] - start, 0, EVT), 0).reshape(requests)
    fetched = exchange(table.reshape(1, 128), hist_cache[0]).reshape(OWNERS * CAP, EVT, 2 * HA)

    x = embeddings
    for step in range(sections):
        made = forward(where, live, x, w_in, w_out, fetched, step == sections - 1)
        if step < sections - 1:
            arriving = passed_along(made[0], "section", 1)
            x = jnp.where(section == step + 1, arriving, x)
    y, x_norm, act, slope_in, slope, own_weights, value, gated, rate = made
    dy = cotangent
    kept = (act, slope_in, slope, own_weights, value, rate)
    for step in reversed(range(sections)):
        dx, dproj = backward(where, live, x, dy, w_in, w_out, fetched, kept)
        if step > 0:
            arriving = passed_along(dx, "section", -1)
            dy = jnp.where(section == step - 1, arriving, dy)
    own_rows = lax.psum_scatter(
        jnp.concatenate([dot(x_norm, dproj, 0, 0), dot(dy, gated, 0, 0)], axis=1).astype(BF16),
        "dp",
        scatter_dimension=0,
        tiled=True,
    ).astype(F32)
    return (y[None], dx[None], own_rows[None, :, : 4 * HA], own_rows[None, :, 4 * HA :])


def solution(mesh):
    placed = (
        P("dp", None),
        P("section", None, None),
        P("section", None, None),
        P("section", "dp", None, None),
        P("dp"),
        P("dp", None),
        P("dp", None, None),
        P("dp", None),
        P("dp", None),
    )
    return jax.shard_map(
        body,
        mesh=mesh,
        in_specs=placed,
        out_specs=(
            P("section", "dp", None),
            P("section", "dp", None),
            P("section", "dp", None),
            P("section", "dp", None),
        ),
        check_vma=False,
    )
```

```python
from functools import partial
import math

import jax
import jax.numpy as jnp
from jax import lax
from jax.experimental import pallas as pl
from jax.experimental.pallas import tpu as pltpu
from jax.sharding import PartitionSpec as P

HEADS = 4
EVT = 128
HBLK = 16
USERS = 2
ROWS = USERS * EVT
D = 1024
HA = 512
HD = HA // HEADS
CAP = 2
GROUP = 4
KEYS = HBLK * EVT
OWNERS = 32
epsilon = 1e-06
SCALE = 1.0 / math.sqrt(HD)
MESH = pl.DeviceIdType.MESH
F32 = jnp.float32
BF16 = jnp.bfloat16


def dot(a, b, ca=1, cb=0):
    return lax.dot_general(a, b, (((ca,), (cb,)), ((), ())), preferred_element_type=F32)


def normed(values):
    centred = values - jnp.mean(values, axis=-1, keepdims=True)
    inverse = lax.rsqrt(jnp.mean(centred * centred, axis=-1, keepdims=True) + epsilon)
    return centred * inverse, inverse


def norm_back(grad, value, inverse):
    return inverse * (
        grad
        - jnp.mean(grad, axis=-1, keepdims=True)
        - value * jnp.mean(grad * value, axis=-1, keepdims=True)
    )


def silu_parts(half):
    t = jnp.tanh(half)
    return half + half * t, 0.5 * ((1.0 + t) + half * (1.0 - t * t))


def barrier_with(peers):
    barrier = pltpu.get_barrier_semaphore()
    for peer in peers:
        pl.semaphore_signal(barrier, inc=1, device_id=peer, device_id_type=MESH)
    pl.semaphore_wait(barrier, len(peers))


def chip_at(offset):
    me = lax.axis_index("dp")
    y, z, c = me // 8, lax.rem(me // 2, 4), lax.rem(me, 2)
    return (
        lax.rem(y + offset[0] + 4, 4) * 8 + lax.rem(z + offset[1] + 4, 4) * 2 + lax.rem(c + offset[2] + 2, 2)
    )


CHIPS = [(1, 1), (3, 3), (2, 0), (0, 2), (1, 3), (3, 1), (2, 2), (1, 0), (3, 0), (0, 1), (0, 3), (1, 2), (3, 2), (2, 1), (2, 3)]
OFFSETS = [(a, b, c) for a, b in CHIPS for c in (0, 1)] + [(0, 0, 1)]


def opposite(offset):
    return tuple(-part for part in offset)


def exchange_kernel(
    table_ref, cache_ref, out_ref, asked, asked_s, outgoing, ask_send, ask_recv, send_sem, recv_sem, local_sem
):
    me = lax.axis_index("dp")
    barrier = pltpu.get_barrier_semaphore()
    for offset in OFFSETS:
        pl.semaphore_signal(barrier, inc=1, device_id={"dp": chip_at(offset)}, device_id_type=MESH)
    pl.semaphore_wait(barrier, OWNERS - 1)

    asks = []
    for i, offset in enumerate(OFFSETS):
        asks.append(
            pltpu.make_async_remote_copy(
                src_ref=table_ref,
                dst_ref=asked.at[i],
                send_sem=ask_send.at[i],
                recv_sem=ask_recv.at[i],
                device_id={"dp": chip_at(offset)},
                device_id_type=MESH,
            )
        )
        asks[-1].start()
    own = pltpu.make_async_copy(table_ref, asked.at[OWNERS - 1], local_sem.at[0])
    own.start()
    own.wait()
    for ask in asks:
        ask.wait()
    down = pltpu.make_async_copy(asked, asked_s, local_sem.at[1])
    down.start()
    down.wait()

    def fill(slot, row):
        for k in range(CAP):
            outgoing[slot, k] = cache_ref[asked_s[row, 0, me * CAP + k]]

    sends = []
    for i, offset in enumerate(OFFSETS):
        back = tuple((-p) % n for p, n in zip(offset, (4, 4, 2)))
        fill(i, OFFSETS.index(back))
        sends.append(
            pltpu.make_async_remote_copy(
                src_ref=outgoing.at[i],
                dst_ref=out_ref.at[me],
                send_sem=send_sem.at[i],
                recv_sem=recv_sem.at[i],
                device_id={"dp": chip_at(offset)},
                device_id_type=MESH,
            )
        )
        sends[-1].start()
    fill(OWNERS - 1, OWNERS - 1)
    kept = pltpu.make_async_copy(outgoing.at[OWNERS - 1], out_ref.at[me], local_sem.at[2])
    kept.start()
    for send in sends:
        send.wait()
    kept.wait()


def exchange(table, cache):
    return pl.pallas_call(
        exchange_kernel,
        out_shape=jax.ShapeDtypeStruct((OWNERS, CAP, EVT, 2 * HA), BF16),
        in_specs=[pl.BlockSpec(memory_space=pltpu.VMEM)] * 2,
        out_specs=pl.BlockSpec(memory_space=pl.ANY),
        scratch_shapes=[
            pltpu.VMEM((OWNERS, 1, 128), jnp.int32),
            pltpu.SMEM((OWNERS, 1, 128), jnp.int32),
            pltpu.VMEM((OWNERS, CAP, EVT, 2 * HA), BF16),
            pltpu.SemaphoreType.DMA((OWNERS,)),
            pltpu.SemaphoreType.DMA((OWNERS,)),
            pltpu.SemaphoreType.DMA((OWNERS,)),
            pltpu.SemaphoreType.DMA((OWNERS,)),
            pltpu.SemaphoreType.DMA((3,)),
        ],
        compiler_params=pltpu.CompilerParams(
            collective_id=0, has_side_effects=True, vmem_limit_bytes=48 << 20
        ),
        name="exchange",
    )(table, cache)


def start_loads(where_ref, fetched_ref, hist, hist_sem):
    def one(r, carry):
        pltpu.make_async_copy(fetched_ref.at[where_ref[r]], hist.at[r], hist_sem.at[r]).start()
        return carry

    lax.fori_loop(0, USERS * HBLK, one, 0)


def wait_loads(fetched_ref, hist, hist_sem):
    def one(r, carry):
        pltpu.make_async_copy(fetched_ref.at[0], hist.at[r], hist_sem.at[r]).wait()
        return carry

    lax.fori_loop(0, USERS * HBLK, one, 0)


def mask_values(live_ref, hist):
    row = lax.broadcasted_iota(jnp.int32, (EVT, HA), 0)

    def one(r, carry):
        keep = (row < live_ref[r]).astype(F32).astype(BF16)
        hist[r, :, HA:] = hist[r, :, HA:] * keep
        return carry

    lax.fori_loop(0, USERS * HBLK, one, 0)


def inverse_count(live_ref, user):
    total = live_ref[user * HBLK]
    for j in range(1, HBLK):
        total = total + live_ref[user * HBLK + j]
    return 1.0 / (jnp.full((EVT, 1), total, jnp.int32).astype(F32) + float(EVT))


def columns(start):
    return pl.ds(pl.multiple_of(start, HD), HD)


def causal_mask():
    return lax.broadcasted_iota(jnp.int32, (EVT, EVT), 1) <= lax.broadcasted_iota(
        jnp.int32, (EVT, EVT), 0
    )


def attend_forward(act, hist, mixed, slope, own_weights, counts):
    causal = causal_mask()

    def one(index, carry):
        user, head = index // HEADS, index % HEADS
        rows = pl.ds(pl.multiple_of(user * EVT, EVT), EVT)
        query = act[rows, columns(2 * HA + head * HD)]
        total = jnp.zeros((EVT, HD), F32)
        for group in range(HBLK // GROUP):
            blocks = pl.ds(user * HBLK + group * GROUP, GROUP)
            keys = hist[blocks, :, columns(head * HD)].reshape(GROUP * EVT, HD)
            values = hist[blocks, :, columns(HA + head * HD)].reshape(GROUP * EVT, HD)
            weights, rise = silu_parts(dot(query, keys, 1, 1) * (0.5 * SCALE))
            total += dot(weights.astype(BF16), values)
            if slope is not None:
                slope[index, :, group * GROUP * EVT : (group + 1) * GROUP * EVT] = (
                    rise * SCALE
                ).astype(BF16)
        keys = act[rows, columns(3 * HA + head * HD)]
        values = act[rows, columns(HA + head * HD)]
        weights, rise = silu_parts(dot(query, keys, 1, 1) * (0.5 * SCALE))
        weights = jnp.where(causal, weights, 0.0).astype(BF16)
        total += dot(weights, values)
        if slope is not None:
            slope[index, :, KEYS:] = jnp.where(causal, rise * SCALE, 0.0).astype(BF16)
            own_weights[index] = weights
        mixed[rows, columns(head * HD)] = total * jnp.where(user == 0, counts[0], counts[1])
        return carry

    lax.fori_loop(0, USERS * HEADS, one, 0)


def forward_kernel(
    keep, where_ref, live_ref, x_ref, w_in_ref, w_out_ref, fetched_ref, *refs
):
    if keep:
        y_ref, x_norm_ref, act, slope_in, slope, own_weights, value_ref, gated_ref, rate_ref = refs[:9]
        refs = refs[9:]
    else:
        y_ref, refs = refs[0], refs[1:]
        slope = own_weights = None
        act, refs = refs[0], refs[1:]
    hist, mixed, hist_sem = refs
    start_loads(where_ref, fetched_ref, hist, hist_sem)
    x = x_ref[...].astype(F32)
    x_norm = normed(x)[0].astype(BF16)
    if keep:
        x_norm_ref[...] = x_norm
    for c in range(4):
        part = slice(c * HA, (c + 1) * HA)
        value, rise = silu_parts(dot(x_norm, w_in_ref[:, part]) * 0.5)
        act[:, part] = value.astype(BF16)
        if keep:
            slope_in[:, part] = rise
    wait_loads(fetched_ref, hist, hist_sem)
    mask_values(live_ref, hist)
    counts = [inverse_count(live_ref, user) for user in range(USERS)]
    attend_forward(act, hist, mixed, slope, own_weights, counts)
    value, rate = normed(mixed[...])
    gated = (value * act[:, :HA].astype(F32)).astype(BF16)
    if keep:
        value_ref[...] = value
        gated_ref[...] = gated
        rate_ref[...] = jnp.broadcast_to(rate, rate_ref.shape)
    y_ref[...] = (x + dot(gated, w_out_ref[...], 1, 1)).astype(BF16)


VM = pl.BlockSpec(memory_space=pltpu.VMEM)
SM = pl.BlockSpec(memory_space=pltpu.SMEM)
ANY = pl.BlockSpec(memory_space=pl.ANY)


def forward(where, live, x, w_in, w_out, fetched, keep):
    outs = [jax.ShapeDtypeStruct((ROWS, D), BF16)]
    scratch = [pltpu.VMEM((USERS * HBLK, EVT, 2 * HA), BF16), pltpu.VMEM((ROWS, HA), F32)]
    scratch += [pltpu.SemaphoreType.DMA((USERS * HBLK,))]
    if keep:
        outs += [
            jax.ShapeDtypeStruct((ROWS, D), BF16),
            jax.ShapeDtypeStruct((ROWS, 4 * HA), BF16),
            jax.ShapeDtypeStruct((ROWS, 4 * HA), F32),
            jax.ShapeDtypeStruct((USERS * HEADS, EVT, KEYS + EVT), BF16),
            jax.ShapeDtypeStruct((USERS * HEADS, EVT, EVT), BF16),
            jax.ShapeDtypeStruct((ROWS, HA), F32),
            jax.ShapeDtypeStruct((ROWS, HA), BF16),
            jax.ShapeDtypeStruct((ROWS, 128), F32),
        ]
    else:
        scratch = [pltpu.VMEM((ROWS, 4 * HA), BF16)] + scratch
    return pl.pallas_call(
        partial(forward_kernel, keep),
        out_shape=outs,
        in_specs=[SM, SM, VM, VM, VM, ANY],
        out_specs=[VM] * len(outs),
        scratch_shapes=scratch,
        compiler_params=pltpu.CompilerParams(vmem_limit_bytes=52 << 20),
        name="forward_keep" if keep else "forward",
    )(where, live, x, w_in, w_out, fetched)


def backward_kernel(
    where_ref, live_ref, x_ref, dy_ref, w_in_ref, w_out_ref, fetched_ref,
    act, slope_in, slope, own_weights, value_ref, rate_ref,
    dx_ref, dproj, hist, dmixed, hist_sem,
):
    start_loads(where_ref, fetched_ref, hist, hist_sem)
    dy = dy_ref[...]
    dgated = dot(dy, w_out_ref[...])
    value = value_ref[...]
    dproj[:, :HA] = (dgated * value * slope_in[:, :HA]).astype(BF16)
    grad = norm_back(dgated * act[:, :HA].astype(F32), value, rate_ref[:, :1])
    for user in range(USERS):
        rows = slice(user * EVT, (user + 1) * EVT)
        dmixed[rows] = (grad[rows] * inverse_count(live_ref, user)).astype(BF16)
    wait_loads(fetched_ref, hist, hist_sem)
    mask_values(live_ref, hist)

    def one(index, carry):
        user, head = index // HEADS, index % HEADS
        rows = pl.ds(pl.multiple_of(user * EVT, EVT), EVT)
        grad_mixed = dmixed[rows, columns(head * HD)]
        total = jnp.zeros((EVT, HD), F32)
        for group in range(HBLK // GROUP):
            blocks = pl.ds(user * HBLK + group * GROUP, GROUP)
            keys = hist[blocks, :, columns(head * HD)].reshape(GROUP * EVT, HD)
            values = hist[blocks, :, columns(HA + head * HD)].reshape(GROUP * EVT, HD)
            rise = slope[index, :, group * GROUP * EVT : (group + 1) * GROUP * EVT].astype(F32)
            ds = (dot(grad_mixed, values, 1, 1) * rise).astype(BF16)
            total += dot(ds, keys)
        query = act[rows, columns(2 * HA + head * HD)]
        keys = act[rows, columns(3 * HA + head * HD)]
        values = act[rows, columns(HA + head * HD)]
        ds = (dot(grad_mixed, values, 1, 1) * slope[index, :, KEYS:].astype(F32)).astype(BF16)
        total += dot(ds, keys)
        dvalue = dot(own_weights[index], grad_mixed, 0, 0)
        dkey = dot(ds, query, 0, 0)
        for base, part in ((HA, dvalue), (2 * HA, total), (3 * HA, dkey)):
            at = columns(base + head * HD)
            dproj[rows, at] = (part * slope_in[rows, at]).astype(BF16)
        return carry

    lax.fori_loop(0, USERS * HEADS, one, 0)
    dnorm = dot(dproj[...], w_in_ref[...], 1, 1)
    x_norm, rate = normed(x_ref[...].astype(F32))
    dx_ref[...] = (dy.astype(F32) + norm_back(dnorm, x_norm, rate)).astype(BF16)


def backward(where, live, x, dy, w_in, w_out, fetched, kept):
    return pl.pallas_call(
        backward_kernel,
        out_shape=[
            jax.ShapeDtypeStruct((ROWS, D), BF16),
            jax.ShapeDtypeStruct((ROWS, 4 * HA), BF16),
        ],
        in_specs=[SM, SM, VM, VM, VM, VM, ANY] + [VM] * 6,
        out_specs=[VM, VM],
        scratch_shapes=[
            pltpu.VMEM((USERS * HBLK, EVT, 2 * HA), BF16),
            pltpu.VMEM((ROWS, HA), BF16),
            pltpu.SemaphoreType.DMA((USERS * HBLK,)),
        ],
        compiler_params=pltpu.CompilerParams(vmem_limit_bytes=52 << 20),
        name="backward",
    )(where, live, x, dy, w_in, w_out, fetched, *kept)


HALF = (4 * HA + HA) // 2
CHUNK = D // OWNERS


def scatter_kernel(
    part_ref, in_ref, out_ref, pair, mine, first, middle, second, pair_sem, first_sem, second_sem
):
    me = lax.axis_index("dp")
    y, z, c = me // 8, lax.rem(me // 2, 4), lax.rem(me, 2)
    steps = (1, 3, 2)
    peers = [(0, 0, 1)] + [(s, 0, 0) for s in steps] + [(0, s, 0) for s in steps]
    barrier = pltpu.get_barrier_semaphore()
    for peer in peers:
        pl.semaphore_signal(barrier, inc=1, device_id={"dp": chip_at(peer)}, device_id_type=MESH)
    pl.semaphore_wait(barrier, len(peers))

    def copy(src, dst, sems, offset):
        made = pltpu.make_async_remote_copy(
            src_ref=src,
            dst_ref=dst,
            send_sem=sems.at[0],
            recv_sem=sems.at[1],
            device_id={"dp": chip_at(offset)},
            device_id_type=MESH,
        )
        made.start()
        return made

    cols = [pl.ds(h * HALF, HALF) for h in range(2)]
    swaps = [
        copy(part_ref.at[:, :, 1 - c, :, cols[h]], pair.at[h], pair_sem.at[h], (0, 0, 1)) for h in range(2)
    ]
    moves = [[], []]
    for h in range(2):
        swaps[h].wait()

        def join(i, carry, h=h):
            total = part_ref[i, :, c, :, h * HALF : (h + 1) * HALF].astype(F32) + pair[h, i].astype(F32)
            mine[h, i] = total.astype(BF16)
            return carry

        lax.fori_loop(0, 4, join, 0)
        for k, s in enumerate(steps):
            offset = (s, 0, 0) if h == 0 else (0, s, 0)
            at = lax.rem((z if h else y) + s, 4)
            src = mine.at[h, :, at] if h else mine.at[h, at]
            moves[h].append(copy(src, first.at[h, k], first_sem.at[h, k], offset))
    later = [[], []]
    for h in range(2):
        for move in moves[h]:
            move.wait()

        def add(i, carry, h=h):
            total = (mine[h, i, z] if h else mine[h, y, i]).astype(F32)
            for k in range(3):
                total += first[h, k, i].astype(F32)
            middle[h, i] = total.astype(BF16)
            return carry

        lax.fori_loop(0, 4, add, 0)
        for k, s in enumerate(steps):
            offset = (0, s, 0) if h == 0 else (s, 0, 0)
            at = lax.rem((y if h else z) + s, 4)
            later[h].append(copy(middle.at[h, at], second.at[h, k], second_sem.at[h, k], offset))
    for h in range(2):
        for move in later[h]:
            move.wait()
        total = middle[h, y if h else z].astype(F32)
        for k in range(3):
            total += second[h, k].astype(F32)
        if h == 0:
            in_ref[:, :HALF] = total
        else:
            in_ref[:, HALF:] = total[:, : 4 * HA - HALF]
            out_ref[...] = total[:, 4 * HA - HALF :]


def summed(part):
    return pl.pallas_call(
        scatter_kernel,
        out_shape=[
            jax.ShapeDtypeStruct((CHUNK, 4 * HA), F32),
            jax.ShapeDtypeStruct((CHUNK, HA), F32),
        ],
        in_specs=[VM],
        out_specs=[VM, VM],
        scratch_shapes=[
            pltpu.VMEM((2, 4, 4, CHUNK, HALF), BF16),
            pltpu.VMEM((2, 4, 4, CHUNK, HALF), BF16),
            pltpu.VMEM((2, 3, 4, CHUNK, HALF), BF16),
            pltpu.VMEM((2, 4, CHUNK, HALF), BF16),
            pltpu.VMEM((2, 3, CHUNK, HALF), BF16),
            pltpu.SemaphoreType.DMA((2, 2)),
            pltpu.SemaphoreType.DMA((2, 3, 2)),
            pltpu.SemaphoreType.DMA((2, 3, 2)),
        ],
        compiler_params=pltpu.CompilerParams(
            collective_id=1, has_side_effects=True, vmem_limit_bytes=40 << 20
        ),
        name="scatter",
    )(part)


def passed_along(array, axis, by):
    peers = lax.axis_size(axis)
    pairs = [(i, i + by) for i in range(peers) if 0 <= i + by < peers]
    return lax.ppermute(array, axis, pairs)


def body(
    embeddings, in_proj, out_proj, hist_cache, hist_len, block_mask, block_owner, block_slot, cotangent
):
    sections = lax.axis_size("section")
    section = lax.axis_index("section")
    w_in, w_out = in_proj[0], out_proj[0]
    requests = USERS * HBLK
    owner = block_owner.reshape(requests)
    order = jnp.arange(requests, dtype=jnp.int32)
    earlier = (owner[:, None] == owner[None, :]) & (order[None, :] < order[:, None])
    where = owner * CAP + jnp.sum(earlier.astype(jnp.int32), axis=1)
    names = jnp.arange(128, dtype=jnp.int32)
    table = jnp.sum(
        jnp.where(where[:, None] == names[None, :], block_slot.reshape(requests, 1), 0), axis=0
    )
    start = jnp.arange(HBLK, dtype=jnp.int32)[None, :] * EVT
    live = jnp.where(block_mask > 0, jnp.clip(hist_len[:, None] - start, 0, EVT), 0).reshape(requests)
    fetched = exchange(table.reshape(1, 128), hist_cache[0]).reshape(OWNERS * CAP, EVT, 2 * HA)

    x = embeddings
    for step in range(sections):
        made = forward(where, live, x, w_in, w_out, fetched, step == sections - 1)
        if step < sections - 1:
            arriving = passed_along(made[0], "section", 1)
            x = jnp.where(section == step + 1, arriving, x)
    y, x_norm, act, slope_in, slope, own_weights, value, gated, rate = made
    dy = cotangent
    kept = (act, slope_in, slope, own_weights, value, rate)
    for step in reversed(range(sections)):
        dx, dproj = backward(where, live, x, dy, w_in, w_out, fetched, kept)
        if step > 0:
            arriving = passed_along(dx, "section", -1)
            dy = jnp.where(section == step - 1, arriving, dy)
    part = jnp.concatenate([dot(x_norm, dproj, 0, 0), dot(dy, gated, 0, 0)], axis=1).astype(BF16)
    grad_in, grad_out = summed(part.reshape(4, 4, 2, CHUNK, 5 * HA))
    return (y[None], dx[None], grad_in[None], grad_out[None])


def solution(mesh):
    placed = (
        P("dp", None),
        P("section", None, None),
        P("section", None, None),
        P("section", "dp", None, None),
        P("dp"),
        P("dp", None),
        P("dp", None, None),
        P("dp", None),
        P("dp", None),
    )
    return jax.shard_map(
        body,
        mesh=mesh,
        in_specs=placed,
        out_specs=(
            P("section", "dp", None),
            P("section", "dp", None),
            P("section", "dp", None),
            P("section", "dp", None),
        ),
        check_vma=False,
    )
```

```python
from functools import partial
import math

import jax
import jax.numpy as jnp
from jax import lax
from jax.experimental import pallas as pl
from jax.experimental.pallas import tpu as pltpu
from jax.sharding import PartitionSpec as P

HEADS = 4
EVT = 128
HBLK = 16
USERS = 2
ROWS = USERS * EVT
D = 1024
HA = 512
HD = HA // HEADS
CAP = 2
GROUP = 4
KEYS = HBLK * EVT
OWNERS = 32
epsilon = 1e-06
SCALE = 1.0 / math.sqrt(HD)
MESH = pl.DeviceIdType.MESH
F32 = jnp.float32
BF16 = jnp.bfloat16


def dot(a, b, ca=1, cb=0):
    return lax.dot_general(a, b, (((ca,), (cb,)), ((), ())), preferred_element_type=F32)


def normed(values):
    centred = values - jnp.mean(values, axis=-1, keepdims=True)
    inverse = lax.rsqrt(jnp.mean(centred * centred, axis=-1, keepdims=True) + epsilon)
    return centred * inverse, inverse


def norm_back(grad, value, inverse):
    return inverse * (
        grad
        - jnp.mean(grad, axis=-1, keepdims=True)
        - value * jnp.mean(grad * value, axis=-1, keepdims=True)
    )


def silu_parts(half):
    t = jnp.tanh(half)
    return half + half * t, 0.5 * ((1.0 + t) + half * (1.0 - t * t))


def chip_at(offset):
    me = lax.axis_index("dp")
    y, z, c = me // 8, lax.rem(me // 2, 4), lax.rem(me, 2)
    return (
        lax.rem(y + offset[0] + 4, 4) * 8 + lax.rem(z + offset[1] + 4, 4) * 2 + lax.rem(c + offset[2] + 2, 2)
    )


CHIPS = [(1, 1), (3, 3), (2, 0), (0, 2), (1, 3), (3, 1), (2, 2), (1, 0), (3, 0), (0, 1), (0, 3), (1, 2), (3, 2), (2, 1), (2, 3)]
OFFSETS = [(a, b, c) for a, b in CHIPS for c in (0, 1)] + [(0, 0, 1)]


def opposite(offset):
    return tuple(-part for part in offset)


def exchange_kernel(
    table_ref, cache_ref, out_ref, asked, asked_s, outgoing, ask_send, ask_recv, send_sem, recv_sem, local_sem
):
    me = lax.axis_index("dp")
    barrier = pltpu.get_barrier_semaphore()
    for offset in OFFSETS:
        pl.semaphore_signal(barrier, inc=1, device_id={"dp": chip_at(offset)}, device_id_type=MESH)
    pl.semaphore_wait(barrier, OWNERS - 1)

    asks = []
    for i, offset in enumerate(OFFSETS):
        asks.append(
            pltpu.make_async_remote_copy(
                src_ref=table_ref,
                dst_ref=asked.at[i],
                send_sem=ask_send.at[i],
                recv_sem=ask_recv.at[i],
                device_id={"dp": chip_at(offset)},
                device_id_type=MESH,
            )
        )
        asks[-1].start()
    own = pltpu.make_async_copy(table_ref, asked.at[OWNERS - 1], local_sem.at[0])
    own.start()
    own.wait()
    for ask in asks:
        ask.wait()
    down = pltpu.make_async_copy(asked, asked_s, local_sem.at[1])
    down.start()
    down.wait()

    def fill(slot, row):
        for k in range(CAP):
            outgoing[slot, k] = cache_ref[asked_s[row, 0, me * CAP + k]]

    sends = []
    for i, offset in enumerate(OFFSETS):
        back = tuple((-p) % n for p, n in zip(offset, (4, 4, 2)))
        fill(i, OFFSETS.index(back))
        sends.append(
            pltpu.make_async_remote_copy(
                src_ref=outgoing.at[i],
                dst_ref=out_ref.at[me],
                send_sem=send_sem.at[i],
                recv_sem=recv_sem.at[i],
                device_id={"dp": chip_at(offset)},
                device_id_type=MESH,
            )
        )
        sends[-1].start()
    fill(OWNERS - 1, OWNERS - 1)
    kept = pltpu.make_async_copy(outgoing.at[OWNERS - 1], out_ref.at[me], local_sem.at[2])
    kept.start()
    for send in sends:
        send.wait()
    kept.wait()


def exchange(table, cache):
    return pl.pallas_call(
        exchange_kernel,
        out_shape=jax.ShapeDtypeStruct((OWNERS, CAP, EVT, 2 * HA), BF16),
        in_specs=[pl.BlockSpec(memory_space=pltpu.VMEM)] * 2,
        out_specs=pl.BlockSpec(memory_space=pl.ANY),
        scratch_shapes=[
            pltpu.VMEM((OWNERS, 1, 128), jnp.int32),
            pltpu.SMEM((OWNERS, 1, 128), jnp.int32),
            pltpu.VMEM((OWNERS, CAP, EVT, 2 * HA), BF16),
            pltpu.SemaphoreType.DMA((OWNERS,)),
            pltpu.SemaphoreType.DMA((OWNERS,)),
            pltpu.SemaphoreType.DMA((OWNERS,)),
            pltpu.SemaphoreType.DMA((OWNERS,)),
            pltpu.SemaphoreType.DMA((3,)),
        ],
        compiler_params=pltpu.CompilerParams(
            collective_id=0, has_side_effects=True, vmem_limit_bytes=48 << 20
        ),
        name="exchange",
    )(table, cache)


VM = pl.BlockSpec(memory_space=pltpu.VMEM)
SM = pl.BlockSpec(memory_space=pltpu.SMEM)
ANY = pl.BlockSpec(memory_space=pl.ANY)


def columns(start):
    return pl.ds(pl.multiple_of(start, HD), HD)


def window_kernel(
    where_ref, live_ref, x_ref, cot_ref, w_in_ref, w_out_ref, fetched_ref,
    y_ref, dx_ref, x_norm_ref, dproj_ref, dy_ref, gated_ref,
    fetched, hist, x_now, x_value, x_rate, act, slope_in, slope, own_weights, mixed, value_ref, rate_ref, dmixed,
    x_arrived, dy_arrived, hist_sem, x_send, x_recv, dy_send, dy_recv,
):
    section = lax.axis_index("section")
    dp = lax.axis_index("dp")
    after, before = lax.rem(section + 1, 4), lax.rem(section + 3, 4)
    barrier = pltpu.get_barrier_semaphore()
    for peer in (before, after):
        pl.semaphore_signal(barrier, inc=1, device_id=(peer, dp), device_id_type=MESH)

    load = pltpu.make_async_copy(fetched_ref, fetched, hist_sem)
    load.start()
    pl.semaphore_wait(barrier, 2)

    def user_rows(user):
        return pl.ds(pl.multiple_of(user * EVT, EVT), EVT)

    def hop(src, dst, user, sends, recvs, peer):
        rows = user_rows(user)
        return pltpu.make_async_remote_copy(
            src_ref=src.at[rows],
            dst_ref=dst.at[rows],
            send_sem=sends.at[user],
            recv_sem=recvs.at[user],
            device_id=(peer, dp),
            device_id_type=MESH,
        )

    def x_hop(user):
        return hop(y_ref, x_arrived, user, x_send, x_recv, after)

    def dy_hop(user):
        return hop(dx_ref, dy_arrived, user, dy_send, dy_recv, before)

    row_of_block = lax.broadcasted_iota(jnp.int32, (EVT, HA), 0)
    causal = lax.broadcasted_iota(jnp.int32, (EVT, EVT), 1) <= lax.broadcasted_iota(
        jnp.int32, (EVT, EVT), 0
    )

    def inverse_count(user):
        total = live_ref[user * HBLK]
        for j in range(1, HBLK):
            total = total + live_ref[user * HBLK + j]
        return 1.0 / (jnp.full((EVT, 1), total, jnp.int32).astype(F32) + float(EVT))

    def history(user, group, start):
        blocks = pl.ds(user * HBLK + group * GROUP, GROUP)
        return hist[blocks, :, columns(start)].reshape(GROUP * EVT, HD)

    def place(r, carry):
        block = fetched[where_ref[r]]
        keep = (row_of_block < live_ref[r]).astype(F32).astype(BF16)
        hist[r, :, :HA] = block[:, :HA]
        hist[r, :, HA:] = block[:, HA:] * keep
        return carry

    @pl.when(section > 0)
    def _():
        load.wait()
        lax.fori_loop(0, USERS * HBLK, place, 0)

    def forward_user(user, carry):
        rows = user_rows(user)

        @pl.when(section == 0)
        def _():
            x_now[rows] = x_ref[rows]

        @pl.when(section > 0)
        def _():
            x_hop(user).wait_recv()
            x_now[rows] = x_arrived[rows]

        x = x_now[rows].astype(F32)
        normal, rate = normed(x)
        x_value[rows] = normal
        x_rate[rows] = jnp.broadcast_to(rate, (EVT, 128))
        x_norm = normal.astype(BF16)
        x_norm_ref[rows] = x_norm
        for c in range(4):
            part = slice(c * HA, (c + 1) * HA)
            made, rise = silu_parts(dot(x_norm, w_in_ref[:, part]) * 0.5)
            act[rows, part] = made.astype(BF16)
            slope_in[rows, part] = rise
        inverse = inverse_count(user)

        @pl.when((section == 0) & (user == 0))
        def _():
            load.wait()

        @pl.when(section == 0)
        def _():
            lax.fori_loop(user * HBLK, (user + 1) * HBLK, place, 0)

        def head_forward(head, carry):
            query = act[rows, columns(2 * HA + head * HD)]
            total = jnp.zeros((EVT, HD), F32)
            for group in range(HBLK // GROUP):
                half = dot(query, history(user, group, head * HD), 1, 1) * (0.5 * SCALE)
                weights = half + half * jnp.tanh(half)
                total += dot(weights.astype(BF16), history(user, group, HA + head * HD))
            half = dot(query, act[rows, columns(3 * HA + head * HD)], 1, 1) * (0.5 * SCALE)
            weights, rise = silu_parts(half)
            weights = jnp.where(causal, weights, 0.0).astype(BF16)
            total += dot(weights, act[rows, columns(HA + head * HD)])
            slope[user * HEADS + head, :, KEYS:] = jnp.where(causal, rise * SCALE, 0.0).astype(BF16)
            own_weights[user * HEADS + head] = weights
            mixed[rows, columns(head * HD)] = total * inverse
            return carry

        lax.fori_loop(0, HEADS, head_forward, 0)
        value, rate = normed(mixed[rows])
        gated = (value * act[rows, :HA].astype(F32)).astype(BF16)
        value_ref[rows] = value
        gated_ref[rows] = gated
        rate_ref[rows] = jnp.broadcast_to(rate, (EVT, 128))
        y_ref[rows] = (x + dot(gated, w_out_ref[...], 1, 1)).astype(BF16)

        @pl.when(section < 3)
        def _():
            x_hop(user).start()

        def head_slope(head, carry):
            query = act[rows, columns(2 * HA + head * HD)]
            for group in range(HBLK // GROUP):
                half = dot(query, history(user, group, head * HD), 1, 1) * (0.5 * SCALE)
                at = slice(group * GROUP * EVT, (group + 1) * GROUP * EVT)
                slope[user * HEADS + head, :, at] = (silu_parts(half)[1] * SCALE).astype(BF16)
            return carry

        lax.fori_loop(0, HEADS, head_slope, 0)
        return carry

    lax.fori_loop(0, USERS, forward_user, 0)

    def backward_user(user, carry):
        rows = user_rows(user)

        @pl.when(section == 3)
        def _():
            dy_ref[rows] = cot_ref[rows]

        @pl.when(section < 3)
        def _():
            dy_hop(user).wait_recv()
            dy_ref[rows] = dy_arrived[rows]

        dy = dy_ref[rows]
        dgated = dot(dy, w_out_ref[...])
        value = value_ref[rows]
        dproj_ref[rows, :HA] = (dgated * value * slope_in[rows, :HA]).astype(BF16)
        grad = norm_back(dgated * act[rows, :HA].astype(F32), value, rate_ref[rows, :1])
        dmixed[rows] = (grad * inverse_count(user)).astype(BF16)

        def head_back(head, carry):
            index = user * HEADS + head
            grad_mixed = dmixed[rows, columns(head * HD)]
            total = jnp.zeros((EVT, HD), F32)
            for group in range(HBLK // GROUP):
                rise = slope[index, :, group * GROUP * EVT : (group + 1) * GROUP * EVT].astype(F32)
                ds = (dot(grad_mixed, history(user, group, HA + head * HD), 1, 1) * rise).astype(BF16)
                total += dot(ds, history(user, group, head * HD))
            query = act[rows, columns(2 * HA + head * HD)]
            keys = act[rows, columns(3 * HA + head * HD)]
            values = act[rows, columns(HA + head * HD)]
            ds = (dot(grad_mixed, values, 1, 1) * slope[index, :, KEYS:].astype(F32)).astype(BF16)
            total += dot(ds, keys)
            dvalue = dot(own_weights[index], grad_mixed, 0, 0)
            dkey = dot(ds, query, 0, 0)
            for base, part in ((HA, dvalue), (2 * HA, total), (3 * HA, dkey)):
                at = columns(base + head * HD)
                dproj_ref[rows, at] = (part * slope_in[rows, at]).astype(BF16)
            return carry

        lax.fori_loop(0, HEADS, head_back, 0)
        dnorm = dot(dproj_ref[rows], w_in_ref[...], 1, 1)
        dx_ref[rows] = (
            dy.astype(F32) + norm_back(dnorm, x_value[rows], x_rate[rows, :1])
        ).astype(BF16)

        @pl.when(section > 0)
        def _():
            dy_hop(user).start()

        return carry

    lax.fori_loop(0, USERS, backward_user, 0)

    def finish(user, carry):
        @pl.when(section < 3)
        def _():
            x_hop(user).wait_send()

        @pl.when(section > 0)
        def _():
            dy_hop(user).wait_send()

        return carry

    lax.fori_loop(0, USERS, finish, 0)


def window(where, live, x, cot, w_in, w_out, fetched):
    heads = USERS * HEADS
    return pl.pallas_call(
        window_kernel,
        out_shape=[
            jax.ShapeDtypeStruct((ROWS, D), BF16),
            jax.ShapeDtypeStruct((ROWS, D), BF16),
            jax.ShapeDtypeStruct((ROWS, D), BF16),
            jax.ShapeDtypeStruct((ROWS, 4 * HA), BF16),
            jax.ShapeDtypeStruct((ROWS, D), BF16),
            jax.ShapeDtypeStruct((ROWS, HA), BF16),
        ],
        in_specs=[SM, SM, VM, VM, VM, VM, ANY],
        out_specs=[VM] * 6,
        scratch_shapes=[
            pltpu.VMEM(fetched.shape, BF16),
            pltpu.VMEM((USERS * HBLK, EVT, 2 * HA), BF16),
            pltpu.VMEM((ROWS, D), BF16),
            pltpu.VMEM((ROWS, D), F32),
            pltpu.VMEM((ROWS, 128), F32),
            pltpu.VMEM((ROWS, 4 * HA), BF16),
            pltpu.VMEM((ROWS, 4 * HA), F32),
            pltpu.VMEM((heads, EVT, KEYS + EVT), BF16),
            pltpu.VMEM((heads, EVT, EVT), BF16),
            pltpu.VMEM((ROWS, HA), F32),
            pltpu.VMEM((ROWS, HA), F32),
            pltpu.VMEM((ROWS, 128), F32),
            pltpu.VMEM((ROWS, HA), BF16),
            pltpu.VMEM((ROWS, D), BF16),
            pltpu.VMEM((ROWS, D), BF16),
            pltpu.SemaphoreType.DMA,
            pltpu.SemaphoreType.DMA((USERS,)),
            pltpu.SemaphoreType.DMA((USERS,)),
            pltpu.SemaphoreType.DMA((USERS,)),
            pltpu.SemaphoreType.DMA((USERS,)),
        ],
        compiler_params=pltpu.CompilerParams(
            collective_id=2, has_side_effects=True, vmem_limit_bytes=52 << 20
        ),
        name="window",
    )(where, live, x, cot, w_in, w_out, fetched)


HALF = (4 * HA + HA) // 2
CHUNK = D // OWNERS


def scatter_kernel(
    part_ref, in_ref, out_ref, pair, mine, first, middle, second, pair_sem, first_sem, second_sem
):
    me = lax.axis_index("dp")
    y, z, c = me // 8, lax.rem(me // 2, 4), lax.rem(me, 2)
    steps = (1, 3, 2)
    peers = [(0, 0, 1)] + [(s, 0, 0) for s in steps] + [(0, s, 0) for s in steps]
    barrier = pltpu.get_barrier_semaphore()
    for peer in peers:
        pl.semaphore_signal(barrier, inc=1, device_id={"dp": chip_at(peer)}, device_id_type=MESH)
    pl.semaphore_wait(barrier, len(peers))

    def copy(src, dst, sems, offset):
        made = pltpu.make_async_remote_copy(
            src_ref=src,
            dst_ref=dst,
            send_sem=sems.at[0],
            recv_sem=sems.at[1],
            device_id={"dp": chip_at(offset)},
            device_id_type=MESH,
        )
        made.start()
        return made

    cols = [pl.ds(h * HALF, HALF) for h in range(2)]
    swaps = [
        copy(part_ref.at[:, :, 1 - c, :, cols[h]], pair.at[h], pair_sem.at[h], (0, 0, 1)) for h in range(2)
    ]
    moves = [[], []]
    for h in range(2):
        swaps[h].wait()

        def join(i, carry, h=h):
            total = part_ref[i, :, c, :, h * HALF : (h + 1) * HALF].astype(F32) + pair[h, i].astype(F32)
            mine[h, i] = total.astype(BF16)
            return carry

        lax.fori_loop(0, 4, join, 0)
        for k, s in enumerate(steps):
            offset = (s, 0, 0) if h == 0 else (0, s, 0)
            at = lax.rem((z if h else y) + s, 4)
            src = mine.at[h, :, at] if h else mine.at[h, at]
            moves[h].append(copy(src, first.at[h, k], first_sem.at[h, k], offset))
    later = [[], []]
    for h in range(2):
        for move in moves[h]:
            move.wait()

        def add(i, carry, h=h):
            total = (mine[h, i, z] if h else mine[h, y, i]).astype(F32)
            for k in range(3):
                total += first[h, k, i].astype(F32)
            middle[h, i] = total.astype(BF16)
            return carry

        lax.fori_loop(0, 4, add, 0)
        for k, s in enumerate(steps):
            offset = (0, s, 0) if h == 0 else (s, 0, 0)
            at = lax.rem((y if h else z) + s, 4)
            later[h].append(copy(middle.at[h, at], second.at[h, k], second_sem.at[h, k], offset))
    for h in range(2):
        for move in later[h]:
            move.wait()
        total = middle[h, y if h else z].astype(F32)
        for k in range(3):
            total += second[h, k].astype(F32)
        if h == 0:
            in_ref[:, :HALF] = total
        else:
            in_ref[:, HALF:] = total[:, : 4 * HA - HALF]
            out_ref[...] = total[:, 4 * HA - HALF :]


def summed(part):
    return pl.pallas_call(
        scatter_kernel,
        out_shape=[
            jax.ShapeDtypeStruct((CHUNK, 4 * HA), F32),
            jax.ShapeDtypeStruct((CHUNK, HA), F32),
        ],
        in_specs=[VM],
        out_specs=[VM, VM],
        scratch_shapes=[
            pltpu.VMEM((2, 4, 4, CHUNK, HALF), BF16),
            pltpu.VMEM((2, 4, 4, CHUNK, HALF), BF16),
            pltpu.VMEM((2, 3, 4, CHUNK, HALF), BF16),
            pltpu.VMEM((2, 4, CHUNK, HALF), BF16),
            pltpu.VMEM((2, 3, CHUNK, HALF), BF16),
            pltpu.SemaphoreType.DMA((2, 2)),
            pltpu.SemaphoreType.DMA((2, 3, 2)),
            pltpu.SemaphoreType.DMA((2, 3, 2)),
        ],
        compiler_params=pltpu.CompilerParams(
            collective_id=1, has_side_effects=True, vmem_limit_bytes=40 << 20
        ),
        name="scatter",
    )(part)


def body(
    embeddings, in_proj, out_proj, hist_cache, hist_len, block_mask, block_owner, block_slot, cotangent
):
    w_in, w_out = in_proj[0], out_proj[0]
    requests = USERS * HBLK
    owner = block_owner.reshape(requests)
    order = jnp.arange(requests, dtype=jnp.int32)
    earlier = (owner[:, None] == owner[None, :]) & (order[None, :] < order[:, None])
    where = owner * CAP + jnp.sum(earlier.astype(jnp.int32), axis=1)
    names = jnp.arange(128, dtype=jnp.int32)
    table = jnp.sum(
        jnp.where(where[:, None] == names[None, :], block_slot.reshape(requests, 1), 0), axis=0
    )
    start = jnp.arange(HBLK, dtype=jnp.int32)[None, :] * EVT
    live = jnp.where(block_mask > 0, jnp.clip(hist_len[:, None] - start, 0, EVT), 0).reshape(requests)
    fetched = exchange(table.reshape(1, 128), hist_cache[0]).reshape(OWNERS * CAP, EVT, 2 * HA)

    y, dx, x_norm, dproj, dy, gated = window(
        where, live, embeddings, cotangent, w_in, w_out, fetched
    )
    part = jnp.concatenate([dot(x_norm, dproj, 0, 0), dot(dy, gated, 0, 0)], axis=1).astype(BF16)
    grad_in, grad_out = summed(part.reshape(4, 4, 2, CHUNK, 5 * HA))
    return (y[None], dx[None], grad_in[None], grad_out[None])


def solution(mesh):
    placed = (
        P("dp", None),
        P("section", None, None),
        P("section", None, None),
        P("section", "dp", None, None),
        P("dp"),
        P("dp", None),
        P("dp", None, None),
        P("dp", None),
        P("dp", None),
    )
    return jax.shard_map(
        body,
        mesh=mesh,
        in_specs=placed,
        out_specs=(
            P("section", "dp", None),
            P("section", "dp", None),
            P("section", "dp", None),
            P("section", "dp", None),
        ),
        check_vma=False,
    )
```

```python
from functools import partial
import math

import jax
import jax.numpy as jnp
from jax import lax
from jax.experimental import pallas as pl
from jax.experimental.pallas import tpu as pltpu
from jax.sharding import PartitionSpec as P

HEADS = 4
EVT = 128
HBLK = 16
USERS = 2
ROWS = USERS * EVT
D = 1024
HA = 512
HD = HA // HEADS
GROUP = 4
KEYS = HBLK * EVT
OWNERS = 32
epsilon = 1e-06
SCALE = 1.0 / math.sqrt(HD)
MESH = pl.DeviceIdType.MESH
F32 = jnp.float32
BF16 = jnp.bfloat16
VM = pl.BlockSpec(memory_space=pltpu.VMEM)
SM = pl.BlockSpec(memory_space=pltpu.SMEM)
ANY = pl.BlockSpec(memory_space=pl.ANY)


def dot(a, b, ca=1, cb=0):
    return lax.dot_general(a, b, (((ca,), (cb,)), ((), ())), preferred_element_type=F32)


def normed(values):
    centred = values - jnp.mean(values, axis=-1, keepdims=True)
    inverse = lax.rsqrt(jnp.mean(centred * centred, axis=-1, keepdims=True) + epsilon)
    return centred * inverse, inverse


def norm_back(grad, value, inverse):
    return inverse * (
        grad
        - jnp.mean(grad, axis=-1, keepdims=True)
        - value * jnp.mean(grad * value, axis=-1, keepdims=True)
    )


def silu_parts(half):
    t = jnp.tanh(half)
    return half + half * t, 0.5 * ((1.0 + t) + half * (1.0 - t * t))


def place():
    me = lax.axis_index("dp")
    return me // 8, lax.rem(me // 2, 4), lax.rem(me, 2)


def chip_at(offset):
    y, z, c = place()
    return lax.rem(y + offset[0], 4) * 8 + lax.rem(z + offset[1], 4) * 2 + lax.rem(c + offset[2], 2)


ORDER = (
    [(1, 0), (3, 0), (2, 0), (1, 1), (3, 3), (2, 1), (2, 3), (1, 3), (3, 1), (2, 2), (1, 2), (3, 2), (0, 1), (0, 3), (0, 2)],
    [(0, 1), (0, 3), (0, 2), (1, 2), (3, 2), (1, 1), (3, 3), (2, 2), (1, 3), (3, 1), (2, 1), (2, 3), (1, 0), (3, 0), (2, 0)],
)
PEERS = [(a, b, c) for a in range(4) for b in range(4) for c in range(2)][1:]
SLOTS = 4
BLOCK = (EVT, 2 * HA)


def name_of(y, z, c):
    return y * 8 + z * 2 + c


def reverse_name(y, z, c):
    return lax.rem(4 - y, 4) * 8 + lax.rem(4 - z, 4) * 2 + c


def to_peer(src, dst, send_sem, recv_sem, peer):
    return pltpu.make_async_remote_copy(
        src_ref=src,
        dst_ref=dst,
        send_sem=send_sem,
        recv_sem=recv_sem,
        device_id={"dp": peer},
        device_id_type=MESH,
    )


def greet_all(peers):
    barrier = pltpu.get_barrier_semaphore()
    for peer in peers:
        pl.semaphore_signal(barrier, inc=1, device_id={"dp": chip_at(peer)}, device_id_type=MESH)
    pl.semaphore_wait(barrier, len(peers))


def both_caches(cache_ref, cache, swap_sem, local_sem):
    core = lax.rem(lax.axis_index("dp"), 2)
    mine = cache.at[pl.ds(core * HBLK, HBLK)]
    swap = to_peer(cache_ref, mine, swap_sem.at[0], swap_sem.at[1], chip_at((0, 0, 1)))
    own = pltpu.make_async_copy(cache_ref, mine, local_sem)
    swap.start()
    own.start()
    return swap, own


def ordered(i, core):
    (y0, z0), (y1, z1) = ORDER[0][i], ORDER[1][i]
    return y0 + core * (y1 - y0), z0 + core * (z1 - z0)


def exchange_kernel(
    table_ref, cache_ref, out_ref, asked_ref, cache, asked_s, outgoing, own_blocks,
    swap_sem, ask_send, ask_recv, one_send, one_recv, two_send, two_recv, local_sem,
):
    y, z, core = place()
    chip = y * 4 + z
    greet_all(PEERS)
    swap, own = both_caches(cache_ref, cache, swap_sem, local_sem.at[0])
    asks = []
    for peer in PEERS:
        name = name_of(*peer)
        asks.append(
            to_peer(table_ref, asked_ref.at[name], ask_send.at[name], ask_recv.at[name], chip_at(peer))
        )
        asks[-1].start()
    row = pltpu.make_async_copy(table_ref, asked_ref.at[0], local_sem.at[1])
    row.start()
    row.wait()
    for ask in asks:
        ask.wait()
    down = pltpu.make_async_copy(asked_ref, asked_s, local_sem.at[2])
    down.start()
    down.wait()
    swap.wait()
    own.wait()

    sends = []
    for i in range(15):
        dy, dz = ordered(i, core)
        name = dy * 4 + dz
        for dc in range(2):
            row = reverse_name(dy, dz, dc)
            if dc == 0:
                outgoing[i, 1] = cache[asked_s[row, 0, chip * SLOTS + 1]]
                outgoing[i, 2] = cache[asked_s[row, 0, chip * SLOTS + 2]]
                src, dst = outgoing.at[i, pl.ds(1, 2)], out_ref.at[chip, pl.ds(1, 2)]
                sems = two_send.at[name], two_recv.at[name]
            else:
                outgoing[i, 0] = cache[asked_s[row, 0, chip * SLOTS]]
                src, dst = outgoing.at[i, 0], out_ref.at[chip, 0]
                sems = one_send.at[name], one_recv.at[name]
            sends.append(to_peer(src, dst, *sems, chip_at((dy, dz, dc))))
            sends[-1].start()
    for k in range(SLOTS):
        own_blocks[k] = cache[asked_s[0, 0, chip * SLOTS + k]]
    kept = pltpu.make_async_copy(own_blocks, out_ref.at[chip], local_sem.at[3])
    kept.start()
    for send in sends:
        send.wait()
    kept.wait()


def exchange(table, cache):
    return pl.pallas_call(
        exchange_kernel,
        out_shape=[
            jax.ShapeDtypeStruct((OWNERS // 2, SLOTS) + BLOCK, BF16),
            jax.ShapeDtypeStruct((OWNERS, 1, 128), jnp.int32),
        ],
        in_specs=[VM, ANY],
        out_specs=[ANY, VM],
        scratch_shapes=[
            pltpu.VMEM((2 * HBLK,) + BLOCK, BF16),
            pltpu.SMEM((OWNERS, 1, 128), jnp.int32),
            pltpu.VMEM((15, 3) + BLOCK, BF16),
            pltpu.VMEM((SLOTS,) + BLOCK, BF16),
            pltpu.SemaphoreType.DMA((2,)),
            pltpu.SemaphoreType.DMA((OWNERS,)),
            pltpu.SemaphoreType.DMA((OWNERS,)),
            pltpu.SemaphoreType.DMA((16,)),
            pltpu.SemaphoreType.DMA((16,)),
            pltpu.SemaphoreType.DMA((16,)),
            pltpu.SemaphoreType.DMA((16,)),
            pltpu.SemaphoreType.DMA((4,)),
        ],
        compiler_params=pltpu.CompilerParams(
            collective_id=0, has_side_effects=True, vmem_limit_bytes=40 << 20
        ),
        name="exchange",
    )(table, cache)


def fourth_kernel(
    asked_ref, cache_ref, got_ref, out_ref, cache, outgoing, swap_sem, send_sem, recv_sem, local_sem
):
    del got_ref
    y, z, core = place()
    chip = y * 4 + z
    peers = [(a, b, 0) for a, b in ORDER[0]]
    greet_all(peers + [(0, 0, 1)])
    swap, own = both_caches(cache_ref, cache, swap_sem, local_sem)
    swap.wait()
    own.wait()
    sends = []
    for i, (dy, dz, _) in enumerate(peers):
        outgoing[i] = cache[asked_ref[reverse_name(dy, dz, 0), 0, chip * SLOTS + 3]]
        sends.append(
            to_peer(
                outgoing.at[i], out_ref.at[chip, 3], send_sem.at[i], recv_sem.at[i], chip_at((dy, dz, 0))
            )
        )
        sends[-1].start()
    for send in sends:
        send.wait()


def fourth(asked, cache, got):
    return pl.pallas_call(
        fourth_kernel,
        out_shape=jax.ShapeDtypeStruct(got.shape, BF16),
        in_specs=[SM, ANY, ANY],
        out_specs=ANY,
        scratch_shapes=[
            pltpu.VMEM((2 * HBLK,) + BLOCK, BF16),
            pltpu.VMEM((15,) + BLOCK, BF16),
            pltpu.SemaphoreType.DMA((2,)),
            pltpu.SemaphoreType.DMA((15,)),
            pltpu.SemaphoreType.DMA((15,)),
            pltpu.SemaphoreType.DMA,
        ],
        input_output_aliases={2: 0},
        compiler_params=pltpu.CompilerParams(
            collective_id=3, has_side_effects=True, vmem_limit_bytes=24 << 20
        ),
        name="fourth",
    )(asked, cache, got)


def columns(start):
    return pl.ds(pl.multiple_of(start, HD), HD)


def window_kernel(
    where_ref, live_ref, x_ref, cot_ref, w_in_ref, w_out_ref, fetched_ref,
    y_ref, dx_ref, x_norm_ref, dproj_ref, dy_ref, gated_ref,
    fetched, hist, x_now, x_value, x_rate, act, slope_in, slope, own_weights, mixed, value_ref, rate_ref, dmixed,
    x_arrived, dy_arrived, hist_sem, x_send, x_recv, dy_send, dy_recv,
):
    section = lax.axis_index("section")
    dp = lax.axis_index("dp")
    after, before = lax.rem(section + 1, 4), lax.rem(section + 3, 4)
    barrier = pltpu.get_barrier_semaphore()
    for peer in (before, after):
        pl.semaphore_signal(barrier, inc=1, device_id=(peer, dp), device_id_type=MESH)

    load = pltpu.make_async_copy(fetched_ref, fetched, hist_sem)
    load.start()
    pl.semaphore_wait(barrier, 2)

    def user_rows(user):
        return pl.ds(pl.multiple_of(user * EVT, EVT), EVT)

    def hop(src, dst, user, sends, recvs, peer):
        rows = user_rows(user)
        return pltpu.make_async_remote_copy(
            src_ref=src.at[rows],
            dst_ref=dst.at[rows],
            send_sem=sends.at[user],
            recv_sem=recvs.at[user],
            device_id=(peer, dp),
            device_id_type=MESH,
        )

    def x_hop(user):
        return hop(y_ref, x_arrived, user, x_send, x_recv, after)

    def dy_hop(user):
        return hop(dx_ref, dy_arrived, user, dy_send, dy_recv, before)

    row_of_block = lax.broadcasted_iota(jnp.int32, (EVT, HA), 0)
    causal = lax.broadcasted_iota(jnp.int32, (EVT, EVT), 1) <= lax.broadcasted_iota(
        jnp.int32, (EVT, EVT), 0
    )

    def inverse_count(user):
        total = live_ref[user * HBLK]
        for j in range(1, HBLK):
            total = total + live_ref[user * HBLK + j]
        return 1.0 / (jnp.full((EVT, 1), total, jnp.int32).astype(F32) + float(EVT))

    def history(user, group, start):
        blocks = pl.ds(user * HBLK + group * GROUP, GROUP)
        return hist[blocks, :, columns(start)].reshape(GROUP * EVT, HD)

    def settle(r, carry):
        block = fetched[where_ref[r]]
        keep = (row_of_block < live_ref[r]).astype(F32).astype(BF16)
        hist[r, :, :HA] = block[:, :HA]
        hist[r, :, HA:] = block[:, HA:] * keep
        return carry

    @pl.when(section > 0)
    def _():
        load.wait()
        lax.fori_loop(0, USERS * HBLK, settle, 0)

    def forward_user(user, carry):
        rows = user_rows(user)

        @pl.when(section == 0)
        def _():
            x_now[rows] = x_ref[rows]

        @pl.when(section > 0)
        def _():
            x_hop(user).wait_recv()
            x_now[rows] = x_arrived[rows]

        x = x_now[rows].astype(F32)
        normal, rate = normed(x)
        x_value[rows] = normal
        x_rate[rows] = jnp.broadcast_to(rate, (EVT, 128))
        x_norm = normal.astype(BF16)
        x_norm_ref[rows] = x_norm
        for c in range(4):
            part = slice(c * HA, (c + 1) * HA)
            made, rise = silu_parts(dot(x_norm, w_in_ref[:, part]) * 0.5)
            act[rows, part] = made.astype(BF16)
            slope_in[rows, part] = rise
        inverse = inverse_count(user)

        @pl.when((section == 0) & (user == 0))
        def _():
            load.wait()

        @pl.when(section == 0)
        def _():
            lax.fori_loop(user * HBLK, (user + 1) * HBLK, settle, 0)

        def head_forward(head, carry):
            query = act[rows, columns(2 * HA + head * HD)]
            total = jnp.zeros((EVT, HD), F32)
            for group in range(HBLK // GROUP):
                half = dot(query, history(user, group, head * HD), 1, 1) * (0.5 * SCALE)
                weights = half + half * jnp.tanh(half)
                total += dot(weights.astype(BF16), history(user, group, HA + head * HD))
            half = dot(query, act[rows, columns(3 * HA + head * HD)], 1, 1) * (0.5 * SCALE)
            weights, rise = silu_parts(half)
            weights = jnp.where(causal, weights, 0.0).astype(BF16)
            total += dot(weights, act[rows, columns(HA + head * HD)])
            slope[user * HEADS + head, :, KEYS:] = jnp.where(causal, rise * SCALE, 0.0).astype(BF16)
            own_weights[user * HEADS + head] = weights
            mixed[rows, columns(head * HD)] = total * inverse
            return carry

        lax.fori_loop(0, HEADS, head_forward, 0)
        value, rate = normed(mixed[rows])
        gated = (value * act[rows, :HA].astype(F32)).astype(BF16)
        value_ref[rows] = value
        gated_ref[rows] = gated
        rate_ref[rows] = jnp.broadcast_to(rate, (EVT, 128))
        y_ref[rows] = (x + dot(gated, w_out_ref[...], 1, 1)).astype(BF16)

        @pl.when(section < 3)
        def _():
            x_hop(user).start()

        def head_slope(head, carry):
            query = act[rows, columns(2 * HA + head * HD)]
            for group in range(HBLK // GROUP):
                half = dot(query, history(user, group, head * HD), 1, 1) * (0.5 * SCALE)
                at = slice(group * GROUP * EVT, (group + 1) * GROUP * EVT)
                slope[user * HEADS + head, :, at] = (silu_parts(half)[1] * SCALE).astype(BF16)
            return carry

        lax.fori_loop(0, HEADS, head_slope, 0)
        return carry

    lax.fori_loop(0, USERS, forward_user, 0)

    def backward_user(user, carry):
        rows = user_rows(user)

        @pl.when(section == 3)
        def _():
            dy_ref[rows] = cot_ref[rows]

        @pl.when(section < 3)
        def _():
            dy_hop(user).wait_recv()
            dy_ref[rows] = dy_arrived[rows]

        dy = dy_ref[rows]
        dgated = dot(dy, w_out_ref[...])
        value = value_ref[rows]
        dproj_ref[rows, :HA] = (dgated * value * slope_in[rows, :HA]).astype(BF16)
        grad = norm_back(dgated * act[rows, :HA].astype(F32), value, rate_ref[rows, :1])
        dmixed[rows] = (grad * inverse_count(user)).astype(BF16)

        def head_back(head, carry):
            index = user * HEADS + head
            grad_mixed = dmixed[rows, columns(head * HD)]
            total = jnp.zeros((EVT, HD), F32)
            for group in range(HBLK // GROUP):
                rise = slope[index, :, group * GROUP * EVT : (group + 1) * GROUP * EVT].astype(F32)
                ds = (dot(grad_mixed, history(user, group, HA + head * HD), 1, 1) * rise).astype(BF16)
                total += dot(ds, history(user, group, head * HD))
            query = act[rows, columns(2 * HA + head * HD)]
            keys = act[rows, columns(3 * HA + head * HD)]
            values = act[rows, columns(HA + head * HD)]
            ds = (dot(grad_mixed, values, 1, 1) * slope[index, :, KEYS:].astype(F32)).astype(BF16)
            total += dot(ds, keys)
            dvalue = dot(own_weights[index], grad_mixed, 0, 0)
            dkey = dot(ds, query, 0, 0)
            for base, part in ((HA, dvalue), (2 * HA, total), (3 * HA, dkey)):
                at = columns(base + head * HD)
                dproj_ref[rows, at] = (part * slope_in[rows, at]).astype(BF16)
            return carry

        lax.fori_loop(0, HEADS, head_back, 0)
        dnorm = dot(dproj_ref[rows], w_in_ref[...], 1, 1)
        dx_ref[rows] = (
            dy.astype(F32) + norm_back(dnorm, x_value[rows], x_rate[rows, :1])
        ).astype(BF16)

        @pl.when(section > 0)
        def _():
            dy_hop(user).start()

        return carry

    lax.fori_loop(0, USERS, backward_user, 0)

    def finish(user, carry):
        @pl.when(section < 3)
        def _():
            x_hop(user).wait_send()

        @pl.when(section > 0)
        def _():
            dy_hop(user).wait_send()

        return carry

    lax.fori_loop(0, USERS, finish, 0)


def window(where, live, x, cot, w_in, w_out, fetched):
    heads = USERS * HEADS
    return pl.pallas_call(
        window_kernel,
        out_shape=[
            jax.ShapeDtypeStruct((ROWS, D), BF16),
            jax.ShapeDtypeStruct((ROWS, D), BF16),
            jax.ShapeDtypeStruct((ROWS, D), BF16),
            jax.ShapeDtypeStruct((ROWS, 4 * HA), BF16),
            jax.ShapeDtypeStruct((ROWS, D), BF16),
            jax.ShapeDtypeStruct((ROWS, HA), BF16),
        ],
        in_specs=[SM, SM, VM, VM, VM, VM, ANY],
        out_specs=[VM] * 6,
        scratch_shapes=[
            pltpu.VMEM(fetched.shape, BF16),
            pltpu.VMEM((USERS * HBLK, EVT, 2 * HA), BF16),
            pltpu.VMEM((ROWS, D), BF16),
            pltpu.VMEM((ROWS, D), F32),
            pltpu.VMEM((ROWS, 128), F32),
            pltpu.VMEM((ROWS, 4 * HA), BF16),
            pltpu.VMEM((ROWS, 4 * HA), F32),
            pltpu.VMEM((heads, EVT, KEYS + EVT), BF16),
            pltpu.VMEM((heads, EVT, EVT), BF16),
            pltpu.VMEM((ROWS, HA), F32),
            pltpu.VMEM((ROWS, HA), F32),
            pltpu.VMEM((ROWS, 128), F32),
            pltpu.VMEM((ROWS, HA), BF16),
            pltpu.VMEM((ROWS, D), BF16),
            pltpu.VMEM((ROWS, D), BF16),
            pltpu.SemaphoreType.DMA,
            pltpu.SemaphoreType.DMA((USERS,)),
            pltpu.SemaphoreType.DMA((USERS,)),
            pltpu.SemaphoreType.DMA((USERS,)),
            pltpu.SemaphoreType.DMA((USERS,)),
        ],
        compiler_params=pltpu.CompilerParams(
            collective_id=2, has_side_effects=True, vmem_limit_bytes=52 << 20
        ),
        name="window",
    )(where, live, x, cot, w_in, w_out, fetched)


HALF = (4 * HA + HA) // 2
CHUNK = D // OWNERS


def scatter_kernel(
    part_ref, in_ref, out_ref, pair, mine, first, middle, second, pair_sem, first_sem, second_sem
):
    me = lax.axis_index("dp")
    y, z, c = me // 8, lax.rem(me // 2, 4), lax.rem(me, 2)
    steps = (1, 3, 2)
    peers = [(0, 0, 1)] + [(s, 0, 0) for s in steps] + [(0, s, 0) for s in steps]
    barrier = pltpu.get_barrier_semaphore()
    for peer in peers:
        pl.semaphore_signal(barrier, inc=1, device_id={"dp": chip_at(peer)}, device_id_type=MESH)
    pl.semaphore_wait(barrier, len(peers))

    def copy(src, dst, sems, offset):
        made = pltpu.make_async_remote_copy(
            src_ref=src,
            dst_ref=dst,
            send_sem=sems.at[0],
            recv_sem=sems.at[1],
            device_id={"dp": chip_at(offset)},
            device_id_type=MESH,
        )
        made.start()
        return made

    cols = [pl.ds(h * HALF, HALF) for h in range(2)]
    swaps = [
        copy(part_ref.at[:, :, 1 - c, :, cols[h]], pair.at[h], pair_sem.at[h], (0, 0, 1)) for h in range(2)
    ]
    moves = [[], []]
    for h in range(2):
        swaps[h].wait()

        def join(i, carry, h=h):
            total = part_ref[i, :, c, :, h * HALF : (h + 1) * HALF].astype(F32) + pair[h, i].astype(F32)
            mine[h, i] = total.astype(BF16)
            return carry

        lax.fori_loop(0, 4, join, 0)
        for k, s in enumerate(steps):
            offset = (s, 0, 0) if h == 0 else (0, s, 0)
            at = lax.rem((z if h else y) + s, 4)
            src = mine.at[h, :, at] if h else mine.at[h, at]
            moves[h].append(copy(src, first.at[h, k], first_sem.at[h, k], offset))
    later = [[], []]
    for h in range(2):
        for move in moves[h]:
            move.wait()

        def add(i, carry, h=h):
            total = (mine[h, i, z] if h else mine[h, y, i]).astype(F32)
            for k in range(3):
                total += first[h, k, i].astype(F32)
            middle[h, i] = total.astype(BF16)
            return carry

        lax.fori_loop(0, 4, add, 0)
        for k, s in enumerate(steps):
            offset = (0, s, 0) if h == 0 else (s, 0, 0)
            at = lax.rem((y if h else z) + s, 4)
            later[h].append(copy(middle.at[h, at], second.at[h, k], second_sem.at[h, k], offset))
    for h in range(2):
        for move in later[h]:
            move.wait()
        total = middle[h, y if h else z].astype(F32)
        for k in range(3):
            total += second[h, k].astype(F32)
        if h == 0:
            in_ref[:, :HALF] = total
        else:
            in_ref[:, HALF:] = total[:, : 4 * HA - HALF]
            out_ref[...] = total[:, 4 * HA - HALF :]


def summed(part):
    return pl.pallas_call(
        scatter_kernel,
        out_shape=[
            jax.ShapeDtypeStruct((CHUNK, 4 * HA), F32),
            jax.ShapeDtypeStruct((CHUNK, HA), F32),
        ],
        in_specs=[VM],
        out_specs=[VM, VM],
        scratch_shapes=[
            pltpu.VMEM((2, 4, 4, CHUNK, HALF), BF16),
            pltpu.VMEM((2, 4, 4, CHUNK, HALF), BF16),
            pltpu.VMEM((2, 3, 4, CHUNK, HALF), BF16),
            pltpu.VMEM((2, 4, CHUNK, HALF), BF16),
            pltpu.VMEM((2, 3, CHUNK, HALF), BF16),
            pltpu.SemaphoreType.DMA((2, 2)),
            pltpu.SemaphoreType.DMA((2, 3, 2)),
            pltpu.SemaphoreType.DMA((2, 3, 2)),
        ],
        compiler_params=pltpu.CompilerParams(
            collective_id=1, has_side_effects=True, vmem_limit_bytes=40 << 20
        ),
        name="scatter",
    )(part)


def body(
    embeddings, in_proj, out_proj, hist_cache, hist_len, block_mask, block_owner, block_slot, cotangent
):
    w_in, w_out = in_proj[0], out_proj[0]
    requests = USERS * HBLK
    start = jnp.arange(HBLK, dtype=jnp.int32)[None, :] * EVT
    live = jnp.where(block_mask > 0, jnp.clip(hist_len[:, None] - start, 0, EVT), 0).reshape(requests)
    wanted = live > 0
    owner = jnp.where(wanted, block_owner.reshape(requests), -2)
    order = jnp.arange(requests, dtype=jnp.int32)
    earlier = (owner[:, None] == owner[None, :]) & (order[None, :] < order[:, None])
    rank = jnp.sum(earlier.astype(jnp.int32), axis=1)
    beside = jnp.sum(((owner ^ 1)[:, None] == owner[None, :]).astype(jnp.int32), axis=1)
    me = lax.axis_index("dp")
    chip, core, side = owner // 2, owner % 2, me % 2
    slot = jnp.where(rank == 0, jnp.where(core == side, 1, 0), jnp.where((core == 1) & (beside == 2), 3, 2))
    where = jnp.where(wanted, chip * SLOTS + slot, me // 2 * SLOTS)
    names = jnp.arange(128, dtype=jnp.int32)
    number = core * HBLK + block_slot.reshape(requests)
    late = wanted & (slot == 3) & (chip != me // 2)
    here = (where[:, None] == names[None, :]) & wanted[:, None]
    table = jnp.sum(
        jnp.where(here, number[:, None], 0)
        + jnp.where(late[:, None] & (names[None, :] == 127), 1, 0),
        axis=0,
    )
    cache = hist_cache[0]
    got, asked = exchange(table.reshape(1, 128), cache)
    got = lax.cond(
        jnp.max(asked[:, 0, 127]) > 0, lambda g: fourth(asked, cache, g), lambda g: g, got
    )
    fetched = got.reshape(OWNERS // 2 * SLOTS, EVT, 2 * HA)
    y, dx, x_norm, dproj, dy, gated = window(
        where, live, embeddings, cotangent, w_in, w_out, fetched
    )
    part = jnp.concatenate([dot(x_norm, dproj, 0, 0), dot(dy, gated, 0, 0)], axis=1).astype(BF16)
    grad_in, grad_out = summed(part.reshape(4, 4, 2, CHUNK, 5 * HA))
    return (y[None], dx[None], grad_in[None], grad_out[None])


def solution(mesh):
    placed = (
        P("dp", None),
        P("section", None, None),
        P("section", None, None),
        P("section", "dp", None, None),
        P("dp"),
        P("dp", None),
        P("dp", None, None),
        P("dp", None),
        P("dp", None),
    )
    return jax.shard_map(
        body,
        mesh=mesh,
        in_specs=placed,
        out_specs=(
            P("section", "dp", None),
            P("section", "dp", None),
            P("section", "dp", None),
            P("section", "dp", None),
        ),
        check_vma=False,
    )
```

```python
from functools import partial
import math

import jax
import jax.numpy as jnp
from jax import lax
from jax.experimental import pallas as pl
from jax.experimental.pallas import tpu as pltpu
from jax.sharding import PartitionSpec as P

HEADS = 4
EVT = 128
HBLK = 16
USERS = 2
ROWS = USERS * EVT
D = 1024
HA = 512
HD = HA // HEADS
GROUP = 8
KEYS = HBLK * EVT
OWNERS = 32
epsilon = 1e-06
SCALE = 1.0 / math.sqrt(HD)
MESH = pl.DeviceIdType.MESH
F32 = jnp.float32
BF16 = jnp.bfloat16
VM = pl.BlockSpec(memory_space=pltpu.VMEM)
SM = pl.BlockSpec(memory_space=pltpu.SMEM)
ANY = pl.BlockSpec(memory_space=pl.ANY)


def dot(a, b, ca=1, cb=0):
    return lax.dot_general(a, b, (((ca,), (cb,)), ((), ())), preferred_element_type=F32)


def normed(values):
    centred = values - jnp.mean(values, axis=-1, keepdims=True)
    inverse = lax.rsqrt(jnp.mean(centred * centred, axis=-1, keepdims=True) + epsilon)
    return centred * inverse, inverse


def norm_back(grad, value, inverse):
    return inverse * (
        grad
        - jnp.mean(grad, axis=-1, keepdims=True)
        - value * jnp.mean(grad * value, axis=-1, keepdims=True)
    )


def silu_parts(half):
    t = jnp.tanh(half)
    return half + half * t, 0.5 * ((1.0 + t) + half * (1.0 - t * t))


def place():
    me = lax.axis_index("dp")
    return me // 8, lax.rem(me // 2, 4), lax.rem(me, 2)


def chip_at(offset):
    y, z, c = place()
    return lax.rem(y + offset[0], 4) * 8 + lax.rem(z + offset[1], 4) * 2 + lax.rem(c + offset[2], 2)


ORDER = (
    [(1, 0), (3, 0), (2, 0), (1, 1), (3, 3), (2, 1), (2, 3), (1, 3), (3, 1), (2, 2), (1, 2), (3, 2), (0, 1), (0, 3), (0, 2)],
    [(0, 1), (0, 3), (0, 2), (1, 2), (3, 2), (1, 1), (3, 3), (2, 2), (1, 3), (3, 1), (2, 1), (2, 3), (1, 0), (3, 0), (2, 0)],
)
PEERS = [(a, b, c) for a in range(4) for b in range(4) for c in range(2)][1:]
SLOTS = 4
BLOCK = (EVT, 2 * HA)


def name_of(y, z, c):
    return y * 8 + z * 2 + c


def reverse_name(y, z, c):
    return lax.rem(4 - y, 4) * 8 + lax.rem(4 - z, 4) * 2 + c


def to_peer(src, dst, send_sem, recv_sem, peer):
    return pltpu.make_async_remote_copy(
        src_ref=src,
        dst_ref=dst,
        send_sem=send_sem,
        recv_sem=recv_sem,
        device_id={"dp": peer},
        device_id_type=MESH,
    )


def greet_all(peers):
    barrier = pltpu.get_barrier_semaphore()
    for peer in peers:
        pl.semaphore_signal(barrier, inc=1, device_id={"dp": chip_at(peer)}, device_id_type=MESH)
    pl.semaphore_wait(barrier, len(peers))


def both_caches(cache_ref, cache, swap_sem, local_sem):
    core = lax.rem(lax.axis_index("dp"), 2)
    mine = cache.at[pl.ds(core * HBLK, HBLK)]
    swap = to_peer(cache_ref, mine, swap_sem.at[0], swap_sem.at[1], chip_at((0, 0, 1)))
    own = pltpu.make_async_copy(cache_ref, mine, local_sem)
    swap.start()
    own.start()
    return swap, own


def ordered(i, core):
    (y0, z0), (y1, z1) = ORDER[0][i], ORDER[1][i]
    return y0 + core * (y1 - y0), z0 + core * (z1 - z0)


def exchange_kernel(
    table_ref, cache_ref, out_ref, asked_ref, cache, asked_s, outgoing, own_blocks,
    swap_sem, ask_send, ask_recv, one_send, one_recv, two_send, two_recv, local_sem,
):
    y, z, core = place()
    chip = y * 4 + z
    greet_all(PEERS)
    swap, own = both_caches(cache_ref, cache, swap_sem, local_sem.at[0])
    asks = []
    for peer in PEERS:
        name = name_of(*peer)
        asks.append(
            to_peer(table_ref, asked_ref.at[name], ask_send.at[name], ask_recv.at[name], chip_at(peer))
        )
        asks[-1].start()
    row = pltpu.make_async_copy(table_ref, asked_ref.at[0], local_sem.at[1])
    row.start()
    row.wait()
    for ask in asks:
        ask.wait()
    down = pltpu.make_async_copy(asked_ref, asked_s, local_sem.at[2])
    down.start()
    down.wait()
    swap.wait()
    own.wait()

    sends = []
    for i in range(15):
        dy, dz = ordered(i, core)
        name = dy * 4 + dz
        for dc in range(2):
            row = reverse_name(dy, dz, dc)
            if dc == 0:
                outgoing[i, 1] = cache[asked_s[row, 0, chip * SLOTS + 1]]
                outgoing[i, 2] = cache[asked_s[row, 0, chip * SLOTS + 2]]
                src, dst = outgoing.at[i, pl.ds(1, 2)], out_ref.at[chip, pl.ds(1, 2)]
                sems = two_send.at[name], two_recv.at[name]
            else:
                outgoing[i, 0] = cache[asked_s[row, 0, chip * SLOTS]]
                src, dst = outgoing.at[i, 0], out_ref.at[chip, 0]
                sems = one_send.at[name], one_recv.at[name]
            sends.append(to_peer(src, dst, *sems, chip_at((dy, dz, dc))))
            sends[-1].start()
    for k in range(SLOTS):
        own_blocks[k] = cache[asked_s[0, 0, chip * SLOTS + k]]
    kept = pltpu.make_async_copy(own_blocks, out_ref.at[chip], local_sem.at[3])
    kept.start()
    for send in sends:
        send.wait()
    kept.wait()


def exchange(table, cache):
    return pl.pallas_call(
        exchange_kernel,
        out_shape=[
            jax.ShapeDtypeStruct((OWNERS // 2, SLOTS) + BLOCK, BF16),
            jax.ShapeDtypeStruct((OWNERS, 1, 128), jnp.int32),
        ],
        in_specs=[VM, ANY],
        out_specs=[ANY, VM],
        scratch_shapes=[
            pltpu.VMEM((2 * HBLK,) + BLOCK, BF16),
            pltpu.SMEM((OWNERS, 1, 128), jnp.int32),
            pltpu.VMEM((15, 3) + BLOCK, BF16),
            pltpu.VMEM((SLOTS,) + BLOCK, BF16),
            pltpu.SemaphoreType.DMA((2,)),
            pltpu.SemaphoreType.DMA((OWNERS,)),
            pltpu.SemaphoreType.DMA((OWNERS,)),
            pltpu.SemaphoreType.DMA((16,)),
            pltpu.SemaphoreType.DMA((16,)),
            pltpu.SemaphoreType.DMA((16,)),
            pltpu.SemaphoreType.DMA((16,)),
            pltpu.SemaphoreType.DMA((4,)),
        ],
        compiler_params=pltpu.CompilerParams(
            collective_id=0, has_side_effects=True, vmem_limit_bytes=40 << 20
        ),
        name="exchange",
    )(table, cache)


def fourth_kernel(
    asked_ref, cache_ref, got_ref, out_ref, cache, outgoing, swap_sem, send_sem, recv_sem, local_sem
):
    del got_ref
    y, z, core = place()
    chip = y * 4 + z
    peers = [(a, b, 0) for a, b in ORDER[0]]
    greet_all(peers + [(0, 0, 1)])
    swap, own = both_caches(cache_ref, cache, swap_sem, local_sem)
    swap.wait()
    own.wait()
    sends = []
    for i, (dy, dz, _) in enumerate(peers):
        outgoing[i] = cache[asked_ref[reverse_name(dy, dz, 0), 0, chip * SLOTS + 3]]
        sends.append(
            to_peer(
                outgoing.at[i], out_ref.at[chip, 3], send_sem.at[i], recv_sem.at[i], chip_at((dy, dz, 0))
            )
        )
        sends[-1].start()
    for send in sends:
        send.wait()


def fourth(asked, cache, got):
    return pl.pallas_call(
        fourth_kernel,
        out_shape=jax.ShapeDtypeStruct(got.shape, BF16),
        in_specs=[SM, ANY, ANY],
        out_specs=ANY,
        scratch_shapes=[
            pltpu.VMEM((2 * HBLK,) + BLOCK, BF16),
            pltpu.VMEM((15,) + BLOCK, BF16),
            pltpu.SemaphoreType.DMA((2,)),
            pltpu.SemaphoreType.DMA((15,)),
            pltpu.SemaphoreType.DMA((15,)),
            pltpu.SemaphoreType.DMA,
        ],
        input_output_aliases={2: 0},
        compiler_params=pltpu.CompilerParams(
            collective_id=3, has_side_effects=True, vmem_limit_bytes=24 << 20
        ),
        name="fourth",
    )(asked, cache, got)


def columns(start):
    return pl.ds(pl.multiple_of(start, HD), HD)


def window_kernel(
    where_ref, live_ref, x_ref, cot_ref, w_in_ref, w_out_ref, fetched_ref,
    y_ref, dx_ref, x_norm_ref, dproj_ref, dy_ref, gated_ref,
    fetched, hist, w_in_t, x_now, x_value, x_rate, act, slope_in, slope, own_weights, mixed, value_ref, rate_ref, dmixed,
    x_arrived, dy_arrived, hist_sem, x_send, x_recv, dy_send, dy_recv,
):
    section = lax.axis_index("section")
    dp = lax.axis_index("dp")
    after, before = lax.rem(section + 1, 4), lax.rem(section + 3, 4)
    barrier = pltpu.get_barrier_semaphore()
    for peer in (before, after):
        pl.semaphore_signal(barrier, inc=1, device_id=(peer, dp), device_id_type=MESH)

    load = pltpu.make_async_copy(fetched_ref, fetched, hist_sem)
    load.start()
    pl.semaphore_wait(barrier, 2)

    def user_rows(user):
        return pl.ds(pl.multiple_of(user * EVT, EVT), EVT)

    def hop(src, dst, user, sends, recvs, peer):
        rows = user_rows(user)
        return pltpu.make_async_remote_copy(
            src_ref=src.at[rows],
            dst_ref=dst.at[rows],
            send_sem=sends.at[user],
            recv_sem=recvs.at[user],
            device_id=(peer, dp),
            device_id_type=MESH,
        )

    def x_hop(user):
        return hop(y_ref, x_arrived, user, x_send, x_recv, after)

    def dy_hop(user):
        return hop(dx_ref, dy_arrived, user, dy_send, dy_recv, before)

    row_of_block = lax.broadcasted_iota(jnp.int32, (EVT, HA), 0)
    causal = lax.broadcasted_iota(jnp.int32, (EVT, EVT), 1) <= lax.broadcasted_iota(
        jnp.int32, (EVT, EVT), 0
    )

    def inverse_count(user):
        total = live_ref[user * HBLK]
        for j in range(1, HBLK):
            total = total + live_ref[user * HBLK + j]
        return 1.0 / (jnp.full((EVT, 1), total, jnp.int32).astype(F32) + float(EVT))

    def history(user, group, start):
        blocks = pl.ds(user * HBLK + group * GROUP, GROUP)
        return hist[blocks, :, columns(start)].reshape(GROUP * EVT, HD)

    def settle(r, carry):
        block = fetched[where_ref[r]]
        keep = (row_of_block < live_ref[r]).astype(F32).astype(BF16)
        hist[r, :, :HA] = block[:, :HA]
        hist[r, :, HA:] = block[:, HA:] * keep
        return carry

    def turn_w_in():
        for k in range(0, 4 * HA, HD):
            w_in_t[k : k + HD] = w_in_ref[:, k : k + HD].T

    @pl.when(section > 0)
    def _():
        turn_w_in()
        load.wait()
        lax.fori_loop(0, USERS * HBLK, settle, 0)

    def forward_user(user, carry):
        rows = user_rows(user)

        @pl.when(section == 0)
        def _():
            x_now[rows] = x_ref[rows]

        @pl.when(section > 0)
        def _():
            x_hop(user).wait_recv()
            x_now[rows] = x_arrived[rows]

        x = x_now[rows].astype(F32)
        normal, rate = normed(x)
        x_value[rows] = normal
        x_rate[rows] = jnp.broadcast_to(rate, (EVT, 128))
        x_norm = normal.astype(BF16)
        x_norm_ref[rows] = x_norm
        for c in range(4):
            part = slice(c * HA, (c + 1) * HA)
            made, rise = silu_parts(dot(x_norm, w_in_ref[:, part]) * 0.5)
            act[rows, part] = made.astype(BF16)
            slope_in[rows, part] = rise
        inverse = inverse_count(user)

        @pl.when((section == 0) & (user == 0))
        def _():
            load.wait()

        @pl.when(section == 0)
        def _():
            lax.fori_loop(user * HBLK, (user + 1) * HBLK, settle, 0)

        def head_forward(head, carry):
            query = act[rows, columns(2 * HA + head * HD)]
            total = jnp.zeros((EVT, HD), F32)
            for group in range(HBLK // GROUP):
                half = dot(query, history(user, group, head * HD), 1, 1) * (0.5 * SCALE)
                weights, rise = silu_parts(half)
                at = slice(group * GROUP * EVT, (group + 1) * GROUP * EVT)
                slope[user * HEADS + head, :, at] = (rise * SCALE).astype(BF16)
                total += dot(weights.astype(BF16), history(user, group, HA + head * HD))
            half = dot(query, act[rows, columns(3 * HA + head * HD)], 1, 1) * (0.5 * SCALE)
            weights, rise = silu_parts(half)
            weights = jnp.where(causal, weights, 0.0).astype(BF16)
            total += dot(weights, act[rows, columns(HA + head * HD)])
            slope[user * HEADS + head, :, KEYS:] = jnp.where(causal, rise * SCALE, 0.0).astype(BF16)
            own_weights[user * HEADS + head] = weights
            mixed[rows, columns(head * HD)] = total * inverse
            return carry

        lax.fori_loop(0, HEADS, head_forward, 0, unroll=True)
        value, rate = normed(mixed[rows])
        gated = (value * act[rows, :HA].astype(F32)).astype(BF16)
        value_ref[rows] = value
        gated_ref[rows] = gated
        rate_ref[rows] = jnp.broadcast_to(rate, (EVT, 128))
        y_ref[rows] = (x + dot(gated, w_out_ref[...], 1, 1)).astype(BF16)

        @pl.when(section < 3)
        def _():
            x_hop(user).start()

        return carry

    lax.fori_loop(0, USERS, forward_user, 0)

    @pl.when(section == 0)
    def _():
        turn_w_in()

    def backward_user(user, carry):
        rows = user_rows(user)

        @pl.when(section == 3)
        def _():
            dy_ref[rows] = cot_ref[rows]

        @pl.when(section < 3)
        def _():
            dy_hop(user).wait_recv()
            dy_ref[rows] = dy_arrived[rows]

        dy = dy_ref[rows]
        dgated = dot(dy, w_out_ref[...])
        value = value_ref[rows]
        dproj_ref[rows, :HA] = (dgated * value * slope_in[rows, :HA]).astype(BF16)
        grad = norm_back(dgated * act[rows, :HA].astype(F32), value, rate_ref[rows, :1])
        dmixed[rows] = (grad * inverse_count(user)).astype(BF16)

        def head_back(head, carry):
            index = user * HEADS + head
            grad_mixed = dmixed[rows, columns(head * HD)]
            total = jnp.zeros((EVT, HD), F32)
            for group in range(HBLK // GROUP):
                rise = slope[index, :, group * GROUP * EVT : (group + 1) * GROUP * EVT].astype(F32)
                ds = (dot(grad_mixed, history(user, group, HA + head * HD), 1, 1) * rise).astype(BF16)
                total += dot(ds, history(user, group, head * HD))
            query = act[rows, columns(2 * HA + head * HD)]
            keys = act[rows, columns(3 * HA + head * HD)]
            values = act[rows, columns(HA + head * HD)]
            ds = (dot(grad_mixed, values, 1, 1) * slope[index, :, KEYS:].astype(F32)).astype(BF16)
            total += dot(ds, keys)
            dvalue = dot(own_weights[index], grad_mixed, 0, 0)
            dkey = dot(ds, query, 0, 0)
            for base, part in ((HA, dvalue), (2 * HA, total), (3 * HA, dkey)):
                at = columns(base + head * HD)
                dproj_ref[rows, at] = (part * slope_in[rows, at]).astype(BF16)
            return carry

        lax.fori_loop(0, HEADS, head_back, 0, unroll=True)
        dnorm = dot(dproj_ref[rows], w_in_t[...])
        dx_ref[rows] = (
            dy.astype(F32) + norm_back(dnorm, x_value[rows], x_rate[rows, :1])
        ).astype(BF16)

        @pl.when(section > 0)
        def _():
            dy_hop(user).start()

        return carry

    lax.fori_loop(0, USERS, backward_user, 0)

    def finish(user, carry):
        @pl.when(section < 3)
        def _():
            x_hop(user).wait_send()

        @pl.when(section > 0)
        def _():
            dy_hop(user).wait_send()

        return carry

    lax.fori_loop(0, USERS, finish, 0)


def window(where, live, x, cot, w_in, w_out, fetched):
    heads = USERS * HEADS
    return pl.pallas_call(
        window_kernel,
        out_shape=[
            jax.ShapeDtypeStruct((ROWS, D), BF16),
            jax.ShapeDtypeStruct((ROWS, D), BF16),
            jax.ShapeDtypeStruct((ROWS, D), BF16),
            jax.ShapeDtypeStruct((ROWS, 4 * HA), BF16),
            jax.ShapeDtypeStruct((ROWS, D), BF16),
            jax.ShapeDtypeStruct((ROWS, HA), BF16),
        ],
        in_specs=[SM, SM, VM, VM, VM, VM, ANY],
        out_specs=[VM] * 6,
        scratch_shapes=[
            pltpu.VMEM(fetched.shape, BF16),
            pltpu.VMEM((USERS * HBLK, EVT, 2 * HA), BF16),
            pltpu.VMEM((4 * HA, D), BF16),
            pltpu.VMEM((ROWS, D), BF16),
            pltpu.VMEM((ROWS, D), F32),
            pltpu.VMEM((ROWS, 128), F32),
            pltpu.VMEM((ROWS, 4 * HA), BF16),
            pltpu.VMEM((ROWS, 4 * HA), F32),
            pltpu.VMEM((heads, EVT, KEYS + EVT), BF16),
            pltpu.VMEM((heads, EVT, EVT), BF16),
            pltpu.VMEM((ROWS, HA), F32),
            pltpu.VMEM((ROWS, HA), F32),
            pltpu.VMEM((ROWS, 128), F32),
            pltpu.VMEM((ROWS, HA), BF16),
            pltpu.VMEM((ROWS, D), BF16),
            pltpu.VMEM((ROWS, D), BF16),
            pltpu.SemaphoreType.DMA,
            pltpu.SemaphoreType.DMA((USERS,)),
            pltpu.SemaphoreType.DMA((USERS,)),
            pltpu.SemaphoreType.DMA((USERS,)),
            pltpu.SemaphoreType.DMA((USERS,)),
        ],
        compiler_params=pltpu.CompilerParams(
            collective_id=2, has_side_effects=True, vmem_limit_bytes=56 << 20
        ),
        name="window",
    )(where, live, x, cot, w_in, w_out, fetched)


PARTS = 4
WIDE = (4 * HA + HA) // PARTS
LAST = 4 * HA - (PARTS - 1) * WIDE
CHUNK = D // OWNERS


def scatter_kernel(
    x_norm_hbm, dproj_hbm, dy_hbm, gated_hbm, in_ref, out_ref,
    x_norm_ref, dproj_ref, dy_ref, gated_ref, load_sem, x_turned, dy_turned, part, pair, mine, first, middle, second, pair_sem, first_sem, second_sem,
):
    y, z, c = place()
    steps = (1, 3, 2)
    loads = [
        pltpu.make_async_copy(src, dst, load_sem.at[i])
        for i, (src, dst) in enumerate(
            [(x_norm_hbm, x_norm_ref), (dproj_hbm, dproj_ref), (dy_hbm, dy_ref), (gated_hbm, gated_ref)]
        )
    ]
    for load in loads:
        load.start()
    greet_all([(0, 0, 1)] + [(s, 0, 0) for s in steps] + [(0, s, 0) for s in steps])

    def copy(src, dst, sems, offset):
        made = to_peer(src, dst, sems.at[0], sems.at[1], chip_at(offset))
        made.start()
        return made

    for load in loads:
        load.wait()
    x_turned[...] = x_norm_ref[...].T

    def multiply(q):
        def one(i, carry):
            rows = pl.ds(pl.multiple_of(i * 256, 256), 256)

            def keep(left, right, start):
                made = dot(left[rows], right).astype(BF16)
                width = made.shape[1]
                part[q, i, :, :, :, start : start + width] = made.reshape(4, 2, CHUNK, width)

            if q < PARTS - 1:
                keep(x_turned, dproj_ref[:, q * WIDE : (q + 1) * WIDE], 0)
            else:
                keep(x_turned, dproj_ref[:, q * WIDE :], 0)
                keep(dy_turned, gated_ref[...], LAST)
            return carry

        lax.fori_loop(0, 4, one, 0)
        return copy(part.at[q, :, :, 1 - c], pair.at[q], pair_sem.at[q], (0, 0, 1))

    def move(q, swap):
        swap.wait()

        def join(i, carry):
            mine[q, i] = (part[q, i, :, c].astype(F32) + pair[q, i].astype(F32)).astype(BF16)
            return carry

        lax.fori_loop(0, 4, join, 0)
        moves = []
        for k, s in enumerate(steps):
            along_z = q % 2
            at = lax.rem((z if along_z else y) + s, 4)
            src = mine.at[q, :, at] if along_z else mine.at[q, at]
            moves.append(copy(src, first.at[q, k], first_sem.at[q, k], (0, s, 0) if along_z else (s, 0, 0)))
        return moves

    swaps, moves, later = [], [], []
    for q in range(PARTS):
        if q == PARTS - 1:
            dy_turned[...] = dy_ref[...].T
        swaps.append(multiply(q))
        if q:
            moves.append(move(q - 1, swaps[q - 1]))
    moves.append(move(PARTS - 1, swaps[PARTS - 1]))
    for q in range(PARTS):
        for made in moves[q]:
            made.wait()
        along_z = q % 2

        def add(i, carry, q=q, along_z=along_z):
            total = (mine[q, i, z] if along_z else mine[q, y, i]).astype(F32)
            for k in range(3):
                total += first[q, k, i].astype(F32)
            middle[q, i] = total.astype(BF16)
            return carry

        lax.fori_loop(0, 4, add, 0)
        sent = []
        for k, s in enumerate(steps):
            at = lax.rem((y if along_z else z) + s, 4)
            sent.append(
                copy(middle.at[q, at], second.at[q, k], second_sem.at[q, k], (s, 0, 0) if along_z else (0, s, 0))
            )
        later.append(sent)
    for q in range(PARTS):
        for made in later[q]:
            made.wait()
        total = middle[q, y if q % 2 else z].astype(F32)
        for k in range(3):
            total += second[q, k].astype(F32)
        if q < PARTS - 1:
            in_ref[:, q * WIDE : (q + 1) * WIDE] = total
        else:
            in_ref[:, q * WIDE :] = total[:, :LAST]
            out_ref[...] = total[:, LAST:]


def summed(x_norm, dproj, dy, gated):
    return pl.pallas_call(
        scatter_kernel,
        out_shape=[
            jax.ShapeDtypeStruct((CHUNK, 4 * HA), F32),
            jax.ShapeDtypeStruct((CHUNK, HA), F32),
        ],
        in_specs=[ANY] * 4,
        out_specs=[VM, VM],
        scratch_shapes=[
            pltpu.VMEM((ROWS, D), BF16),
            pltpu.VMEM((ROWS, 4 * HA), BF16),
            pltpu.VMEM((ROWS, D), BF16),
            pltpu.VMEM((ROWS, HA), BF16),
            pltpu.SemaphoreType.DMA((4,)),
            pltpu.VMEM((D, ROWS), BF16),
            pltpu.VMEM((D, ROWS), BF16),
            pltpu.VMEM((PARTS, 4, 4, 2, CHUNK, WIDE), BF16),
            pltpu.VMEM((PARTS, 4, 4, CHUNK, WIDE), BF16),
            pltpu.VMEM((PARTS, 4, 4, CHUNK, WIDE), BF16),
            pltpu.VMEM((PARTS, 3, 4, CHUNK, WIDE), BF16),
            pltpu.VMEM((PARTS, 4, CHUNK, WIDE), BF16),
            pltpu.VMEM((PARTS, 3, CHUNK, WIDE), BF16),
            pltpu.SemaphoreType.DMA((PARTS, 2)),
            pltpu.SemaphoreType.DMA((PARTS, 3, 2)),
            pltpu.SemaphoreType.DMA((PARTS, 3, 2)),
        ],
        compiler_params=pltpu.CompilerParams(
            collective_id=1, has_side_effects=True, vmem_limit_bytes=60 << 20
        ),
        name="scatter",
    )(x_norm, dproj, dy, gated)


def body(
    embeddings, in_proj, out_proj, hist_cache, hist_len, block_mask, block_owner, block_slot, cotangent
):
    w_in, w_out = in_proj[0], out_proj[0]
    requests = USERS * HBLK
    start = jnp.arange(HBLK, dtype=jnp.int32)[None, :] * EVT
    live = jnp.where(block_mask > 0, jnp.clip(hist_len[:, None] - start, 0, EVT), 0).reshape(requests)
    wanted = live > 0
    owner = jnp.where(wanted, block_owner.reshape(requests), -2)
    order = jnp.arange(requests, dtype=jnp.int32)
    earlier = (owner[:, None] == owner[None, :]) & (order[None, :] < order[:, None])
    rank = jnp.sum(earlier.astype(jnp.int32), axis=1)
    beside = jnp.sum(((owner ^ 1)[:, None] == owner[None, :]).astype(jnp.int32), axis=1)
    me = lax.axis_index("dp")
    chip, core, side = owner // 2, owner % 2, me % 2
    slot = jnp.where(rank == 0, jnp.where(core == side, 1, 0), jnp.where((core == 1) & (beside == 2), 3, 2))
    where = jnp.where(wanted, chip * SLOTS + slot, me // 2 * SLOTS)
    names = jnp.arange(128, dtype=jnp.int32)
    number = core * HBLK + block_slot.reshape(requests)
    late = wanted & (slot == 3) & (chip != me // 2)
    here = (where[:, None] == names[None, :]) & wanted[:, None]
    table = jnp.sum(
        jnp.where(here, number[:, None], 0)
        + jnp.where(late[:, None] & (names[None, :] == 127), 1, 0),
        axis=0,
    )
    cache = hist_cache[0]
    got, asked = exchange(table.reshape(1, 128), cache)
    got = lax.cond(
        jnp.max(asked[:, 0, 127]) > 0, lambda g: fourth(asked, cache, g), lambda g: g, got
    )
    fetched = got.reshape(OWNERS // 2 * SLOTS, EVT, 2 * HA)
    y, dx, x_norm, dproj, dy, gated = window(
        where, live, embeddings, cotangent, w_in, w_out, fetched
    )
    grad_in, grad_out = summed(x_norm, dproj, dy, gated)
    return (y[None], dx[None], grad_in[None], grad_out[None])


def solution(mesh):
    placed = (
        P("dp", None),
        P("section", None, None),
        P("section", None, None),
        P("section", "dp", None, None),
        P("dp"),
        P("dp", None),
        P("dp", None, None),
        P("dp", None),
        P("dp", None),
    )
    return jax.shard_map(
        body,
        mesh=mesh,
        in_specs=placed,
        out_specs=(
            P("section", "dp", None),
            P("section", "dp", None),
            P("section", "dp", None),
            P("section", "dp", None),
        ),
        check_vma=False,
    )
```

```python
from functools import partial
import math

import jax
import jax.numpy as jnp
from jax import lax
from jax.experimental import pallas as pl
from jax.experimental.pallas import tpu as pltpu
from jax.sharding import PartitionSpec as P

HEADS = 4
EVT = 128
HBLK = 16
USERS = 2
ROWS = USERS * EVT
D = 1024
HA = 512
HD = HA // HEADS
GROUP = 8
KEYS = HBLK * EVT
OWNERS = 32
epsilon = 1e-06
SCALE = 1.0 / math.sqrt(HD)
MESH = pl.DeviceIdType.MESH
F32 = jnp.float32
BF16 = jnp.bfloat16
VM = pl.BlockSpec(memory_space=pltpu.VMEM)
SM = pl.BlockSpec(memory_space=pltpu.SMEM)
ANY = pl.BlockSpec(memory_space=pl.ANY)


def dot(a, b, ca=1, cb=0):
    return lax.dot_general(a, b, (((ca,), (cb,)), ((), ())), preferred_element_type=F32)


def normed(values):
    centred = values - jnp.mean(values, axis=-1, keepdims=True)
    inverse = lax.rsqrt(jnp.mean(centred * centred, axis=-1, keepdims=True) + epsilon)
    return centred * inverse, inverse


def norm_back(grad, value, inverse):
    return inverse * (
        grad
        - jnp.mean(grad, axis=-1, keepdims=True)
        - value * jnp.mean(grad * value, axis=-1, keepdims=True)
    )


def silu_parts(half):
    t = jnp.tanh(half)
    return half + half * t, 0.5 * ((1.0 + t) + half * (1.0 - t * t))


def place():
    me = lax.axis_index("dp")
    return me // 8, lax.rem(me // 2, 4), lax.rem(me, 2)


def chip_at(offset):
    y, z, c = place()
    return lax.rem(y + offset[0], 4) * 8 + lax.rem(z + offset[1], 4) * 2 + lax.rem(c + offset[2], 2)


ORDER = (
    [(1, 0), (3, 0), (2, 0), (1, 1), (3, 3), (2, 1), (2, 3), (1, 3), (3, 1), (2, 2), (1, 2), (3, 2), (0, 1), (0, 3), (0, 2)],
    [(0, 1), (0, 3), (0, 2), (1, 2), (3, 2), (1, 1), (3, 3), (2, 2), (1, 3), (3, 1), (2, 1), (2, 3), (1, 0), (3, 0), (2, 0)],
)
PEERS = [(a, b, c) for a in range(4) for b in range(4) for c in range(2)][1:]
SLOTS = 4
BLOCK = (EVT, 2 * HA)


def name_of(y, z, c):
    return y * 8 + z * 2 + c


def reverse_name(y, z, c):
    return lax.rem(4 - y, 4) * 8 + lax.rem(4 - z, 4) * 2 + c


def to_peer(src, dst, send_sem, recv_sem, peer):
    return pltpu.make_async_remote_copy(
        src_ref=src,
        dst_ref=dst,
        send_sem=send_sem,
        recv_sem=recv_sem,
        device_id={"dp": peer},
        device_id_type=MESH,
    )


def greet_all(peers):
    barrier = pltpu.get_barrier_semaphore()
    for peer in peers:
        pl.semaphore_signal(barrier, inc=1, device_id={"dp": chip_at(peer)}, device_id_type=MESH)
    pl.semaphore_wait(barrier, len(peers))


def both_caches(cache_ref, cache, swap_sem, local_sem):
    core = lax.rem(lax.axis_index("dp"), 2)
    mine = cache.at[pl.ds(core * HBLK, HBLK)]
    swap = to_peer(cache_ref, mine, swap_sem.at[0], swap_sem.at[1], chip_at((0, 0, 1)))
    own = pltpu.make_async_copy(cache_ref, mine, local_sem)
    swap.start()
    own.start()
    return swap, own


def ordered(i, core):
    (y0, z0), (y1, z1) = ORDER[0][i], ORDER[1][i]
    return y0 + core * (y1 - y0), z0 + core * (z1 - z0)


def exchange_kernel(
    table_ref, cache_ref, out_ref, asked_ref, cache, asked_s, outgoing, own_blocks,
    swap_sem, ask_send, ask_recv, one_send, one_recv, two_send, two_recv, local_sem,
):
    y, z, core = place()
    chip = y * 4 + z
    greet_all(PEERS)
    swap, own = both_caches(cache_ref, cache, swap_sem, local_sem.at[0])
    asks = []
    for peer in PEERS:
        name = name_of(*peer)
        asks.append(
            to_peer(table_ref, asked_ref.at[name], ask_send.at[name], ask_recv.at[name], chip_at(peer))
        )
        asks[-1].start()
    row = pltpu.make_async_copy(table_ref, asked_ref.at[0], local_sem.at[1])
    row.start()
    row.wait()
    for ask in asks:
        ask.wait()
    down = pltpu.make_async_copy(asked_ref, asked_s, local_sem.at[2])
    down.start()
    down.wait()
    swap.wait()
    own.wait()

    sends = []
    for i in range(15):
        dy, dz = ordered(i, core)
        name = dy * 4 + dz
        for dc in range(2):
            row = reverse_name(dy, dz, dc)
            if dc == 0:
                outgoing[i, 1] = cache[asked_s[row, 0, chip * SLOTS + 1]]
                outgoing[i, 2] = cache[asked_s[row, 0, chip * SLOTS + 2]]
                src, dst = outgoing.at[i, pl.ds(1, 2)], out_ref.at[chip, pl.ds(1, 2)]
                sems = two_send.at[name], two_recv.at[name]
            else:
                outgoing[i, 0] = cache[asked_s[row, 0, chip * SLOTS]]
                src, dst = outgoing.at[i, 0], out_ref.at[chip, 0]
                sems = one_send.at[name], one_recv.at[name]
            sends.append(to_peer(src, dst, *sems, chip_at((dy, dz, dc))))
            sends[-1].start()
    for k in range(SLOTS):
        own_blocks[k] = cache[asked_s[0, 0, chip * SLOTS + k]]
    kept = pltpu.make_async_copy(own_blocks, out_ref.at[chip], local_sem.at[3])
    kept.start()
    for send in sends:
        send.wait()
    kept.wait()


def exchange(table, cache):
    return pl.pallas_call(
        exchange_kernel,
        out_shape=[
            jax.ShapeDtypeStruct((OWNERS // 2, SLOTS) + BLOCK, BF16),
            jax.ShapeDtypeStruct((OWNERS, 1, 128), jnp.int32),
        ],
        in_specs=[VM, ANY],
        out_specs=[ANY, VM],
        scratch_shapes=[
            pltpu.VMEM((2 * HBLK,) + BLOCK, BF16),
            pltpu.SMEM((OWNERS, 1, 128), jnp.int32),
            pltpu.VMEM((15, 3) + BLOCK, BF16),
            pltpu.VMEM((SLOTS,) + BLOCK, BF16),
            pltpu.SemaphoreType.DMA((2,)),
            pltpu.SemaphoreType.DMA((OWNERS,)),
            pltpu.SemaphoreType.DMA((OWNERS,)),
            pltpu.SemaphoreType.DMA((16,)),
            pltpu.SemaphoreType.DMA((16,)),
            pltpu.SemaphoreType.DMA((16,)),
            pltpu.SemaphoreType.DMA((16,)),
            pltpu.SemaphoreType.DMA((4,)),
        ],
        compiler_params=pltpu.CompilerParams(
            collective_id=0, has_side_effects=True, vmem_limit_bytes=40 << 20
        ),
        name="exchange",
    )(table, cache)


def fourth_kernel(
    asked_ref, cache_ref, got_ref, out_ref, cache, outgoing, swap_sem, send_sem, recv_sem, local_sem
):
    del got_ref
    y, z, core = place()
    chip = y * 4 + z
    peers = [(a, b, 0) for a, b in ORDER[0]]
    greet_all(peers + [(0, 0, 1)])
    swap, own = both_caches(cache_ref, cache, swap_sem, local_sem)
    swap.wait()
    own.wait()
    sends = []
    for i, (dy, dz, _) in enumerate(peers):
        outgoing[i] = cache[asked_ref[reverse_name(dy, dz, 0), 0, chip * SLOTS + 3]]
        sends.append(
            to_peer(
                outgoing.at[i], out_ref.at[chip, 3], send_sem.at[i], recv_sem.at[i], chip_at((dy, dz, 0))
            )
        )
        sends[-1].start()
    for send in sends:
        send.wait()


def fourth(asked, cache, got):
    return pl.pallas_call(
        fourth_kernel,
        out_shape=jax.ShapeDtypeStruct(got.shape, BF16),
        in_specs=[SM, ANY, ANY],
        out_specs=ANY,
        scratch_shapes=[
            pltpu.VMEM((2 * HBLK,) + BLOCK, BF16),
            pltpu.VMEM((15,) + BLOCK, BF16),
            pltpu.SemaphoreType.DMA((2,)),
            pltpu.SemaphoreType.DMA((15,)),
            pltpu.SemaphoreType.DMA((15,)),
            pltpu.SemaphoreType.DMA,
        ],
        input_output_aliases={2: 0},
        compiler_params=pltpu.CompilerParams(
            collective_id=3, has_side_effects=True, vmem_limit_bytes=24 << 20
        ),
        name="fourth",
    )(asked, cache, got)


def columns(start):
    return pl.ds(pl.multiple_of(start, HD), HD)


def window_kernel(
    where_ref, live_ref, x_ref, cot_ref, w_in_ref, w_out_ref, fetched_ref,
    made_ref, x_norm_ref, dproj_ref, dy_ref, gated_ref,
    fetched, hist, w_in_t, x_now, x_value, x_rate, act, slope_in, slope, own_weights, mixed, value_ref, rate_ref, dmixed,
    x_arrived, dy_arrived, hist_sem, x_send, x_recv, dy_send, dy_recv,
):
    y_ref, dx_ref = made_ref.at[0], made_ref.at[1]
    section = lax.axis_index("section")
    dp = lax.axis_index("dp")
    after, before = lax.rem(section + 1, 4), lax.rem(section + 3, 4)
    barrier = pltpu.get_barrier_semaphore()
    for peer in (before, after):
        pl.semaphore_signal(barrier, inc=1, device_id=(peer, dp), device_id_type=MESH)

    load = pltpu.make_async_copy(fetched_ref, fetched, hist_sem)
    load.start()
    pl.semaphore_wait(barrier, 2)

    def user_rows(user):
        return pl.ds(pl.multiple_of(user * EVT, EVT), EVT)

    def hop(src, dst, user, sends, recvs, peer):
        rows = user_rows(user)
        return pltpu.make_async_remote_copy(
            src_ref=src.at[rows],
            dst_ref=dst.at[rows],
            send_sem=sends.at[user],
            recv_sem=recvs.at[user],
            device_id=(peer, dp),
            device_id_type=MESH,
        )

    def x_hop(user):
        return hop(y_ref, x_arrived, user, x_send, x_recv, after)

    def dy_hop(user):
        return hop(dx_ref, dy_arrived, user, dy_send, dy_recv, before)

    row_of_block = lax.broadcasted_iota(jnp.int32, (EVT, HA), 0)
    causal = lax.broadcasted_iota(jnp.int32, (EVT, EVT), 1) <= lax.broadcasted_iota(
        jnp.int32, (EVT, EVT), 0
    )

    def inverse_count(user):
        total = live_ref[user * HBLK]
        for j in range(1, HBLK):
            total = total + live_ref[user * HBLK + j]
        return 1.0 / (jnp.full((EVT, 1), total, jnp.int32).astype(F32) + float(EVT))

    def history(user, group, start):
        blocks = pl.ds(user * HBLK + group * GROUP, GROUP)
        return hist[blocks, :, columns(start)].reshape(GROUP * EVT, HD)

    def settle(r, carry):
        block = fetched[where_ref[r]]
        keep = (row_of_block < live_ref[r]).astype(F32).astype(BF16)
        hist[r, :, :HA] = block[:, :HA]
        hist[r, :, HA:] = block[:, HA:] * keep
        return carry

    def turn_w_in():
        for k in range(0, 4 * HA, HD):
            w_in_t[k : k + HD] = w_in_ref[:, k : k + HD].T

    @pl.when(section > 0)
    def _():
        turn_w_in()
        load.wait()
        lax.fori_loop(0, USERS * HBLK, settle, 0)

    def forward_user(user, carry):
        rows = user_rows(user)

        @pl.when(section == 0)
        def _():
            x_now[rows] = x_ref[rows]

        @pl.when(section > 0)
        def _():
            x_hop(user).wait_recv()
            x_now[rows] = x_arrived[rows]

        x = x_now[rows].astype(F32)
        normal, rate = normed(x)
        x_value[rows] = normal
        x_rate[rows] = jnp.broadcast_to(rate, (EVT, 128))
        x_norm = normal.astype(BF16)
        x_norm_ref[rows] = x_norm
        for c in range(4):
            part = slice(c * HA, (c + 1) * HA)
            made, rise = silu_parts(dot(x_norm, w_in_ref[:, part]) * 0.5)
            act[rows, part] = made.astype(BF16)
            slope_in[rows, part] = rise
        inverse = inverse_count(user)

        @pl.when((section == 0) & (user == 0))
        def _():
            load.wait()

        @pl.when(section == 0)
        def _():
            lax.fori_loop(user * HBLK, (user + 1) * HBLK, settle, 0)

        def head_forward(head, carry):
            query = act[rows, columns(2 * HA + head * HD)]
            total = jnp.zeros((EVT, HD), F32)
            for group in range(HBLK // GROUP):
                half = dot(query, history(user, group, head * HD), 1, 1) * (0.5 * SCALE)
                weights, rise = silu_parts(half)
                at = slice(group * GROUP * EVT, (group + 1) * GROUP * EVT)
                slope[user * HEADS + head, :, at] = (rise * SCALE).astype(BF16)
                total += dot(weights.astype(BF16), history(user, group, HA + head * HD))
            half = dot(query, act[rows, columns(3 * HA + head * HD)], 1, 1) * (0.5 * SCALE)
            weights, rise = silu_parts(half)
            weights = jnp.where(causal, weights, 0.0).astype(BF16)
            total += dot(weights, act[rows, columns(HA + head * HD)])
            slope[user * HEADS + head, :, KEYS:] = jnp.where(causal, rise * SCALE, 0.0).astype(BF16)
            own_weights[user * HEADS + head] = weights
            mixed[rows, columns(head * HD)] = total * inverse
            return carry

        lax.fori_loop(0, HEADS, head_forward, 0, unroll=True)
        value, rate = normed(mixed[rows])
        gated = (value * act[rows, :HA].astype(F32)).astype(BF16)
        value_ref[rows] = value
        gated_ref[rows] = gated
        rate_ref[rows] = jnp.broadcast_to(rate, (EVT, 128))
        y_ref[rows] = (x + dot(gated, w_out_ref[...], 1, 1)).astype(BF16)

        @pl.when(section < 3)
        def _():
            x_hop(user).start()

        return carry


    def backward_user(user, carry):
        rows = user_rows(user)

        @pl.when(section == 3)
        def _():
            dy_ref[rows] = cot_ref[rows]

        @pl.when(section < 3)
        def _():
            dy_hop(user).wait_recv()
            dy_ref[rows] = dy_arrived[rows]

        dy = dy_ref[rows]
        dgated = dot(dy, w_out_ref[...])
        value = value_ref[rows]
        dproj_ref[rows, :HA] = (dgated * value * slope_in[rows, :HA]).astype(BF16)
        grad = norm_back(dgated * act[rows, :HA].astype(F32), value, rate_ref[rows, :1])
        dmixed[rows] = (grad * inverse_count(user)).astype(BF16)

        def head_back(head, carry):
            index = user * HEADS + head
            grad_mixed = dmixed[rows, columns(head * HD)]
            total = jnp.zeros((EVT, HD), F32)
            for group in range(HBLK // GROUP):
                rise = slope[index, :, group * GROUP * EVT : (group + 1) * GROUP * EVT].astype(F32)
                ds = (dot(grad_mixed, history(user, group, HA + head * HD), 1, 1) * rise).astype(BF16)
                total += dot(ds, history(user, group, head * HD))
            query = act[rows, columns(2 * HA + head * HD)]
            keys = act[rows, columns(3 * HA + head * HD)]
            values = act[rows, columns(HA + head * HD)]
            ds = (dot(grad_mixed, values, 1, 1) * slope[index, :, KEYS:].astype(F32)).astype(BF16)
            total += dot(ds, keys)
            dvalue = dot(own_weights[index], grad_mixed, 0, 0)
            dkey = dot(ds, query, 0, 0)
            for base, part in ((HA, dvalue), (2 * HA, total), (3 * HA, dkey)):
                at = columns(base + head * HD)
                dproj_ref[rows, at] = (part * slope_in[rows, at]).astype(BF16)
            return carry

        lax.fori_loop(0, HEADS, head_back, 0, unroll=True)
        dnorm = dot(dproj_ref[rows], w_in_t[...])
        dx_ref[rows] = (
            dy.astype(F32) + norm_back(dnorm, x_value[rows], x_rate[rows, :1])
        ).astype(BF16)

        @pl.when(section > 0)
        def _():
            dy_hop(user).start()

        return carry

    def one_pass(i, carry):
        last = section == 3
        user = jnp.where(last, i // 2, lax.rem(i, 2))
        back = jnp.where(last, lax.rem(i, 2), i // 2)

        @pl.when(back == 0)
        def _():
            forward_user(user, 0)

        @pl.when((section == 0) & (i == USERS))
        def _():
            turn_w_in()

        @pl.when(back == 1)
        def _():
            backward_user(user, 0)

        return carry

    lax.fori_loop(0, 2 * USERS, one_pass, 0)

    def finish(user, carry):
        @pl.when(section < 3)
        def _():
            x_hop(user).wait_send()

        @pl.when(section > 0)
        def _():
            dy_hop(user).wait_send()

        return carry

    lax.fori_loop(0, USERS, finish, 0)


def window(where, live, x, cot, w_in, w_out, fetched):
    heads = USERS * HEADS
    return pl.pallas_call(
        window_kernel,
        out_shape=[
            jax.ShapeDtypeStruct((2, ROWS, D), BF16),
            jax.ShapeDtypeStruct((ROWS, D), BF16),
            jax.ShapeDtypeStruct((ROWS, 4 * HA), BF16),
            jax.ShapeDtypeStruct((ROWS, D), BF16),
            jax.ShapeDtypeStruct((ROWS, HA), BF16),
        ],
        in_specs=[SM, SM, VM, VM, VM, VM, ANY],
        out_specs=[VM] * 5,
        scratch_shapes=[
            pltpu.VMEM(fetched.shape, BF16),
            pltpu.VMEM((USERS * HBLK, EVT, 2 * HA), BF16),
            pltpu.VMEM((4 * HA, D), BF16),
            pltpu.VMEM((ROWS, D), BF16),
            pltpu.VMEM((ROWS, D), F32),
            pltpu.VMEM((ROWS, 128), F32),
            pltpu.VMEM((ROWS, 4 * HA), BF16),
            pltpu.VMEM((ROWS, 4 * HA), F32),
            pltpu.VMEM((heads, EVT, KEYS + EVT), BF16),
            pltpu.VMEM((heads, EVT, EVT), BF16),
            pltpu.VMEM((ROWS, HA), F32),
            pltpu.VMEM((ROWS, HA), F32),
            pltpu.VMEM((ROWS, 128), F32),
            pltpu.VMEM((ROWS, HA), BF16),
            pltpu.VMEM((ROWS, D), BF16),
            pltpu.VMEM((ROWS, D), BF16),
            pltpu.SemaphoreType.DMA,
            pltpu.SemaphoreType.DMA((USERS,)),
            pltpu.SemaphoreType.DMA((USERS,)),
            pltpu.SemaphoreType.DMA((USERS,)),
            pltpu.SemaphoreType.DMA((USERS,)),
        ],
        compiler_params=pltpu.CompilerParams(
            collective_id=2, has_side_effects=True, vmem_limit_bytes=56 << 20
        ),
        name="window",
    )(where, live, x, cot, w_in, w_out, fetched)


PARTS = 4
WIDE = (4 * HA + HA) // PARTS
LAST = 4 * HA - (PARTS - 1) * WIDE
CHUNK = D // OWNERS


def scatter_kernel(
    x_norm_hbm, dproj_hbm, dy_hbm, gated_hbm, sum_ref,
    x_norm_ref, dproj_ref, dy_ref, gated_ref, load_sem, x_turned, dy_turned, part, pair, mine, first, middle, second, pair_sem, first_sem, second_sem,
):
    y, z, c = place()
    steps = (1, 3, 2)
    loads = [
        pltpu.make_async_copy(src, dst, load_sem.at[i])
        for i, (src, dst) in enumerate(
            [(x_norm_hbm, x_norm_ref), (dproj_hbm, dproj_ref), (dy_hbm, dy_ref), (gated_hbm, gated_ref)]
        )
    ]
    for load in loads:
        load.start()
    greet_all([(0, 0, 1)] + [(s, 0, 0) for s in steps] + [(0, s, 0) for s in steps])

    def copy(src, dst, sems, offset):
        made = to_peer(src, dst, sems.at[0], sems.at[1], chip_at(offset))
        made.start()
        return made

    for load in loads:
        load.wait()
    x_turned[...] = x_norm_ref[...].T

    def multiply(q):
        def one(i, carry):
            rows = pl.ds(pl.multiple_of(i * 256, 256), 256)

            def keep(left, right, start):
                made = dot(left[rows], right).astype(BF16)
                width = made.shape[1]
                part[q, i, :, :, :, start : start + width] = made.reshape(4, 2, CHUNK, width)

            if q < PARTS - 1:
                keep(x_turned, dproj_ref[:, q * WIDE : (q + 1) * WIDE], 0)
            else:
                keep(x_turned, dproj_ref[:, q * WIDE :], 0)
                keep(dy_turned, gated_ref[...], LAST)
            return carry

        lax.fori_loop(0, 4, one, 0)
        return copy(part.at[q, :, :, 1 - c], pair.at[q], pair_sem.at[q], (0, 0, 1))

    def move(q, swap):
        swap.wait()

        def join(i, carry):
            mine[q, i] = (part[q, i, :, c].astype(F32) + pair[q, i].astype(F32)).astype(BF16)
            return carry

        lax.fori_loop(0, 4, join, 0)
        moves = []
        for k, s in enumerate(steps):
            along_z = q % 2
            at = lax.rem((z if along_z else y) + s, 4)
            src = mine.at[q, :, at] if along_z else mine.at[q, at]
            moves.append(copy(src, first.at[q, k], first_sem.at[q, k], (0, s, 0) if along_z else (s, 0, 0)))
        return moves

    swaps, moves, later = [], [], []
    for q in range(PARTS):
        if q == PARTS - 1:
            dy_turned[...] = dy_ref[...].T
        swaps.append(multiply(q))
        if q:
            moves.append(move(q - 1, swaps[q - 1]))
    moves.append(move(PARTS - 1, swaps[PARTS - 1]))
    for q in range(PARTS):
        for made in moves[q]:
            made.wait()
        along_z = q % 2

        def add(i, carry, q=q, along_z=along_z):
            total = (mine[q, i, z] if along_z else mine[q, y, i]).astype(F32)
            for k in range(3):
                total += first[q, k, i].astype(F32)
            middle[q, i] = total.astype(BF16)
            return carry

        lax.fori_loop(0, 4, add, 0)
        sent = []
        for k, s in enumerate(steps):
            at = lax.rem((y if along_z else z) + s, 4)
            sent.append(
                copy(middle.at[q, at], second.at[q, k], second_sem.at[q, k], (s, 0, 0) if along_z else (0, s, 0))
            )
        later.append(sent)
    for q in range(PARTS):
        for made in later[q]:
            made.wait()
        total = middle[q, y if q % 2 else z].astype(F32)
        for k in range(3):
            total += second[q, k].astype(F32)
        sum_ref[:, q * WIDE : (q + 1) * WIDE] = total


def summed(x_norm, dproj, dy, gated):
    return pl.pallas_call(
        scatter_kernel,
        out_shape=jax.ShapeDtypeStruct((CHUNK, 5 * HA), F32),
        in_specs=[ANY] * 4,
        out_specs=VM,
        scratch_shapes=[
            pltpu.VMEM((ROWS, D), BF16),
            pltpu.VMEM((ROWS, 4 * HA), BF16),
            pltpu.VMEM((ROWS, D), BF16),
            pltpu.VMEM((ROWS, HA), BF16),
            pltpu.SemaphoreType.DMA((4,)),
            pltpu.VMEM((D, ROWS), BF16),
            pltpu.VMEM((D, ROWS), BF16),
            pltpu.VMEM((PARTS, 4, 4, 2, CHUNK, WIDE), BF16),
            pltpu.VMEM((PARTS, 4, 4, CHUNK, WIDE), BF16),
            pltpu.VMEM((PARTS, 4, 4, CHUNK, WIDE), BF16),
            pltpu.VMEM((PARTS, 3, 4, CHUNK, WIDE), BF16),
            pltpu.VMEM((PARTS, 4, CHUNK, WIDE), BF16),
            pltpu.VMEM((PARTS, 3, CHUNK, WIDE), BF16),
            pltpu.SemaphoreType.DMA((PARTS, 2)),
            pltpu.SemaphoreType.DMA((PARTS, 3, 2)),
            pltpu.SemaphoreType.DMA((PARTS, 3, 2)),
        ],
        compiler_params=pltpu.CompilerParams(
            collective_id=1, has_side_effects=True, vmem_limit_bytes=60 << 20
        ),
        name="scatter",
    )(x_norm, dproj, dy, gated)


def body(
    embeddings, in_proj, out_proj, hist_cache, hist_len, block_mask, block_owner, block_slot, cotangent
):
    w_in, w_out = in_proj[0], out_proj[0]
    requests = USERS * HBLK
    start = jnp.arange(HBLK, dtype=jnp.int32)[None, :] * EVT
    live = jnp.where(block_mask > 0, jnp.clip(hist_len[:, None] - start, 0, EVT), 0).reshape(requests)
    wanted = live > 0
    owner = jnp.where(wanted, block_owner.reshape(requests), -2)
    order = jnp.arange(requests, dtype=jnp.int32)
    earlier = (owner[:, None] == owner[None, :]) & (order[None, :] < order[:, None])
    rank = jnp.sum(earlier.astype(jnp.int32), axis=1)
    beside = jnp.sum(((owner ^ 1)[:, None] == owner[None, :]).astype(jnp.int32), axis=1)
    me = lax.axis_index("dp")
    chip, core, side = owner // 2, owner % 2, me % 2
    slot = jnp.where(rank == 0, jnp.where(core == side, 1, 0), jnp.where((core == 1) & (beside == 2), 3, 2))
    where = jnp.where(wanted, chip * SLOTS + slot, me // 2 * SLOTS)
    names = jnp.arange(128, dtype=jnp.int32)
    number = core * HBLK + block_slot.reshape(requests)
    late = wanted & (slot == 3) & (chip != me // 2)
    here = (where[:, None] == names[None, :]) & wanted[:, None]
    table = jnp.sum(
        jnp.where(here, number[:, None], 0)
        + jnp.where(late[:, None] & (names[None, :] == 127), 1, 0),
        axis=0,
    )
    cache = hist_cache[0]
    got, asked = exchange(table.reshape(1, 128), cache)
    got = lax.cond(
        jnp.max(asked[:, 0, 127]) > 0, lambda g: fourth(asked, cache, g), lambda g: g, got
    )
    fetched = got.reshape(OWNERS // 2 * SLOTS, EVT, 2 * HA)
    made, x_norm, dproj, dy, gated = window(
        where, live, embeddings, cotangent, w_in, w_out, fetched
    )
    grads = summed(x_norm, dproj, dy, gated)[None]
    return (made[:1], made[1:], grads[:, :, : 4 * HA], grads[:, :, 4 * HA :])


def solution(mesh):
    placed = (
        P("dp", None),
        P("section", None, None),
        P("section", None, None),
        P("section", "dp", None, None),
        P("dp"),
        P("dp", None),
        P("dp", None, None),
        P("dp", None),
        P("dp", None),
    )
    return jax.shard_map(
        body,
        mesh=mesh,
        in_specs=placed,
        out_specs=(
            P("section", "dp", None),
            P("section", "dp", None),
            P("section", "dp", None),
            P("section", "dp", None),
        ),
        check_vma=False,
    )
```

```python
from functools import partial
import math

import jax
import jax.numpy as jnp
from jax import lax
from jax.experimental import pallas as pl
from jax.experimental.pallas import tpu as pltpu
from jax.sharding import PartitionSpec as P

HEADS = 4
EVT = 128
HBLK = 16
USERS = 2
ROWS = USERS * EVT
D = 1024
HA = 512
HD = HA // HEADS
GROUP = 8
KEYS = HBLK * EVT
OWNERS = 32
epsilon = 1e-06
SCALE = 1.0 / math.sqrt(HD)
MESH = pl.DeviceIdType.MESH
F32 = jnp.float32
BF16 = jnp.bfloat16
VM = pl.BlockSpec(memory_space=pltpu.VMEM)
SM = pl.BlockSpec(memory_space=pltpu.SMEM)
ANY = pl.BlockSpec(memory_space=pl.ANY)


def dot(a, b, ca=1, cb=0):
    return lax.dot_general(a, b, (((ca,), (cb,)), ((), ())), preferred_element_type=F32)


def normed(values):
    centred = values - jnp.mean(values, axis=-1, keepdims=True)
    inverse = lax.rsqrt(jnp.mean(centred * centred, axis=-1, keepdims=True) + epsilon)
    return centred * inverse, inverse


def norm_back(grad, value, inverse):
    return inverse * (
        grad
        - jnp.mean(grad, axis=-1, keepdims=True)
        - value * jnp.mean(grad * value, axis=-1, keepdims=True)
    )


def silu_parts(half):
    t = jnp.tanh(half)
    return half + half * t, 0.5 * ((1.0 + t) + half * (1.0 - t * t))


def place():
    me = lax.axis_index("dp")
    return me // 8, lax.rem(me // 2, 4), lax.rem(me, 2)


def chip_at(offset):
    y, z, c = place()
    return lax.rem(y + offset[0], 4) * 8 + lax.rem(z + offset[1], 4) * 2 + lax.rem(c + offset[2], 2)


ORDER = (
    [(1, 0), (3, 0), (2, 0), (1, 1), (3, 3), (2, 1), (2, 3), (1, 3), (3, 1), (2, 2), (1, 2), (3, 2), (0, 1), (0, 3), (0, 2)],
    [(0, 1), (0, 3), (0, 2), (1, 2), (3, 2), (1, 1), (3, 3), (2, 2), (1, 3), (3, 1), (2, 1), (2, 3), (1, 0), (3, 0), (2, 0)],
)
PEERS = [(a, b, c) for a in range(4) for b in range(4) for c in range(2)][1:]
SLOTS = 4
BLOCK = (EVT, 2 * HA)


def name_of(y, z, c):
    return y * 8 + z * 2 + c


def reverse_name(y, z, c):
    return lax.rem(4 - y, 4) * 8 + lax.rem(4 - z, 4) * 2 + c


def to_peer(src, dst, send_sem, recv_sem, peer):
    return pltpu.make_async_remote_copy(
        src_ref=src,
        dst_ref=dst,
        send_sem=send_sem,
        recv_sem=recv_sem,
        device_id={"dp": peer},
        device_id_type=MESH,
    )


def greet_all(peers):
    barrier = pltpu.get_barrier_semaphore()
    for peer in peers:
        pl.semaphore_signal(barrier, inc=1, device_id={"dp": chip_at(peer)}, device_id_type=MESH)
    pl.semaphore_wait(barrier, len(peers))


def both_caches(cache_ref, cache, swap_sem, local_sem):
    core = lax.rem(lax.axis_index("dp"), 2)
    mine = cache.at[pl.ds(core * HBLK, HBLK)]
    swap = to_peer(cache_ref, mine, swap_sem.at[0], swap_sem.at[1], chip_at((0, 0, 1)))
    own = pltpu.make_async_copy(cache_ref, mine, local_sem)
    swap.start()
    own.start()
    return swap, own


def ordered(i, core):
    (y0, z0), (y1, z1) = ORDER[0][i], ORDER[1][i]
    return y0 + core * (y1 - y0), z0 + core * (z1 - z0)


def exchange_kernel(
    table_ref, cache_ref, out_ref, asked_ref, cache, asked_s, outgoing, own_blocks,
    swap_sem, ask_send, ask_recv, one_send, one_recv, two_send, two_recv, local_sem,
):
    y, z, core = place()
    chip = y * 4 + z
    greet_all(PEERS)
    swap, own = both_caches(cache_ref, cache, swap_sem, local_sem.at[0])
    asks = []
    for peer in PEERS:
        name = name_of(*peer)
        asks.append(
            to_peer(table_ref, asked_ref.at[name], ask_send.at[name], ask_recv.at[name], chip_at(peer))
        )
        asks[-1].start()
    row = pltpu.make_async_copy(table_ref, asked_ref.at[0], local_sem.at[1])
    row.start()
    row.wait()
    for ask in asks:
        ask.wait()
    down = pltpu.make_async_copy(asked_ref, asked_s, local_sem.at[2])
    down.start()
    down.wait()
    swap.wait()
    own.wait()

    sends = []
    for i in range(15):
        dy, dz = ordered(i, core)
        name = dy * 4 + dz
        for dc in range(2):
            row = reverse_name(dy, dz, dc)
            if dc == 0:
                outgoing[i, 1] = cache[asked_s[row, 0, chip * SLOTS + 1]]
                outgoing[i, 2] = cache[asked_s[row, 0, chip * SLOTS + 2]]
                src, dst = outgoing.at[i, pl.ds(1, 2)], out_ref.at[chip, pl.ds(1, 2)]
                sems = two_send.at[name], two_recv.at[name]
            else:
                outgoing[i, 0] = cache[asked_s[row, 0, chip * SLOTS]]
                src, dst = outgoing.at[i, 0], out_ref.at[chip, 0]
                sems = one_send.at[name], one_recv.at[name]
            sends.append(to_peer(src, dst, *sems, chip_at((dy, dz, dc))))
            sends[-1].start()
    for k in range(SLOTS):
        own_blocks[k] = cache[asked_s[0, 0, chip * SLOTS + k]]
    kept = pltpu.make_async_copy(own_blocks, out_ref.at[chip], local_sem.at[3])
    kept.start()
    for send in sends:
        send.wait()
    kept.wait()


def exchange(table, cache):
    return pl.pallas_call(
        exchange_kernel,
        out_shape=[
            jax.ShapeDtypeStruct((OWNERS // 2, SLOTS) + BLOCK, BF16),
            jax.ShapeDtypeStruct((OWNERS, 1, 128), jnp.int32),
        ],
        in_specs=[VM, ANY],
        out_specs=[ANY, VM],
        scratch_shapes=[
            pltpu.VMEM((2 * HBLK,) + BLOCK, BF16),
            pltpu.SMEM((OWNERS, 1, 128), jnp.int32),
            pltpu.VMEM((15, 3) + BLOCK, BF16),
            pltpu.VMEM((SLOTS,) + BLOCK, BF16),
            pltpu.SemaphoreType.DMA((2,)),
            pltpu.SemaphoreType.DMA((OWNERS,)),
            pltpu.SemaphoreType.DMA((OWNERS,)),
            pltpu.SemaphoreType.DMA((16,)),
            pltpu.SemaphoreType.DMA((16,)),
            pltpu.SemaphoreType.DMA((16,)),
            pltpu.SemaphoreType.DMA((16,)),
            pltpu.SemaphoreType.DMA((4,)),
        ],
        compiler_params=pltpu.CompilerParams(
            collective_id=0, has_side_effects=True, vmem_limit_bytes=40 << 20
        ),
        name="exchange",
    )(table, cache)


def fourth_kernel(
    asked_ref, cache_ref, got_ref, out_ref, cache, outgoing, swap_sem, send_sem, recv_sem, local_sem
):
    del got_ref
    y, z, core = place()
    chip = y * 4 + z
    peers = [(a, b, 0) for a, b in ORDER[0]]
    greet_all(peers + [(0, 0, 1)])
    swap, own = both_caches(cache_ref, cache, swap_sem, local_sem)
    swap.wait()
    own.wait()
    sends = []
    for i, (dy, dz, _) in enumerate(peers):
        outgoing[i] = cache[asked_ref[reverse_name(dy, dz, 0), 0, chip * SLOTS + 3]]
        sends.append(
            to_peer(
                outgoing.at[i], out_ref.at[chip, 3], send_sem.at[i], recv_sem.at[i], chip_at((dy, dz, 0))
            )
        )
        sends[-1].start()
    for send in sends:
        send.wait()


def fourth(asked, cache, got):
    return pl.pallas_call(
        fourth_kernel,
        out_shape=jax.ShapeDtypeStruct(got.shape, BF16),
        in_specs=[SM, ANY, ANY],
        out_specs=ANY,
        scratch_shapes=[
            pltpu.VMEM((2 * HBLK,) + BLOCK, BF16),
            pltpu.VMEM((15,) + BLOCK, BF16),
            pltpu.SemaphoreType.DMA((2,)),
            pltpu.SemaphoreType.DMA((15,)),
            pltpu.SemaphoreType.DMA((15,)),
            pltpu.SemaphoreType.DMA,
        ],
        input_output_aliases={2: 0},
        compiler_params=pltpu.CompilerParams(
            collective_id=3, has_side_effects=True, vmem_limit_bytes=24 << 20
        ),
        name="fourth",
    )(asked, cache, got)


def columns(start):
    return pl.ds(pl.multiple_of(start, HD), HD)


def window_kernel(
    where_ref, live_ref, x_ref, cot_ref, w_in_ref, w_out_ref, fetched_ref,
    made_ref, x_norm_ref, dproj_ref, dy_ref, gated_ref,
    fetched, hist, w_in_t, x_now, x_value, x_rate, act, slope_in, slope, own_weights, mixed, value_ref, rate_ref, dmixed,
    x_arrived, dy_arrived, hist_sem, x_send, x_recv, dy_send, dy_recv,
):
    y_ref, dx_ref = made_ref.at[0], made_ref.at[1]
    section = lax.axis_index("section")
    dp = lax.axis_index("dp")
    after, before = lax.rem(section + 1, 4), lax.rem(section + 3, 4)
    barrier = pltpu.get_barrier_semaphore()
    for peer in (before, after):
        pl.semaphore_signal(barrier, inc=1, device_id=(peer, dp), device_id_type=MESH)

    load = pltpu.make_async_copy(fetched_ref, fetched, hist_sem)
    load.start()
    pl.semaphore_wait(barrier, 2)

    def user_rows(user):
        return pl.ds(pl.multiple_of(user * EVT, EVT), EVT)

    def hop(src, dst, user, sends, recvs, peer):
        rows = user_rows(user)
        return pltpu.make_async_remote_copy(
            src_ref=src.at[rows],
            dst_ref=dst.at[rows],
            send_sem=sends.at[user],
            recv_sem=recvs.at[user],
            device_id=(peer, dp),
            device_id_type=MESH,
        )

    def x_hop(user):
        return hop(y_ref, x_arrived, user, x_send, x_recv, after)

    def dy_hop(user):
        return hop(dx_ref, dy_arrived, user, dy_send, dy_recv, before)

    row_of_block = lax.broadcasted_iota(jnp.int32, (EVT, HA), 0)
    causal = lax.broadcasted_iota(jnp.int32, (EVT, EVT), 1) <= lax.broadcasted_iota(
        jnp.int32, (EVT, EVT), 0
    )

    def inverse_count(user):
        total = live_ref[user * HBLK]
        for j in range(1, HBLK):
            total = total + live_ref[user * HBLK + j]
        return 1.0 / (jnp.full((EVT, 1), total, jnp.int32).astype(F32) + float(EVT))

    def history(user, group, start):
        blocks = pl.ds(user * HBLK + group * GROUP, GROUP)
        return hist[blocks, :, columns(start)].reshape(GROUP * EVT, HD)

    def settle(r, carry):
        block = fetched[where_ref[r]]
        keep = (row_of_block < live_ref[r]).astype(F32).astype(BF16)
        hist[r, :, :HA] = block[:, :HA]
        hist[r, :, HA:] = block[:, HA:] * keep
        return carry

    def turn_w_in():
        for k in range(0, 4 * HA, HD):
            w_in_t[k : k + HD] = w_in_ref[:, k : k + HD].T

    @pl.when(section > 0)
    def _():
        turn_w_in()
        load.wait()
        lax.fori_loop(0, USERS * HBLK, settle, 0)

    def forward_user(user, carry):
        rows = user_rows(user)

        @pl.when(section == 0)
        def _():
            x_now[rows] = x_ref[rows]

        @pl.when(section > 0)
        def _():
            x_hop(user).wait_recv()
            x_now[rows] = x_arrived[rows]

        x = x_now[rows].astype(F32)
        normal, rate = normed(x)
        x_value[rows] = normal
        x_rate[rows] = jnp.broadcast_to(rate, (EVT, 128))
        x_norm = normal.astype(BF16)
        x_norm_ref[rows] = x_norm
        for c in range(4):
            part = slice(c * HA, (c + 1) * HA)
            made, rise = silu_parts(dot(x_norm, w_in_ref[:, part]) * 0.5)
            act[rows, part] = made.astype(BF16)
            slope_in[rows, part] = rise
        inverse = inverse_count(user)

        @pl.when((section == 0) & (user == 0))
        def _():
            load.wait()

        @pl.when(section == 0)
        def _():
            lax.fori_loop(user * HBLK, (user + 1) * HBLK, settle, 0)

        def head_forward(head, carry):
            query = act[rows, columns(2 * HA + head * HD)]
            total = jnp.zeros((EVT, HD), F32)
            for group in range(HBLK // GROUP):
                half = dot(query, history(user, group, head * HD), 1, 1) * (0.5 * SCALE)
                weights, rise = silu_parts(half)
                at = slice(group * GROUP * EVT, (group + 1) * GROUP * EVT)
                slope[user * HEADS + head, :, at] = (rise * SCALE).astype(BF16)
                total += dot(weights.astype(BF16), history(user, group, HA + head * HD))
            half = dot(query, act[rows, columns(3 * HA + head * HD)], 1, 1) * (0.5 * SCALE)
            weights, rise = silu_parts(half)
            weights = jnp.where(causal, weights, 0.0).astype(BF16)
            total += dot(weights, act[rows, columns(HA + head * HD)])
            slope[user * HEADS + head, :, KEYS:] = jnp.where(causal, rise * SCALE, 0.0).astype(BF16)
            own_weights[user * HEADS + head] = weights
            mixed[rows, columns(head * HD)] = total * inverse
            return carry

        lax.fori_loop(0, HEADS, head_forward, 0, unroll=True)
        value, rate = normed(mixed[rows])
        gated = (value * act[rows, :HA].astype(F32)).astype(BF16)
        value_ref[rows] = value
        gated_ref[rows] = gated
        rate_ref[rows] = jnp.broadcast_to(rate, (EVT, 128))
        y_ref[rows] = (x + dot(gated, w_out_ref[...], 1, 1)).astype(BF16)

        @pl.when(section < 3)
        def _():
            x_hop(user).start()

        return carry


    def backward_user(user, carry):
        rows = user_rows(user)

        @pl.when(section == 3)
        def _():
            dy_ref[rows] = cot_ref[rows]

        @pl.when(section < 3)
        def _():
            dy_hop(user).wait_recv()
            dy_ref[rows] = dy_arrived[rows]

        dy = dy_ref[rows]
        dgated = dot(dy, w_out_ref[...])
        value = value_ref[rows]
        dproj_ref[rows, :HA] = (dgated * value * slope_in[rows, :HA]).astype(BF16)
        grad = norm_back(dgated * act[rows, :HA].astype(F32), value, rate_ref[rows, :1])
        dmixed[rows] = (grad * inverse_count(user)).astype(BF16)

        def head_back(head, carry):
            index = user * HEADS + head
            grad_mixed = dmixed[rows, columns(head * HD)]
            total = jnp.zeros((EVT, HD), F32)
            for group in range(HBLK // GROUP):
                rise = slope[index, :, group * GROUP * EVT : (group + 1) * GROUP * EVT].astype(F32)
                ds = (dot(grad_mixed, history(user, group, HA + head * HD), 1, 1) * rise).astype(BF16)
                total += dot(ds, history(user, group, head * HD))
            query = act[rows, columns(2 * HA + head * HD)]
            keys = act[rows, columns(3 * HA + head * HD)]
            values = act[rows, columns(HA + head * HD)]
            ds = (dot(grad_mixed, values, 1, 1) * slope[index, :, KEYS:].astype(F32)).astype(BF16)
            total += dot(ds, keys)
            dvalue = dot(own_weights[index], grad_mixed, 0, 0)
            dkey = dot(ds, query, 0, 0)
            for base, part in ((HA, dvalue), (2 * HA, total), (3 * HA, dkey)):
                at = columns(base + head * HD)
                dproj_ref[rows, at] = (part * slope_in[rows, at]).astype(BF16)
            return carry

        lax.fori_loop(0, HEADS, head_back, 0, unroll=True)
        dnorm = dot(dproj_ref[rows], w_in_t[...])
        dx_ref[rows] = (
            dy.astype(F32) + norm_back(dnorm, x_value[rows], x_rate[rows, :1])
        ).astype(BF16)

        @pl.when(section > 0)
        def _():
            dy_hop(user).start()

        return carry

    def one_pass(i, carry):
        last = section == 3
        user = jnp.where(last, i // 2, lax.rem(i, 2))
        back = jnp.where(last, lax.rem(i, 2), i // 2)

        @pl.when(back == 0)
        def _():
            forward_user(user, 0)

        @pl.when((section == 0) & (i == USERS))
        def _():
            turn_w_in()

        @pl.when(back == 1)
        def _():
            backward_user(user, 0)

        return carry

    lax.fori_loop(0, 2 * USERS, one_pass, 0)

    def finish(user, carry):
        @pl.when(section < 3)
        def _():
            x_hop(user).wait_send()

        @pl.when(section > 0)
        def _():
            dy_hop(user).wait_send()

        return carry

    lax.fori_loop(0, USERS, finish, 0)


def window(where, live, x, cot, w_in, w_out, fetched):
    heads = USERS * HEADS
    return pl.pallas_call(
        window_kernel,
        out_shape=[
            jax.ShapeDtypeStruct((2, ROWS, D), BF16),
            jax.ShapeDtypeStruct((ROWS, D), BF16),
            jax.ShapeDtypeStruct((ROWS, 4 * HA), BF16),
            jax.ShapeDtypeStruct((ROWS, D), BF16),
            jax.ShapeDtypeStruct((ROWS, HA), BF16),
        ],
        in_specs=[SM, SM, VM, VM, VM, VM, ANY],
        out_specs=[VM] * 5,
        scratch_shapes=[
            pltpu.VMEM(fetched.shape, BF16),
            pltpu.VMEM((USERS * HBLK, EVT, 2 * HA), BF16),
            pltpu.VMEM((4 * HA, D), BF16),
            pltpu.VMEM((ROWS, D), BF16),
            pltpu.VMEM((ROWS, D), F32),
            pltpu.VMEM((ROWS, 128), F32),
            pltpu.VMEM((ROWS, 4 * HA), BF16),
            pltpu.VMEM((ROWS, 4 * HA), F32),
            pltpu.VMEM((heads, EVT, KEYS + EVT), BF16),
            pltpu.VMEM((heads, EVT, EVT), BF16),
            pltpu.VMEM((ROWS, HA), F32),
            pltpu.VMEM((ROWS, HA), F32),
            pltpu.VMEM((ROWS, 128), F32),
            pltpu.VMEM((ROWS, HA), BF16),
            pltpu.VMEM((ROWS, D), BF16),
            pltpu.VMEM((ROWS, D), BF16),
            pltpu.SemaphoreType.DMA,
            pltpu.SemaphoreType.DMA((USERS,)),
            pltpu.SemaphoreType.DMA((USERS,)),
            pltpu.SemaphoreType.DMA((USERS,)),
            pltpu.SemaphoreType.DMA((USERS,)),
        ],
        compiler_params=pltpu.CompilerParams(
            collective_id=2, has_side_effects=True, vmem_limit_bytes=56 << 20
        ),
        name="window",
    )(where, live, x, cot, w_in, w_out, fetched)


PARTS = 10
WIDE = (4 * HA + HA) // PARTS
CHUNK = D // OWNERS


def scatter_kernel(
    x_norm_hbm, dproj_hbm, dy_hbm, gated_hbm, sum_ref,
    x_norm_ref, dproj_ref, dy_ref, gated_ref, load_sem, x_turned, dy_turned, part, pair, mine, first, middle, second, pair_sem, first_sem, second_sem,
):
    y, z, c = place()
    steps = (2, 1, 3)
    loads = [
        pltpu.make_async_copy(src, dst, load_sem.at[i])
        for i, (src, dst) in enumerate(
            [(x_norm_hbm, x_norm_ref), (dproj_hbm, dproj_ref), (dy_hbm, dy_ref), (gated_hbm, gated_ref)]
        )
    ]
    for load in loads:
        load.start()
    greet_all([(0, 0, 1)] + [(s, 0, 0) for s in steps] + [(0, s, 0) for s in steps])

    def copy(src, dst, sems, offset):
        made = to_peer(src, dst, sems.at[0], sems.at[1], chip_at(offset))
        made.start()
        return made

    for load in loads:
        load.wait()
    x_turned[...] = x_norm_ref[...].T

    def multiply(q):
        def one(i, carry):
            rows = pl.ds(pl.multiple_of(i * 256, 256), 256)

            def keep(left, right, start):
                made = dot(left[rows], right).astype(BF16)
                width = made.shape[1]
                part[q, i, :, :, :, start : start + width] = made.reshape(4, 2, CHUNK, width)

            low, high = q * WIDE, (q + 1) * WIDE
            if low < 4 * HA:
                keep(x_turned, dproj_ref[:, low : min(high, 4 * HA)], 0)
            if high > 4 * HA:
                start = max(low, 4 * HA)
                keep(dy_turned, gated_ref[:, start - 4 * HA : high - 4 * HA], start - low)
            return carry

        lax.fori_loop(0, 4, one, 0)
        return copy(part.at[q, :, :, 1 - c], pair.at[q], pair_sem.at[q], (0, 0, 1))

    def move(q, swap):
        swap.wait()

        def join(i, carry):
            mine[q, i] = (part[q, i, :, c].astype(F32) + pair[q, i].astype(F32)).astype(BF16)
            return carry

        lax.fori_loop(0, 4, join, 0)
        moves = []
        for k, s in enumerate(steps):
            along_z = q % 2
            at = lax.rem((z if along_z else y) + s, 4)
            src = mine.at[q, :, at] if along_z else mine.at[q, at]
            moves.append(copy(src, first.at[q, k], first_sem.at[q, k], (0, s, 0) if along_z else (s, 0, 0)))
        return moves

    swaps, moves, later = [], [], []
    for q in range(PARTS):
        if q * WIDE < 4 * HA <= (q + 1) * WIDE:
            dy_turned[...] = dy_ref[...].T
        swaps.append(multiply(q))
        if q:
            moves.append(move(q - 1, swaps[q - 1]))
    moves.append(move(PARTS - 1, swaps[PARTS - 1]))
    for q in range(PARTS):
        for made in moves[q]:
            made.wait()
        along_z = q % 2

        def add(i, carry, q=q, along_z=along_z):
            total = (mine[q, i, z] if along_z else mine[q, y, i]).astype(F32)
            for k in range(3):
                total += first[q, k, i].astype(F32)
            middle[q, i] = total.astype(BF16)
            return carry

        lax.fori_loop(0, 4, add, 0)
        sent = []
        for k, s in enumerate(steps):
            at = lax.rem((y if along_z else z) + s, 4)
            sent.append(
                copy(middle.at[q, at], second.at[q, k], second_sem.at[q, k], (s, 0, 0) if along_z else (0, s, 0))
            )
        later.append(sent)
    for q in range(PARTS):
        for made in later[q]:
            made.wait()
        total = middle[q, y if q % 2 else z].astype(F32)
        for k in range(3):
            total += second[q, k].astype(F32)
        sum_ref[:, q * WIDE : (q + 1) * WIDE] = total


def summed(x_norm, dproj, dy, gated):
    return pl.pallas_call(
        scatter_kernel,
        out_shape=jax.ShapeDtypeStruct((CHUNK, 5 * HA), F32),
        in_specs=[ANY] * 4,
        out_specs=VM,
        scratch_shapes=[
            pltpu.VMEM((ROWS, D), BF16),
            pltpu.VMEM((ROWS, 4 * HA), BF16),
            pltpu.VMEM((ROWS, D), BF16),
            pltpu.VMEM((ROWS, HA), BF16),
            pltpu.SemaphoreType.DMA((4,)),
            pltpu.VMEM((D, ROWS), BF16),
            pltpu.VMEM((D, ROWS), BF16),
            pltpu.VMEM((PARTS, 4, 4, 2, CHUNK, WIDE), BF16),
            pltpu.VMEM((PARTS, 4, 4, CHUNK, WIDE), BF16),
            pltpu.VMEM((PARTS, 4, 4, CHUNK, WIDE), BF16),
            pltpu.VMEM((PARTS, 3, 4, CHUNK, WIDE), BF16),
            pltpu.VMEM((PARTS, 4, CHUNK, WIDE), BF16),
            pltpu.VMEM((PARTS, 3, CHUNK, WIDE), BF16),
            pltpu.SemaphoreType.DMA((PARTS, 2)),
            pltpu.SemaphoreType.DMA((PARTS, 3, 2)),
            pltpu.SemaphoreType.DMA((PARTS, 3, 2)),
        ],
        compiler_params=pltpu.CompilerParams(
            collective_id=1, has_side_effects=True, vmem_limit_bytes=60 << 20
        ),
        name="scatter",
    )(x_norm, dproj, dy, gated)


def body(
    embeddings, in_proj, out_proj, hist_cache, hist_len, block_mask, block_owner, block_slot, cotangent
):
    w_in, w_out = in_proj[0], out_proj[0]
    requests = USERS * HBLK
    start = jnp.arange(HBLK, dtype=jnp.int32)[None, :] * EVT
    live = jnp.where(block_mask > 0, jnp.clip(hist_len[:, None] - start, 0, EVT), 0).reshape(requests)
    wanted = live > 0
    owner = jnp.where(wanted, block_owner.reshape(requests), -2)
    order = jnp.arange(requests, dtype=jnp.int32)
    earlier = (owner[:, None] == owner[None, :]) & (order[None, :] < order[:, None])
    rank = jnp.sum(earlier.astype(jnp.int32), axis=1)
    beside = jnp.sum(((owner ^ 1)[:, None] == owner[None, :]).astype(jnp.int32), axis=1)
    me = lax.axis_index("dp")
    chip, core, side = owner // 2, owner % 2, me % 2
    slot = jnp.where(rank == 0, jnp.where(core == side, 1, 0), jnp.where((core == 1) & (beside == 2), 3, 2))
    where = jnp.where(wanted, chip * SLOTS + slot, me // 2 * SLOTS)
    names = jnp.arange(128, dtype=jnp.int32)
    number = core * HBLK + block_slot.reshape(requests)
    late = wanted & (slot == 3) & (chip != me // 2)
    here = (where[:, None] == names[None, :]) & wanted[:, None]
    table = jnp.sum(
        jnp.where(here, number[:, None], 0)
        + jnp.where(late[:, None] & (names[None, :] == 127), 1, 0),
        axis=0,
    )
    cache = hist_cache[0]
    got, asked = exchange(table.reshape(1, 128), cache)
    got = lax.cond(
        jnp.max(asked[:, 0, 127]) > 0, lambda g: fourth(asked, cache, g), lambda g: g, got
    )
    fetched = got.reshape(OWNERS // 2 * SLOTS, EVT, 2 * HA)
    made, x_norm, dproj, dy, gated = window(
        where, live, embeddings, cotangent, w_in, w_out, fetched
    )
    grads = summed(x_norm, dproj, dy, gated)[None]
    return (made[:1], made[1:], grads[:, :, : 4 * HA], grads[:, :, 4 * HA :])


def solution(mesh):
    placed = (
        P("dp", None),
        P("section", None, None),
        P("section", None, None),
        P("section", "dp", None, None),
        P("dp"),
        P("dp", None),
        P("dp", None, None),
        P("dp", None),
        P("dp", None),
    )
    return jax.shard_map(
        body,
        mesh=mesh,
        in_specs=placed,
        out_specs=(
            P("section", "dp", None),
            P("section", "dp", None),
            P("section", "dp", None),
            P("section", "dp", None),
        ),
        check_vma=False,
    )
```

```python
from functools import partial
import math

import jax
import jax.numpy as jnp
from jax import lax
from jax.experimental import pallas as pl
from jax.experimental.pallas import tpu as pltpu
from jax.sharding import PartitionSpec as P

HEADS = 4
EVT = 128
HBLK = 16
USERS = 2
ROWS = USERS * EVT
D = 1024
HA = 512
HD = HA // HEADS
GROUP = 16
KEYS = HBLK * EVT
OWNERS = 32
epsilon = 1e-06
SCALE = 1.0 / math.sqrt(HD)
MESH = pl.DeviceIdType.MESH
F32 = jnp.float32
BF16 = jnp.bfloat16
VM = pl.BlockSpec(memory_space=pltpu.VMEM)
SM = pl.BlockSpec(memory_space=pltpu.SMEM)
ANY = pl.BlockSpec(memory_space=pl.ANY)


def dot(a, b, ca=1, cb=0):
    return lax.dot_general(a, b, (((ca,), (cb,)), ((), ())), preferred_element_type=F32)


def normed(values):
    centred = values - jnp.mean(values, axis=-1, keepdims=True)
    inverse = lax.rsqrt(jnp.mean(centred * centred, axis=-1, keepdims=True) + epsilon)
    return centred * inverse, inverse


def norm_back(grad, value, inverse):
    return inverse * (
        grad
        - jnp.mean(grad, axis=-1, keepdims=True)
        - value * jnp.mean(grad * value, axis=-1, keepdims=True)
    )


def silu_parts(half):
    t = jnp.tanh(half)
    return half + half * t, 0.5 * ((1.0 + t) + half * (1.0 - t * t))


def place():
    me = lax.axis_index("dp")
    return me // 8, lax.rem(me // 2, 4), lax.rem(me, 2)


def chip_at(offset):
    y, z, c = place()
    return lax.rem(y + offset[0], 4) * 8 + lax.rem(z + offset[1], 4) * 2 + lax.rem(c + offset[2], 2)


ORDER = (
    [(1, 0), (3, 0), (2, 0), (1, 1), (3, 3), (2, 1), (2, 3), (1, 3), (3, 1), (2, 2), (1, 2), (3, 2), (0, 1), (0, 3), (0, 2)],
    [(0, 1), (0, 3), (0, 2), (1, 2), (3, 2), (1, 1), (3, 3), (2, 2), (1, 3), (3, 1), (2, 1), (2, 3), (1, 0), (3, 0), (2, 0)],
)
PEERS = [(a, b, c) for a in range(4) for b in range(4) for c in range(2)][1:]
SLOTS = 4
BLOCK = (EVT, 2 * HA)


def name_of(y, z, c):
    return y * 8 + z * 2 + c


def reverse_name(y, z, c):
    return lax.rem(4 - y, 4) * 8 + lax.rem(4 - z, 4) * 2 + c


def to_peer(src, dst, send_sem, recv_sem, peer):
    return pltpu.make_async_remote_copy(
        src_ref=src,
        dst_ref=dst,
        send_sem=send_sem,
        recv_sem=recv_sem,
        device_id={"dp": peer},
        device_id_type=MESH,
    )


def greet_all(peers):
    barrier = pltpu.get_barrier_semaphore()
    for peer in peers:
        pl.semaphore_signal(barrier, inc=1, device_id={"dp": chip_at(peer)}, device_id_type=MESH)
    pl.semaphore_wait(barrier, len(peers))


def both_caches(cache_ref, cache, swap_sem, local_sem):
    core = lax.rem(lax.axis_index("dp"), 2)
    mine = cache.at[pl.ds(core * HBLK, HBLK)]
    swap = to_peer(cache_ref, mine, swap_sem.at[0], swap_sem.at[1], chip_at((0, 0, 1)))
    own = pltpu.make_async_copy(cache_ref, mine, local_sem)
    swap.start()
    own.start()
    return swap, own


def ordered(i, core):
    (y0, z0), (y1, z1) = ORDER[0][i], ORDER[1][i]
    return y0 + core * (y1 - y0), z0 + core * (z1 - z0)


def exchange_kernel(
    table_ref, cache_ref, out_ref, asked_ref, cache, asked_s, outgoing, own_blocks,
    swap_sem, ask_send, ask_recv, one_send, one_recv, two_send, two_recv, local_sem,
):
    y, z, core = place()
    chip = y * 4 + z
    greet_all(PEERS)
    swap, own = both_caches(cache_ref, cache, swap_sem, local_sem.at[0])
    asks = []
    for peer in PEERS:
        name = name_of(*peer)
        asks.append(
            to_peer(table_ref, asked_ref.at[name], ask_send.at[name], ask_recv.at[name], chip_at(peer))
        )
        asks[-1].start()
    row = pltpu.make_async_copy(table_ref, asked_ref.at[0], local_sem.at[1])
    row.start()
    row.wait()
    for ask in asks:
        ask.wait()
    down = pltpu.make_async_copy(asked_ref, asked_s, local_sem.at[2])
    down.start()
    down.wait()
    swap.wait()
    own.wait()

    sends = []
    for i in range(15):
        dy, dz = ordered(i, core)
        name = dy * 4 + dz
        for dc in range(2):
            row = reverse_name(dy, dz, dc)
            if dc == 0:
                outgoing[i, 1] = cache[asked_s[row, 0, chip * SLOTS + 1]]
                outgoing[i, 2] = cache[asked_s[row, 0, chip * SLOTS + 2]]
                src, dst = outgoing.at[i, pl.ds(1, 2)], out_ref.at[chip, pl.ds(1, 2)]
                sems = two_send.at[name], two_recv.at[name]
            else:
                outgoing[i, 0] = cache[asked_s[row, 0, chip * SLOTS]]
                src, dst = outgoing.at[i, 0], out_ref.at[chip, 0]
                sems = one_send.at[name], one_recv.at[name]
            sends.append(to_peer(src, dst, *sems, chip_at((dy, dz, dc))))
            sends[-1].start()
    for k in range(SLOTS):
        own_blocks[k] = cache[asked_s[0, 0, chip * SLOTS + k]]
    kept = pltpu.make_async_copy(own_blocks, out_ref.at[chip], local_sem.at[3])
    kept.start()
    for send in sends:
        send.wait()
    kept.wait()


def exchange(table, cache):
    return pl.pallas_call(
        exchange_kernel,
        out_shape=[
            jax.ShapeDtypeStruct((OWNERS // 2, SLOTS) + BLOCK, BF16),
            jax.ShapeDtypeStruct((OWNERS, 1, 128), jnp.int32),
        ],
        in_specs=[VM, ANY],
        out_specs=[ANY, VM],
        scratch_shapes=[
            pltpu.VMEM((2 * HBLK,) + BLOCK, BF16),
            pltpu.SMEM((OWNERS, 1, 128), jnp.int32),
            pltpu.VMEM((15, 3) + BLOCK, BF16),
            pltpu.VMEM((SLOTS,) + BLOCK, BF16),
            pltpu.SemaphoreType.DMA((2,)),
            pltpu.SemaphoreType.DMA((OWNERS,)),
            pltpu.SemaphoreType.DMA((OWNERS,)),
            pltpu.SemaphoreType.DMA((16,)),
            pltpu.SemaphoreType.DMA((16,)),
            pltpu.SemaphoreType.DMA((16,)),
            pltpu.SemaphoreType.DMA((16,)),
            pltpu.SemaphoreType.DMA((4,)),
        ],
        compiler_params=pltpu.CompilerParams(
            collective_id=0, has_side_effects=True, vmem_limit_bytes=40 << 20
        ),
        name="exchange",
    )(table, cache)


def fourth_kernel(
    asked_ref, cache_ref, got_ref, out_ref, cache, outgoing, swap_sem, send_sem, recv_sem, local_sem
):
    del got_ref
    y, z, core = place()
    chip = y * 4 + z
    peers = [(a, b, 0) for a, b in ORDER[0]]
    greet_all(peers + [(0, 0, 1)])
    swap, own = both_caches(cache_ref, cache, swap_sem, local_sem)
    swap.wait()
    own.wait()
    sends = []
    for i, (dy, dz, _) in enumerate(peers):
        outgoing[i] = cache[asked_ref[reverse_name(dy, dz, 0), 0, chip * SLOTS + 3]]
        sends.append(
            to_peer(
                outgoing.at[i], out_ref.at[chip, 3], send_sem.at[i], recv_sem.at[i], chip_at((dy, dz, 0))
            )
        )
        sends[-1].start()
    for send in sends:
        send.wait()


def fourth(asked, cache, got):
    return pl.pallas_call(
        fourth_kernel,
        out_shape=jax.ShapeDtypeStruct(got.shape, BF16),
        in_specs=[SM, ANY, ANY],
        out_specs=ANY,
        scratch_shapes=[
            pltpu.VMEM((2 * HBLK,) + BLOCK, BF16),
            pltpu.VMEM((15,) + BLOCK, BF16),
            pltpu.SemaphoreType.DMA((2,)),
            pltpu.SemaphoreType.DMA((15,)),
            pltpu.SemaphoreType.DMA((15,)),
            pltpu.SemaphoreType.DMA,
        ],
        input_output_aliases={2: 0},
        compiler_params=pltpu.CompilerParams(
            collective_id=3, has_side_effects=True, vmem_limit_bytes=24 << 20
        ),
        name="fourth",
    )(asked, cache, got)


def columns(start):
    return pl.ds(pl.multiple_of(start, HD), HD)


def window_kernel(
    where_ref, live_ref, x_ref, cot_ref, w_in_ref, w_out_ref, fetched_ref,
    made_ref, x_norm_ref, dproj_ref, dy_ref, gated_ref,
    fetched, hist, w_in_t, x_now, x_value, x_rate, act, slope_in, slope, own_weights, mixed, value_ref, rate_ref, dmixed,
    x_arrived, dy_arrived, hist_sem, x_send, x_recv, dy_send, dy_recv,
):
    y_ref, dx_ref = made_ref.at[0], made_ref.at[1]
    section = lax.axis_index("section")
    dp = lax.axis_index("dp")
    after, before = lax.rem(section + 1, 4), lax.rem(section + 3, 4)
    barrier = pltpu.get_barrier_semaphore()
    for peer in (before, after):
        pl.semaphore_signal(barrier, inc=1, device_id=(peer, dp), device_id_type=MESH)

    load = pltpu.make_async_copy(fetched_ref, fetched, hist_sem)
    load.start()
    pl.semaphore_wait(barrier, 2)

    def user_rows(user):
        return pl.ds(pl.multiple_of(user * EVT, EVT), EVT)

    def hop(src, dst, user, sends, recvs, peer):
        rows = user_rows(user)
        return pltpu.make_async_remote_copy(
            src_ref=src.at[rows],
            dst_ref=dst.at[rows],
            send_sem=sends.at[user],
            recv_sem=recvs.at[user],
            device_id=(peer, dp),
            device_id_type=MESH,
        )

    def x_hop(user):
        return hop(y_ref, x_arrived, user, x_send, x_recv, after)

    def dy_hop(user):
        return hop(dx_ref, dy_arrived, user, dy_send, dy_recv, before)

    row_of_block = lax.broadcasted_iota(jnp.int32, (EVT, HA), 0)
    causal = lax.broadcasted_iota(jnp.int32, (EVT, EVT), 1) <= lax.broadcasted_iota(
        jnp.int32, (EVT, EVT), 0
    )

    def inverse_count(user):
        total = live_ref[user * HBLK]
        for j in range(1, HBLK):
            total = total + live_ref[user * HBLK + j]
        return 1.0 / (jnp.full((EVT, 1), total, jnp.int32).astype(F32) + float(EVT))

    def history(user, group, start):
        blocks = pl.ds(user * HBLK + group * GROUP, GROUP)
        return hist[blocks, :, columns(start)].reshape(GROUP * EVT, HD)

    def settle(r, carry):
        block = fetched[where_ref[r]]
        keep = (row_of_block < live_ref[r]).astype(F32).astype(BF16)
        hist[r, :, :HA] = block[:, :HA]
        hist[r, :, HA:] = block[:, HA:] * keep
        return carry

    def turn_w_in():
        for k in range(0, 4 * HA, HD):
            w_in_t[k : k + HD] = w_in_ref[:, k : k + HD].T

    @pl.when(section > 0)
    def _():
        turn_w_in()
        load.wait()
        lax.fori_loop(0, USERS * HBLK, settle, 0)

    def forward_user(user, carry):
        rows = user_rows(user)

        @pl.when(section == 0)
        def _():
            x_now[rows] = x_ref[rows]

        @pl.when(section > 0)
        def _():
            x_hop(user).wait_recv()
            x_now[rows] = x_arrived[rows]

        x = x_now[rows].astype(F32)
        normal, rate = normed(x)
        x_value[rows] = normal
        x_rate[rows] = jnp.broadcast_to(rate, (EVT, 128))
        x_norm = normal.astype(BF16)
        x_norm_ref[rows] = x_norm
        for c in range(4):
            part = slice(c * HA, (c + 1) * HA)
            made, rise = silu_parts(dot(x_norm, w_in_ref[:, part]) * 0.5)
            act[rows, part] = made.astype(BF16)
            slope_in[rows, part] = rise
        inverse = inverse_count(user)

        @pl.when((section == 0) & (user == 0))
        def _():
            load.wait()

        @pl.when(section == 0)
        def _():
            lax.fori_loop(user * HBLK, (user + 1) * HBLK, settle, 0)

        def head_forward(head, carry):
            query = act[rows, columns(2 * HA + head * HD)]
            total = jnp.zeros((EVT, HD), F32)
            for group in range(HBLK // GROUP):
                half = dot(query, history(user, group, head * HD), 1, 1) * (0.5 * SCALE)
                weights, rise = silu_parts(half)
                at = slice(group * GROUP * EVT, (group + 1) * GROUP * EVT)
                slope[user * HEADS + head, :, at] = (rise * SCALE).astype(BF16)
                total += dot(weights.astype(BF16), history(user, group, HA + head * HD))
            half = dot(query, act[rows, columns(3 * HA + head * HD)], 1, 1) * (0.5 * SCALE)
            weights, rise = silu_parts(half)
            weights = jnp.where(causal, weights, 0.0).astype(BF16)
            total += dot(weights, act[rows, columns(HA + head * HD)])
            slope[user * HEADS + head, :, KEYS:] = jnp.where(causal, rise * SCALE, 0.0).astype(BF16)
            own_weights[user * HEADS + head] = weights
            mixed[rows, columns(head * HD)] = total * inverse
            return carry

        lax.fori_loop(0, HEADS, head_forward, 0, unroll=True)
        value, rate = normed(mixed[rows])
        gated = (value * act[rows, :HA].astype(F32)).astype(BF16)
        value_ref[rows] = value
        gated_ref[rows] = gated
        rate_ref[rows] = jnp.broadcast_to(rate, (EVT, 128))
        y_ref[rows] = (x + dot(gated, w_out_ref[...], 1, 1)).astype(BF16)

        @pl.when(section < 3)
        def _():
            x_hop(user).start()

        return carry


    def backward_user(user, carry):
        rows = user_rows(user)

        @pl.when(section == 3)
        def _():
            dy_ref[rows] = cot_ref[rows]

        @pl.when(section < 3)
        def _():
            dy_hop(user).wait_recv()
            dy_ref[rows] = dy_arrived[rows]

        dy = dy_ref[rows]
        dgated = dot(dy, w_out_ref[...])
        value = value_ref[rows]
        dproj_ref[rows, :HA] = (dgated * value * slope_in[rows, :HA]).astype(BF16)
        grad = norm_back(dgated * act[rows, :HA].astype(F32), value, rate_ref[rows, :1])
        dmixed[rows] = (grad * inverse_count(user)).astype(BF16)

        def head_back(head, carry):
            index = user * HEADS + head
            grad_mixed = dmixed[rows, columns(head * HD)]
            total = jnp.zeros((EVT, HD), F32)
            for group in range(HBLK // GROUP):
                rise = slope[index, :, group * GROUP * EVT : (group + 1) * GROUP * EVT].astype(F32)
                ds = (dot(grad_mixed, history(user, group, HA + head * HD), 1, 1) * rise).astype(BF16)
                total += dot(ds, history(user, group, head * HD))
            query = act[rows, columns(2 * HA + head * HD)]
            keys = act[rows, columns(3 * HA + head * HD)]
            values = act[rows, columns(HA + head * HD)]
            ds = (dot(grad_mixed, values, 1, 1) * slope[index, :, KEYS:].astype(F32)).astype(BF16)
            total += dot(ds, keys)
            dvalue = dot(own_weights[index], grad_mixed, 0, 0)
            dkey = dot(ds, query, 0, 0)
            for base, part in ((HA, dvalue), (2 * HA, total), (3 * HA, dkey)):
                at = columns(base + head * HD)
                dproj_ref[rows, at] = (part * slope_in[rows, at]).astype(BF16)
            return carry

        lax.fori_loop(0, HEADS, head_back, 0, unroll=True)
        dnorm = dot(dproj_ref[rows], w_in_t[...])
        dx_ref[rows] = (
            dy.astype(F32) + norm_back(dnorm, x_value[rows], x_rate[rows, :1])
        ).astype(BF16)

        @pl.when(section > 0)
        def _():
            dy_hop(user).start()

        return carry

    def one_pass(i, carry):
        last = section == 3
        user = jnp.where(last, i // 2, lax.rem(i, 2))
        back = jnp.where(last, lax.rem(i, 2), i // 2)

        @pl.when(back == 0)
        def _():
            forward_user(user, 0)

        @pl.when((section == 0) & (i == USERS))
        def _():
            turn_w_in()

        @pl.when(back == 1)
        def _():
            backward_user(user, 0)

        return carry

    lax.fori_loop(0, 2 * USERS, one_pass, 0)

    def finish(user, carry):
        @pl.when(section < 3)
        def _():
            x_hop(user).wait_send()

        @pl.when(section > 0)
        def _():
            dy_hop(user).wait_send()

        return carry

    lax.fori_loop(0, USERS, finish, 0)


def window(where, live, x, cot, w_in, w_out, fetched):
    heads = USERS * HEADS
    return pl.pallas_call(
        window_kernel,
        out_shape=[
            jax.ShapeDtypeStruct((2, ROWS, D), BF16),
            jax.ShapeDtypeStruct((ROWS, D), BF16),
            jax.ShapeDtypeStruct((ROWS, 4 * HA), BF16),
            jax.ShapeDtypeStruct((ROWS, D), BF16),
            jax.ShapeDtypeStruct((ROWS, HA), BF16),
        ],
        in_specs=[SM, SM, VM, VM, VM, VM, ANY],
        out_specs=[VM] * 5,
        scratch_shapes=[
            pltpu.VMEM(fetched.shape, BF16),
            pltpu.VMEM((USERS * HBLK, EVT, 2 * HA), BF16),
            pltpu.VMEM((4 * HA, D), BF16),
            pltpu.VMEM((ROWS, D), BF16),
            pltpu.VMEM((ROWS, D), F32),
            pltpu.VMEM((ROWS, 128), F32),
            pltpu.VMEM((ROWS, 4 * HA), BF16),
            pltpu.VMEM((ROWS, 4 * HA), F32),
            pltpu.VMEM((heads, EVT, KEYS + EVT), BF16),
            pltpu.VMEM((heads, EVT, EVT), BF16),
            pltpu.VMEM((ROWS, HA), F32),
            pltpu.VMEM((ROWS, HA), F32),
            pltpu.VMEM((ROWS, 128), F32),
            pltpu.VMEM((ROWS, HA), BF16),
            pltpu.VMEM((ROWS, D), BF16),
            pltpu.VMEM((ROWS, D), BF16),
            pltpu.SemaphoreType.DMA,
            pltpu.SemaphoreType.DMA((USERS,)),
            pltpu.SemaphoreType.DMA((USERS,)),
            pltpu.SemaphoreType.DMA((USERS,)),
            pltpu.SemaphoreType.DMA((USERS,)),
        ],
        compiler_params=pltpu.CompilerParams(
            collective_id=2, has_side_effects=True, vmem_limit_bytes=56 << 20
        ),
        name="window",
    )(where, live, x, cot, w_in, w_out, fetched)


PARTS = 10
WIDE = (4 * HA + HA) // PARTS
CHUNK = D // OWNERS


def scatter_kernel(
    x_norm_hbm, dproj_hbm, dy_hbm, gated_hbm, sum_ref,
    x_norm_ref, dproj_ref, dy_ref, gated_ref, load_sem, x_turned, dy_turned, part, pair, mine, first, middle, second, pair_sem, first_sem, second_sem,
):
    y, z, c = place()
    steps = (2, 1, 3)
    loads = [
        pltpu.make_async_copy(src, dst, load_sem.at[i])
        for i, (src, dst) in enumerate(
            [(x_norm_hbm, x_norm_ref), (dproj_hbm, dproj_ref), (dy_hbm, dy_ref), (gated_hbm, gated_ref)]
        )
    ]
    for load in loads:
        load.start()
    greet_all([(0, 0, 1)] + [(s, 0, 0) for s in steps] + [(0, s, 0) for s in steps])

    def copy(src, dst, sems, offset):
        made = to_peer(src, dst, sems.at[0], sems.at[1], chip_at(offset))
        made.start()
        return made

    for load in loads:
        load.wait()
    x_turned[...] = x_norm_ref[...].T

    def multiply(q):
        def one(i, carry):
            rows = pl.ds(pl.multiple_of(i * 256, 256), 256)

            def keep(left, right, start):
                made = dot(left[rows], right).astype(BF16)
                width = made.shape[1]
                part[q, i, :, :, :, start : start + width] = made.reshape(4, 2, CHUNK, width)

            low, high = q * WIDE, (q + 1) * WIDE
            if low < 4 * HA:
                keep(x_turned, dproj_ref[:, low : min(high, 4 * HA)], 0)
            if high > 4 * HA:
                start = max(low, 4 * HA)
                keep(dy_turned, gated_ref[:, start - 4 * HA : high - 4 * HA], start - low)
            return carry

        lax.fori_loop(0, 4, one, 0)
        return copy(part.at[q, :, :, 1 - c], pair.at[q], pair_sem.at[q], (0, 0, 1))

    def move(q, swap):
        swap.wait()

        def join(i, carry):
            mine[q, i] = (part[q, i, :, c].astype(F32) + pair[q, i].astype(F32)).astype(BF16)
            return carry

        lax.fori_loop(0, 4, join, 0)
        moves = []
        for k, s in enumerate(steps):
            along_z = q % 2
            at = lax.rem((z if along_z else y) + s, 4)
            src = mine.at[q, :, at] if along_z else mine.at[q, at]
            moves.append(copy(src, first.at[q, k], first_sem.at[q, k], (0, s, 0) if along_z else (s, 0, 0)))
        return moves

    swaps, moves, later = [], [], []
    for q in range(PARTS):
        if q * WIDE < 4 * HA <= (q + 1) * WIDE:
            dy_turned[...] = dy_ref[...].T
        swaps.append(multiply(q))
        if q:
            moves.append(move(q - 1, swaps[q - 1]))
    moves.append(move(PARTS - 1, swaps[PARTS - 1]))
    for q in range(PARTS):
        for made in moves[q]:
            made.wait()
        along_z = q % 2

        def add(i, carry, q=q, along_z=along_z):
            total = (mine[q, i, z] if along_z else mine[q, y, i]).astype(F32)
            for k in range(3):
                total += first[q, k, i].astype(F32)
            middle[q, i] = total.astype(BF16)
            return carry

        lax.fori_loop(0, 4, add, 0)
        sent = []
        for k, s in enumerate(steps):
            at = lax.rem((y if along_z else z) + s, 4)
            sent.append(
                copy(middle.at[q, at], second.at[q, k], second_sem.at[q, k], (s, 0, 0) if along_z else (0, s, 0))
            )
        later.append(sent)
    for q in range(PARTS):
        for made in later[q]:
            made.wait()
        total = middle[q, y if q % 2 else z].astype(F32)
        for k in range(3):
            total += second[q, k].astype(F32)
        sum_ref[:, q * WIDE : (q + 1) * WIDE] = total


def summed(x_norm, dproj, dy, gated):
    return pl.pallas_call(
        scatter_kernel,
        out_shape=jax.ShapeDtypeStruct((CHUNK, 5 * HA), F32),
        in_specs=[ANY] * 4,
        out_specs=VM,
        scratch_shapes=[
            pltpu.VMEM((ROWS, D), BF16),
            pltpu.VMEM((ROWS, 4 * HA), BF16),
            pltpu.VMEM((ROWS, D), BF16),
            pltpu.VMEM((ROWS, HA), BF16),
            pltpu.SemaphoreType.DMA((4,)),
            pltpu.VMEM((D, ROWS), BF16),
            pltpu.VMEM((D, ROWS), BF16),
            pltpu.VMEM((PARTS, 4, 4, 2, CHUNK, WIDE), BF16),
            pltpu.VMEM((PARTS, 4, 4, CHUNK, WIDE), BF16),
            pltpu.VMEM((PARTS, 4, 4, CHUNK, WIDE), BF16),
            pltpu.VMEM((PARTS, 3, 4, CHUNK, WIDE), BF16),
            pltpu.VMEM((PARTS, 4, CHUNK, WIDE), BF16),
            pltpu.VMEM((PARTS, 3, CHUNK, WIDE), BF16),
            pltpu.SemaphoreType.DMA((PARTS, 2)),
            pltpu.SemaphoreType.DMA((PARTS, 3, 2)),
            pltpu.SemaphoreType.DMA((PARTS, 3, 2)),
        ],
        compiler_params=pltpu.CompilerParams(
            collective_id=1, has_side_effects=True, vmem_limit_bytes=60 << 20
        ),
        name="scatter",
    )(x_norm, dproj, dy, gated)


def body(
    embeddings, in_proj, out_proj, hist_cache, hist_len, block_mask, block_owner, block_slot, cotangent
):
    w_in, w_out = in_proj[0], out_proj[0]
    requests = USERS * HBLK
    start = jnp.arange(HBLK, dtype=jnp.int32)[None, :] * EVT
    live = jnp.where(block_mask > 0, jnp.clip(hist_len[:, None] - start, 0, EVT), 0).reshape(requests)
    wanted = live > 0
    owner = jnp.where(wanted, block_owner.reshape(requests), -2)
    order = jnp.arange(requests, dtype=jnp.int32)
    earlier = (owner[:, None] == owner[None, :]) & (order[None, :] < order[:, None])
    rank = jnp.sum(earlier.astype(jnp.int32), axis=1)
    beside = jnp.sum(((owner ^ 1)[:, None] == owner[None, :]).astype(jnp.int32), axis=1)
    me = lax.axis_index("dp")
    chip, core, side = owner // 2, owner % 2, me % 2
    slot = jnp.where(rank == 0, jnp.where(core == side, 1, 0), jnp.where((core == 1) & (beside == 2), 3, 2))
    where = jnp.where(wanted, chip * SLOTS + slot, me // 2 * SLOTS)
    names = jnp.arange(128, dtype=jnp.int32)
    number = core * HBLK + block_slot.reshape(requests)
    late = wanted & (slot == 3) & (chip != me // 2)
    here = (where[:, None] == names[None, :]) & wanted[:, None]
    table = jnp.sum(
        jnp.where(here, number[:, None], 0)
        + jnp.where(late[:, None] & (names[None, :] == 127), 1, 0),
        axis=0,
    )
    cache = hist_cache[0]
    got, asked = exchange(table.reshape(1, 128), cache)
    got = lax.cond(
        jnp.max(asked[:, 0, 127]) > 0, lambda g: fourth(asked, cache, g), lambda g: g, got
    )
    fetched = got.reshape(OWNERS // 2 * SLOTS, EVT, 2 * HA)
    made, x_norm, dproj, dy, gated = window(
        where, live, embeddings, cotangent, w_in, w_out, fetched
    )
    grads = summed(x_norm, dproj, dy, gated)[None]
    return (made[:1], made[1:], grads[:, :, : 4 * HA], grads[:, :, 4 * HA :])


def solution(mesh):
    placed = (
        P("dp", None),
        P("section", None, None),
        P("section", None, None),
        P("section", "dp", None, None),
        P("dp"),
        P("dp", None),
        P("dp", None, None),
        P("dp", None),
        P("dp", None),
    )
    return jax.shard_map(
        body,
        mesh=mesh,
        in_specs=placed,
        out_specs=(
            P("section", "dp", None),
            P("section", "dp", None),
            P("section", "dp", None),
            P("section", "dp", None),
        ),
        check_vma=False,
    )
```
